32 devices in a mesh: seq: 8 (over y, x, core), grp: 4 (over z).
Axes of the slice: x: 2, y: 2, z: 4, core: 2. Of those that a mesh axis runs over, the one named last changes fastest.
Arguments:
- tokens: bfloat16 [4, 2048, 1024], P('grp', 'seq'), may hold values from -6 to 6
- memory: bfloat16 [4, 320, 1024], P('grp', 'seq'), may hold values from -6 to 6
- cotangent: bfloat16 [4, 2048, 1024], P('grp', 'seq'), may hold values from -6 to 6
- windows: int32 [4], P('grp'), may hold values from 512 to 2048, as said below
- mem_lengths: int32 [4], P('grp'), may hold values from 60 to 320, as said below
- owners: int32 [64], replicated, may hold values from 0 to 31, as said below
- master: float32 [96, 256, 1024], P(('seq', 'grp'))
- first_moment: float32 [96, 256, 1024], P(('seq', 'grp'))
- second_moment: float32 [96, 256, 1024], P(('seq', 'grp')), as said below
- vectors: float32 [17, 1024], replicated
- vec_first: float32 [17, 1024], replicated, may hold values from -256 to 256
- vec_second: float32 [17, 1024], replicated, may hold values from 682.6667 to 2730.6667
Outputs:
- mixed: bfloat16 [4, 2048, 1024], P('grp', 'seq')
- grad_tokens: float32 [4, 2048, 1024], P('grp', 'seq')
- grad_memory: float32 [4, 320, 1024], P('grp', 'seq')
- new_first: float32 [96, 256, 1024], P(('seq', 'grp'))
- new_second: float32 [96, 256, 1024], P(('seq', 'grp'))
- new_master: float32 [96, 256, 1024], P(('seq', 'grp'))
- master_copy: bfloat16 [96, 256, 1024], P(('seq', 'grp'))
- vec_first_out: float32 [17, 1024], replicated
- vec_second_out: float32 [17, 1024], replicated
- vectors_out: float32 [17, 1024], replicated
- grad_out_bias: float32 [1024], replicated
The draws below stay inside these ranges and needn't reach their ends.
Inputs may be any that keep to these rules, and one draw needn't show every extreme that they name: `owners`: each device owns at most 3 units and half of the devices own exactly 3. `windows`: one sequence of each group of 1 sequence has window 2048. `mem_lengths`: one sequence of each group of 1 sequence has all 320 memory keys valid; valid keys come first. `second_moment`: positive.
All inputs are finite; a program needn't handle non-finite values.
Results may differ from the reference program's by a relative error of at most 0.024.
Values may be sent and summed in bfloat16 or wider, within the bound.
A program may use at most 448 MiB of HBM per device.

```python
import math
import jax
import jax.numpy as jnp
from jax import lax

D = 1024
FF = 4096
HEADS = 16
HDIM = 64
BLK = 256
SEQS = 1
MEM_DEV = 40
UNIT_DEV = 2
STEP = 10
SLOTS = 3
LENGTH = 2048
NSEQ = 4
TOKENS = 8192
MEM = 320
UNITS = 64
UROWS = 256
NVEC = 17


def owner_table(key):
    key = jax.random.fold_in(key, 11)
    first_key, second_key = jax.random.split(key)
    holders = UNITS // UNIT_DEV
    heavy_load = UNIT_DEV + UNIT_DEV // 2
    light_load = UNIT_DEV - UNIT_DEV // 2
    holder_order = jax.random.permutation(first_key, holders)
    shuffled = jax.random.permutation(second_key, UNITS)
    positions = jnp.arange(UNITS)
    split_point = holders // 2 * heavy_load
    holder_rank = jnp.where(positions < split_point, positions // heavy_load, holders // 2 + (positions - split_point) // light_load)
    return jnp.zeros((UNITS,), jnp.int32).at[shuffled].set(holder_order[holder_rank].astype(jnp.int32))


def slot_kinds(key):
    owners = owner_table(key)
    positions = jnp.arange(UNITS)
    same_owner = owners[None, :] == owners[:, None]
    slot_rank = jnp.sum((same_owner & (positions[None, :] < positions[:, None])).astype(jnp.int32), axis=1)
    placed = owners * SLOTS + slot_rank
    unit_at = jnp.zeros((UNITS // UNIT_DEV * SLOTS,), jnp.int32).at[placed].set(positions.astype(jnp.int32))
    first_row = unit_at * UROWS
    return jnp.where(first_row < 8 * D, first_row // D, jnp.where(first_row < 8 * D + FF, 8, 9))


def weight_scales():
    return jnp.array([1.0, 1.0, 1.0, 8.0, 1.0, 1.0, 1.0, 5.0, 1.0, math.sqrt(D / FF)], jnp.float32) / math.sqrt(D)


def grad_scales():
    return jnp.array([0.1, 0.1, 0.3, 0.15, 0.1, 0.1, 0.2, 0.2, 0.25, 0.6], jnp.float32) * math.sqrt(TOKENS)


def draw_master(key, part):
    matrix_kind = slot_kinds(key)
    key = jax.random.fold_in(key, 1)
    row_scale = weight_scales()[matrix_kind][:, None, None]
    array_shape = (matrix_kind.shape[0], UROWS, D)
    values = jax.random.normal(key, array_shape, jnp.float32)
    return values * row_scale


def draw_first_moment(key, part):
    matrix_kind = slot_kinds(key)
    key = jax.random.fold_in(key, 2)
    row_scale = grad_scales()[matrix_kind][:, None, None]
    return jax.random.normal(key, (matrix_kind.shape[0], UROWS, D), jnp.float32) * row_scale


def draw_second_moment(key, part):
    matrix_kind = slot_kinds(key)
    key = jax.random.fold_in(key, 3)
    row_scale = grad_scales()[matrix_kind][:, None, None]
    factor = jnp.exp(jax.random.uniform(key, (matrix_kind.shape[0], UROWS, D), jnp.float32, 0.0, math.log(4.0)))
    return factor * row_scale * row_scale / 3.0


def draw_owners(key, part):
    return owner_table(key)


def draw_windows(key, part):
    key = jax.random.fold_in(key, 5)
    first_key, second_key = jax.random.split(key)
    span_draw = jax.random.randint(first_key, (NSEQ,), 2 * BLK, LENGTH + 1)
    full_pick = jax.random.randint(second_key, (NSEQ // SEQS,), 0, SEQS)
    full_mask = jnp.arange(NSEQ) % SEQS == jnp.repeat(full_pick, SEQS)
    return jnp.where(full_mask, LENGTH, span_draw).astype(jnp.int32)


def draw_mem_lengths(key, part):
    key = jax.random.fold_in(key, 6)
    first_key, second_key, third_key = jax.random.split(key, 3)
    short_len = MEM // 4 + jax.random.randint(first_key, (NSEQ,), -(MEM_DEV // 2), MEM_DEV // 2 + 1)
    coin_flip = jax.random.randint(second_key, (NSEQ,), 0, 2)
    full_pick = jax.random.randint(third_key, (NSEQ // SEQS,), 0, SEQS)
    full_mask = (jnp.arange(NSEQ) % SEQS == jnp.repeat(full_pick, SEQS)) | (coin_flip == 1)
    return jnp.where(full_mask, MEM, short_len).astype(jnp.int32)


def draw_vectors(key, part):
    key = jax.random.fold_in(key, 7)
    first_key, second_key = jax.random.split(key)
    row_ids = jnp.arange(NVEC)[:, None]
    gain_draw = jax.random.uniform(first_key, (NVEC, D), jnp.float32, 0.5, 1.5)
    shifts = 0.3 * jax.random.normal(second_key, (NVEC, D), jnp.float32)
    return jnp.where((row_ids < 6) & (row_ids % 2 == 0), gain_draw, shifts)


def block_scale(own_key, dims, pieces, low, high):
    gain, own = 1.0, jax.random.fold_in(own_key, 6)
    for axis_at, shards_of in pieces:
        heights = jnp.exp(jax.random.uniform(jax.random.fold_in(own, axis_at), (shards_of,), jnp.float32, low / len(pieces), high / len(pieces)))
        gain = gain * jnp.repeat(heights, dims[axis_at] // shards_of).reshape([-1 if axis == axis_at else 1 for axis in range(len(dims))])
    return gain


def gaussian(own_key, dims, scale, reach, shards=(), dtype=jnp.bfloat16):
    values = scale * jax.random.normal(own_key, dims, jnp.float32)
    if shards:
        values = values * block_scale(own_key, dims, shards, -0.22, 0.18)
    return jnp.clip(values, -reach, reach).astype(dtype)


def setup_inputs(seed: int = 0) -> dict:
    keys = jax.random.split(jax.random.key(seed), 13)
    return {
        "tokens": gaussian(keys[0], (NSEQ, LENGTH, D), 1.0, 6.0, ((0, 4), (1, 8))),
        "memory": gaussian(keys[1], (NSEQ, MEM, D), 1.0, 6.0, ((0, 4), (1, 8))),
        "cotangent": gaussian(keys[2], (NSEQ, LENGTH, D), 1.0, 6.0, ((0, 4), (1, 8))),
        "windows": draw_windows(jax.random.fold_in(keys[12], 71), 0),
        "mem_lengths": draw_mem_lengths(jax.random.fold_in(keys[12], 71), 0),
        "owners": draw_owners(jax.random.fold_in(keys[12], 71), 0),
        "master": draw_master(jax.random.fold_in(keys[12], 71), 0),
        "first_moment": draw_first_moment(jax.random.fold_in(keys[12], 71), 0),
        "second_moment": draw_second_moment(jax.random.fold_in(keys[12], 71), 0),
        "vectors": draw_vectors(jax.random.fold_in(keys[12], 71), 0),
        "vec_first": gaussian(keys[10], (NVEC, D), (0.5 * TOKENS ** 0.5), 256.0, (), jnp.float32),
        "vec_second": jnp.clip(jnp.exp(jax.random.uniform(keys[11], (NVEC, D), jnp.float32, math.log(682.6667), math.log(2730.6667))), 682.6667, 2730.6667),
    }


NEG_FILL = -1e+30
NORM_EPS = 1e-05
BETA_ONE = 0.5
BETA_TWO = 0.75
RATE_MATRIX = 0.03
RATE_VECTOR = 0.4
WEIGHT_DECAY = 0.01
ADAM_EPS = 1e-08

@jax.custom_vjp
def low(v):
    return lax.optimization_barrier(v.astype(jnp.bfloat16)).astype(jnp.float32)

@jax.custom_vjp
def low_back(v):
    return v

def low_keep(v):
    return (low(v), None)

def low_pass(kept, grad):
    return (grad,)

def back_keep(v):
    return (v, None)

def back_low(kept, grad):
    return (low(grad),)
low.defvjp(low_keep, low_pass)
low_back.defvjp(back_keep, back_low)

def product(left, right):
    return jnp.dot(left, right, precision=lax.Precision.HIGHEST, preferred_element_type=jnp.float32)

def slot_tables(owners, slot_count, holders):
    unit_count = owners.shape[0]
    positions = lax.iota(jnp.int32, unit_count)
    same_owner = owners[None, :] == owners[:, None]
    slot_rank = lax.optimization_barrier(jnp.sum((same_owner & (positions[None, :] < positions[:, None])).astype(jnp.int32), axis=1))
    placed = (owners * slot_count + slot_rank).astype(jnp.int32)
    slot_ids = lax.iota(jnp.int32, holders * slot_count)
    matches = slot_ids[:, None] == placed[None, :]
    occupied = lax.optimization_barrier(jnp.sum(matches.astype(jnp.int32), axis=1)) > 0
    unit_at = lax.optimization_barrier(jnp.sum(jnp.where(matches, positions[None, :], 0), axis=1)).astype(jnp.int32)
    return (placed, unit_at, occupied)

def layer_norm(stream, gain_row, shift_row):
    row_mean = lax.optimization_barrier(jnp.mean(stream, axis=-1, keepdims=True))
    centered = stream - row_mean
    variance = lax.optimization_barrier(jnp.mean(centered * centered, axis=-1, keepdims=True))
    return centered * lax.rsqrt(variance + NORM_EPS) * gain_row + shift_row

def self_attention(query_act, key_act, value_act, window):
    length = query_act.shape[0]
    span = min(512, length)
    groups = length // BLK
    key_heads = key_act.reshape(groups, BLK, HEADS, HDIM)
    value_heads = value_act.reshape(groups, BLK, HEADS, HDIM)
    key_pos = lax.iota(jnp.int32, length).reshape(groups, BLK)

    def query_block(block_item):
        query_tile, query_pos = block_item
        scores = low_back(HDIM ** (-0.5) * jnp.einsum('qhd,nkhd->hqnk', query_tile, key_heads, precision=lax.Precision.HIGHEST))
        allowed = (key_pos[None] <= query_pos[:, None, None]) & (key_pos[None] > query_pos[:, None, None] - window)
        masked = jnp.where(allowed[None], scores, NEG_FILL)
        block_top = lax.optimization_barrier(jnp.max(masked, axis=-1))
        prob_tile = jnp.where(allowed[None], jnp.exp(masked - block_top[..., None]), 0.0)
        block_part = low_back(jnp.einsum('hqnk,nkhd->hqnd', low(prob_tile), value_heads, precision=lax.Precision.HIGHEST))
        row_best = lax.optimization_barrier(jnp.max(block_top, axis=-1))
        lifted = jnp.exp(block_top - row_best[..., None])
        row_total = lax.optimization_barrier(jnp.sum(lifted * lax.optimization_barrier(jnp.sum(prob_tile, axis=-1)), axis=-1))
        attended = lax.optimization_barrier(jnp.sum(lifted[..., None] * block_part, axis=2)) / row_total[..., None]
        return jnp.swapaxes(attended, 0, 1).reshape(span, D)
    query_tiles = query_act.reshape(length // span, span, HEADS, HDIM)
    positions = lax.iota(jnp.int32, length).reshape(length // span, span)
    return lax.map(jax.checkpoint(query_block), (query_tiles, positions)).reshape(length, D)

def cross_attention(query_act, key_act, value_act, mem_valid):
    length = query_act.shape[0]
    span = min(512, length)
    key_heads = key_act.reshape(-1, HEADS, HDIM)
    value_heads = value_act.reshape(-1, HEADS, HDIM)
    allowed = lax.iota(jnp.int32, key_act.shape[0]) < mem_valid

    def query_block(query_tile):
        scores = low_back(HDIM ** (-0.5) * jnp.einsum('qhd,khd->hqk', query_tile, key_heads, precision=lax.Precision.HIGHEST))
        masked = jnp.where(allowed[None, None], scores, NEG_FILL)
        block_top = lax.optimization_barrier(jnp.max(masked, axis=-1))
        prob_tile = jnp.where(allowed[None, None], jnp.exp(masked - block_top[..., None]), 0.0)
        block_part = low_back(jnp.einsum('hqk,khd->hqd', low(prob_tile), value_heads, precision=lax.Precision.HIGHEST))
        attended = block_part / lax.optimization_barrier(jnp.sum(prob_tile, axis=-1))[..., None]
        return jnp.swapaxes(attended, 0, 1).reshape(span, D)
    query_tiles = query_act.reshape(length // span, span, HEADS, HDIM)
    return lax.map(jax.checkpoint(query_block), query_tiles).reshape(length, D)

def decoder_layer(stacked, vectors, stream, memory_rows, window, mem_valid):
    weights_low = low(stacked)
    self_query = weights_low[0:D]
    self_key = weights_low[D:2 * D]
    self_value = weights_low[2 * D:3 * D]
    self_out = weights_low[3 * D:4 * D]
    cross_query = weights_low[4 * D:5 * D]
    cross_key = weights_low[5 * D:6 * D]
    cross_value = weights_low[6 * D:7 * D]
    cross_out = weights_low[7 * D:8 * D]
    hidden_in = weights_low[8 * D:8 * D + FF]
    hidden_out = weights_low[8 * D + FF:]
    bias_rows = FF // D
    normed_self = low(layer_norm(stream, vectors[0], vectors[1]))
    query_act = low(low_back(product(normed_self, self_query) + vectors[6]))
    key_act = low(low_back(product(normed_self, self_key)))
    value_act = low(low_back(product(normed_self, self_value) + vectors[7]))
    attended = low(low_back(self_attention(query_act, key_act, value_act, window)))
    after_self = stream + low_back(product(attended, self_out) + vectors[8])
    normed_cross = low(layer_norm(after_self, vectors[2], vectors[3]))
    cross_queries = low(low_back(product(normed_cross, cross_query) + vectors[9]))
    mem_key_act = low(low_back(product(memory_rows, cross_key)))
    mem_value_act = low(low_back(product(memory_rows, cross_value) + vectors[10]))
    crossed = low(low_back(cross_attention(cross_queries, mem_key_act, mem_value_act, mem_valid)))
    after_cross = after_self + low_back(product(crossed, cross_out) + vectors[11])
    normed_mlp = low(layer_norm(after_cross, vectors[4], vectors[5]))
    pre_act = low_back(product(normed_mlp, hidden_in.T) + vectors[12:12 + bias_rows].reshape(FF))
    activation = low(jax.nn.gelu(pre_act, approximate=False))
    return after_cross + low_back(product(activation, hidden_out) + vectors[12 + bias_rows])

def adam_step(weight, first, second_in, upstream, rate, decay):
    first_new = BETA_ONE * first + (1.0 - BETA_ONE) * upstream
    second_new = BETA_TWO * second_in + (1.0 - BETA_TWO) * upstream * upstream
    first_hat = first_new / (1.0 - BETA_ONE ** STEP)
    second_hat = second_new / (1.0 - BETA_TWO ** STEP)
    weight_new = weight - rate * (first_hat / (jnp.sqrt(second_hat) + ADAM_EPS) + decay * weight)
    return (first_new, second_new, weight_new)

def reference(tokens, memory, cotangent, windows, mem_lengths, owners, master, first_moment, second_moment, vectors, vec_first, vec_second):
    holders = UNITS // UNIT_DEV
    placed, unit_at, occupied = slot_tables(owners, SLOTS, holders)
    stacked = master[placed].reshape(UNITS * UROWS, D)

    def one_sequence(running, seq_item):
        stream, memory_rows, upstream, window, mem_valid = seq_item

        def forward(stacked_in, vectors_in, stream_in, memory_in):
            return decoder_layer(stacked_in, vectors_in, stream_in, memory_in, window, mem_valid)
        result, pullback = jax.vjp(forward, stacked, vectors, stream.astype(jnp.float32), memory_rows.astype(jnp.float32))
        grad_stack, grad_vec, grad_stream, grad_mem = pullback(upstream.astype(jnp.float32))
        return ((running[0] + grad_stack, running[1] + grad_vec), (result.astype(jnp.bfloat16), grad_stream, grad_mem))
    initial = (jnp.zeros(stacked.shape, jnp.float32), jnp.zeros(vectors.shape, jnp.float32))
    (grad_stack, grad_vec), (mixed, grad_tokens, grad_memory) = lax.scan(one_sequence, initial, (tokens, memory, cotangent, windows, mem_lengths))
    grad_units = grad_stack.reshape(UNITS, UROWS, D)
    grad_slots = jnp.where(occupied[:, None, None], grad_units[unit_at], 0.0)
    new_first, new_second, new_master = adam_step(master, first_moment, second_moment, grad_slots, RATE_MATRIX, WEIGHT_DECAY)
    master_copy = new_master.astype(jnp.bfloat16)
    vec_first_out, vec_second_out, vectors_out = adam_step(vectors, vec_first, vec_second, grad_vec, RATE_VECTOR, 0.0)
    grad_out_bias = grad_vec[NVEC - 1]
    return (mixed, grad_tokens, grad_memory, new_first, new_second, new_master, master_copy, vec_first_out, vec_second_out, vectors_out, grad_out_bias)
```

```python
import functools

import jax
import jax.numpy as jnp
from jax import lax
from jax.experimental import pallas as pl
from jax.experimental.pallas import tpu as pltpu
from jax.sharding import PartitionSpec as P

D = 1024
FF = 4096
HEADS = 16
HDIM = 64
STEP = 10


NEG_FILL = -1e30
NORM_EPS = 1e-05
BETA_ONE = 0.5
BETA_TWO = 0.75
RATE_MATRIX = 0.03
RATE_VECTOR = 0.4
WEIGHT_DECAY = 0.01
ADAM_EPS = 1e-08

BF16 = jnp.bfloat16
F32 = jnp.float32
LANES = 128
GROUP_UNITS = 4
GATHER_LIGHT = 4
REDUCE_LIGHT = 4
MIB = 1 << 20


def product(left, right):
    return jnp.dot(left, right, preferred_element_type=F32)


def product_tn(left, right):
    return jnp.einsum("rd,re->de", left, right, preferred_element_type=F32)


def product_nt(left, right):
    return jnp.einsum("rd,ed->re", left, right, preferred_element_type=F32)


def slot_tables(owners, slot_count, holders):
    unit_count = owners.shape[0]
    positions = lax.iota(jnp.int32, unit_count)
    same_owner = owners[None, :] == owners[:, None]
    slot_rank = jnp.sum(
        (same_owner & (positions[None, :] < positions[:, None])).astype(jnp.int32), axis=1
    )
    placed = owners * slot_count + slot_rank
    slot_ids = lax.iota(jnp.int32, holders * slot_count)
    matches = slot_ids[:, None] == placed[None, :]
    occupied = jnp.sum(matches.astype(jnp.int32), axis=1) > 0
    unit_at = jnp.sum(jnp.where(matches, positions[None, :], 0), axis=1)
    return (placed, unit_at, occupied)


def norm_forward(stream, gain_row, shift_row):
    row_mean = jnp.mean(stream, axis=-1, keepdims=True)
    centered = stream - row_mean
    inverse = lax.rsqrt(jnp.mean(centered * centered, axis=-1, keepdims=True) + NORM_EPS)
    normal_form = centered * inverse
    return (normal_form * gain_row + shift_row, normal_form, inverse)


def norm_backward(upstream, normal_form, inverse, gain_row):
    scaled = upstream * gain_row
    first_term = jnp.mean(scaled, axis=-1, keepdims=True)
    second_term = jnp.mean(scaled * normal_form, axis=-1, keepdims=True)
    grad_in = inverse * (scaled - first_term - normal_form * second_term)
    return (grad_in, jnp.sum(upstream * normal_form, axis=0), jnp.sum(upstream, axis=0))


def gelu_exact(values):
    return jax.nn.gelu(values, approximate=False)


def adam_step(weight, first, second_in, upstream, rate, decay):
    first_new = BETA_ONE * first + (1.0 - BETA_ONE) * upstream
    second_new = BETA_TWO * second_in + (1.0 - BETA_TWO) * upstream * upstream
    first_hat = first_new / (1.0 - BETA_ONE**STEP)
    second_hat = second_new / (1.0 - BETA_TWO**STEP)
    weight_new = weight - rate * (first_hat / (jnp.sqrt(second_hat) + ADAM_EPS) + decay * weight)
    return (first_new, second_new, weight_new)


def remote(src, dst, send_sem, recv_sem, target):
    return pltpu.make_async_remote_copy(
        src_ref=src,
        dst_ref=dst,
        send_sem=send_sem,
        recv_sem=recv_sem,
        device_id=target,
        device_id_type=pl.DeviceIdType.MESH,
    )


def greet_all(me, total, target_of):
    barrier = pltpu.get_barrier_semaphore()

    def signal(step, carry):
        pl.semaphore_signal(
            barrier,
            inc=1,
            device_id=target_of(lax.rem(me + step, total)),
            device_id_type=pl.DeviceIdType.MESH,
        )
        return carry

    lax.fori_loop(1, total, signal, 0)
    pl.semaphore_wait(barrier, total - 1)


class Place:
    def __init__(self, planes):
        self.seq = lax.axis_index("seq")
        self.z = lax.axis_index("grp")
        self.planes = planes
        self.core = lax.rem(self.seq, 2)
        self.x = lax.rem(lax.div(self.seq, 2), 2)
        self.y = lax.div(self.seq, 4)

    def at(self, core, x, y, z):
        return (y * 4 + x * 2 + core, z)

    def sibling(self):
        return self.at(1 - self.core, self.x, self.y, self.z)

    def x_peer(self):
        return self.at(self.core, 1 - self.x, self.y, self.z)

    def y_peer(self):
        return self.at(self.core, self.x, 1 - self.y, self.z)

    def above(self):
        return (self.seq, self.z + 1)

    def below(self):
        return (self.seq, self.z - 1)

    def peers(self, half):
        return (self.x_peer(), self.y_peer()) if half == 0 else (self.y_peer(), self.x_peer())

    def bits(self, half):
        return (self.y, self.x) if half == 0 else (self.x, self.y)


def tile_of(device, planes, half, unit_rows):
    seq, z = lax.div(device, planes), lax.rem(device, planes)
    core, x, y = lax.rem(seq, 2), lax.rem(lax.div(seq, 2), 2), lax.div(seq, 4)
    wide, narrow = jnp.where(half == 0, y, x), jnp.where(half == 0, x, y)
    half_rows = unit_rows // 2
    block = half_rows // planes
    first_row = pl.multiple_of(half * half_rows + z * block, block)
    first_column = pl.multiple_of((core * 4 + wide * 2 + narrow) * LANES, LANES)
    return (pl.ds(first_row, block), pl.ds(first_column, LANES))


def loop(first, last, work):
    def one(index, carry):
        work(index)
        return carry

    lax.fori_loop(first, last, one, 0)


class Gather:
    def __init__(self, planes, own_ref, whole_ref, own_sem, z_send, z_recv, p_send, p_recv):
        self.place = Place(planes)
        self.planes = planes
        self.z = self.place.z
        self.own_ref, self.whole_ref = own_ref, whole_ref
        self.own_sem = own_sem
        self.z_send, self.z_recv = z_send, z_recv
        self.p_send, self.p_recv = p_send, p_recv
        self.groups = whole_ref.shape[0]
        self.split = GATHER_LIGHT
        self.leave = 1 + 2 * (planes - 1)
        self.arrived = self.leave + 3

    def block(self, g, half, plane):
        wide, narrow = self.place.bits(half)
        first = self.place.core * 4 + wide * 2 + narrow
        return self.whole_ref.at[g, half, first, plane]

    def pair(self, g, half, plane):
        wide, narrow = self.place.bits(half)
        return self.whole_ref.at[g, half, pl.ds(self.place.core * 4 + wide * 2, 2), plane]

    def line(self, g, half, way, hop, plane, light):
        ref = self.block(g, half, plane) if light else self.pair(g, half, plane)
        return remote(
            self.own_ref.at[g, half] if light and hop == 0 else ref,
            ref,
            self.z_send.at[g, half, way, hop],
            self.z_recv.at[g, half, way, hop],
            self.place.above() if way == 0 else self.place.below(),
        )

    def planar(self, g, half, order, light, arriving=False):
        wide, narrow = self.place.bits(half)
        core = self.place.core
        if order == 0:
            first = core * 4 + wide * 2 + (1 - narrow if arriving else narrow)
            if light:
                ref = src = self.whole_ref.at[g, half, first]
            else:
                ref = self.whole_ref.at[g, half, first, self.z]
                src = self.own_ref.at[g, half]
        else:
            if order == 1:
                first, columns = core * 4 + (1 - wide if arriving else wide) * 2, 2
            else:
                first, columns = (1 - core if arriving else core) * 4, 4
            ref = src = self.whole_ref.at[g, half, pl.ds(first, columns)]
        target = self.place.peers(half)[order] if order < 2 else self.place.sibling()
        return remote(
            src, ref, self.p_send.at[g, half, order], self.p_recv.at[g, half, order], target
        )

    def own_copy(self, g, half):
        return pltpu.make_async_copy(
            self.own_ref.at[g, half],
            self.block(g, half, self.z),
            self.own_sem.at[g, half],
        )

    def enter_line(self, g, half, light):
        z = self.z

        @pl.when(z < self.planes - 1)
        def _():
            self.line(g, half, 0, 0, z, light).start()

        @pl.when(z > 0)
        def _():
            self.line(g, half, 1, 0, z, light).start()

    def hop(self, g, half, k, light):
        z, planes = self.z, self.planes

        @pl.when(z >= k)
        def _():
            self.line(g, half, 0, k - 1, z - k, light).wait_recv()

        if k < planes - 1:

            @pl.when((z >= k) & (z < planes - 1))
            def _():
                self.line(g, half, 0, k, z - k, light).start()

        @pl.when(z + k < planes)
        def _():
            self.line(g, half, 1, k - 1, z + k, light).wait_recv()

        if k < planes - 1:

            @pl.when((z + k < planes) & (z > 0))
            def _():
                self.line(g, half, 1, k, z + k, light).start()

    def exchange(self, g, half, order, light):
        self.planar(g, half, order, light, arriving=True).wait_recv()
        if order < 2:
            self.planar(g, half, order + 1, light).start()

    def heavy_start(self, g, half):
        self.own_copy(g, half).start()
        self.planar(g, half, 0, False).start()

    def heavy_enter(self, g, half):
        self.own_copy(g, half).wait()
        self.planar(g, half, 0, False, arriving=True).wait_recv()
        self.enter_line(g, half, False)

    def heavy_leave(self, g, half):
        self.hop(g, half, self.planes - 1, False)
        self.planar(g, half, 1, False).start()

    def light_start(self, g, half):
        self.own_copy(g, half).start()
        self.enter_line(g, half, True)

    def light_leave(self, g, half):
        self.hop(g, half, self.planes - 1, True)
        self.own_copy(g, half).wait()
        self.planar(g, half, 0, True).start()

    def tick(self, t):
        planes, leave = self.planes, self.leave

        def during(lag, action, first, last):
            g = t - lag

            @pl.when((g >= first) & (g < last))
            def _():
                for half in range(2):
                    action(g, half)

        def heavy(lag, action):
            during(lag, action, self.split, self.groups)

        def light(lag, action):
            during(lag, action, 0, self.split)

        during(leave + 3, lambda g, half: self.exchange(g, half, 2, False), 0, self.groups)
        during(leave + 2, lambda g, half: self.exchange(g, half, 1, False), 0, self.groups)
        heavy(leave, self.heavy_leave)
        light(leave, lambda g, half: self.exchange(g, half, 0, True))
        for k in reversed(range(1, planes - 1)):
            heavy(1 + 2 * k, lambda g, half, k=k: self.hop(g, half, k, False))
        light(leave - 2, self.light_leave)
        for k in reversed(range(1, planes - 1)):
            light(1 + k, lambda g, half, k=k: self.hop(g, half, k, True))
        heavy(1, self.heavy_enter)
        heavy(0, self.heavy_start)
        light(0, self.light_start)

    def drain(self):
        z, planes = self.z, self.planes

        def one(g, light):
            for half in range(2):
                for k in range(planes - 1):

                    @pl.when((z >= k) & (z < planes - 1))
                    def _(half=half, k=k):
                        self.line(g, half, 0, k, z - k, light).wait_send()

                    @pl.when((z + k < planes) & (z > 0))
                    def _(half=half, k=k):
                        self.line(g, half, 1, k, z + k, light).wait_send()

                for order in range(3):
                    self.planar(g, half, order, light).wait_send()

        loop(0, self.split, lambda g: one(g, True))
        loop(self.split, self.groups, lambda g: one(g, False))


def gather_scratch(planes, groups):
    dma = pltpu.SemaphoreType.DMA
    return [
        dma((groups, 2)),
        dma((groups, 2, 2, planes - 1)),
        dma((groups, 2, 2, planes - 1)),
        dma((groups, 2, 3)),
        dma((groups, 2, 3)),
    ]


NORM_ROWS = 32


def norm_into(stream_ref, gain_row, shift_row, out_ref):
    def one(block):
        span = pl.ds(pl.multiple_of(block * NORM_ROWS, NORM_ROWS), NORM_ROWS)
        normed = norm_forward(stream_ref[span].astype(F32), gain_row, shift_row)[0]
        out_ref[span] = normed.astype(BF16)

    loop(0, out_ref.shape[0] // NORM_ROWS, one)


def weight_block(weight_ref, slot, block, unit):
    halves, planes = weight_ref.shape[1], weight_ref.shape[3]
    return [weight_ref[slot, h, block, p, unit] for h in range(halves) for p in range(planes)]


def dot_tiles(left, weight_ref, slot, emit, turned=False, unrolled=False):
    blocks, units = weight_ref.shape[2], weight_ref.shape[4]

    def one(j, carry):
        if turned:
            weight = jnp.concatenate(
                [jnp.concatenate(weight_block(weight_ref, slot, b, j), 0) for b in range(blocks)], 1
            )
            emit(j, dot_nt(left, weight))
        else:
            weight = jnp.concatenate(
                [
                    jnp.concatenate(
                        sum(
                            (weight_block(weight_ref, slot, 2 * j + b, u) for u in range(units)),
                            [],
                        ),
                        0,
                    )
                    for b in range(2)
                ],
                1,
            )
            emit(j, dot_nn(left, weight))
        return carry

    if unrolled:
        for j in range(4):
            one(j, 0)
    else:
        lax.fori_loop(0, 4, one, 0)


TRAVEL = (0, 1, 2, 3, 5, 6, 4, 7, 8, 9, 10, 11, 12, 13, 14, 15)
REDUCE = (12, 13, 14, 15, 8, 9, 10, 11, 7, 4, 3, 5, 6, 0, 1, 2)


def tables_kernel(slots, owners_ref, holder_ref, slot_ref, group_ref, unit_ref, count):
    holders = count.shape[0]

    def clear(n, carry):
        count[n] = 0
        for s in range(slots):
            group_ref[n * slots + s] = -1
            unit_ref[n * slots + s] = 0
        return carry

    lax.fori_loop(0, holders, clear, 0)
    for unit in range(owners_ref.shape[0]):
        matrix, part = divmod(unit, GROUP_UNITS)
        owner = owners_ref[unit]
        slot = count[owner]
        count[owner] = slot + 1
        travel = TRAVEL.index(matrix) * GROUP_UNITS + part
        holder_ref[travel] = owner
        slot_ref[travel] = slot
        group_ref[owner * slots + slot] = REDUCE.index(matrix)
        unit_ref[owner * slots + slot] = part


def owner_tables(owners, slots, holders):
    units = owners.shape[0]
    smem = pl.BlockSpec(memory_space=pltpu.SMEM)
    return pl.pallas_call(
        functools.partial(tables_kernel, slots),
        out_shape=(jax.ShapeDtypeStruct((units,), jnp.int32),) * 2
        + (jax.ShapeDtypeStruct((holders * slots,), jnp.int32),) * 2,
        in_specs=[smem],
        out_specs=(smem,) * 4,
        scratch_shapes=[pltpu.SMEM((holders,), jnp.int32)],
        name="owner_tables",
    )(owners)


def forward_kernel(
    seqs,
    planes,
    window_ref,
    length_ref,
    holder_ref,
    slot_ref,
    master_ref,
    tokens_ref,
    memory_ref,
    vectors_ref,
    whole_ref,
    h1_ref,
    joined_ref,
    qkv_all,
    rounded,
    log_ref,
    x2_ref,
    h2_ref,
    cq_ref,
    mem_ref,
    crossed_low_ref,
    cross_log_ref,
    x3_ref,
    h3_ref,
    act_ref,
    slope_ref,
    mixed_ref,
    master_wide,
    master_low,
    tiles,
    own,
    memory_came,
    memory_wide,
    memory_all,
    weights,
    qkv_out,
    down,
    own_sem,
    z_send,
    z_recv,
    p_send,
    p_recv,
    load_sem,
    master_sem,
    tile_send,
    tile_recv,
    memory_send,
    memory_recv,
    send_sem,
    recv_sem,
    back_send,
    back_recv,
):
    fetch = pltpu.make_async_copy(master_ref, master_wide, master_sem)
    fetch.start()
    gather = Gather(planes, own, whole_ref, own_sem, z_send, z_recv, p_send, p_recv)
    place = gather.place
    me, z = place.seq, place.z
    rows = tokens_ref.shape[0]
    width = D // seqs
    tile = 2 * LANES
    total = seqs * planes
    here = me * planes + z
    mem_rows = memory_all.shape[0] // seqs
    greet_all(here, total, lambda j: (lax.div(j, planes), lax.rem(j, planes)))

    def vector(index):
        return vectors_ref[index : index + 1]

    def columns_of(j):
        return pl.ds(pl.multiple_of(j * tile, tile), tile)

    def tile_copy(peer, slot, half):
        tile_rows, tile_columns = tile_of(peer, planes, half, master_low.shape[1])
        return remote(
            master_low.at[:, tile_rows, tile_columns],
            tiles.at[slot, half],
            tile_send.at[peer, half],
            tile_recv.at[slot, half],
            (lax.div(peer, planes), lax.rem(peer, planes)),
        )

    def memory_copy(peer, slot):
        return remote(
            memory_ref, memory_came.at[slot], memory_send.at[peer], memory_recv.at[slot], (peer, z)
        )

    def spread():
        fetch.wait()
        part = 64

        def lower(index):
            slot, block = lax.div(index, master_low.shape[1] // part), lax.rem(
                index, master_low.shape[1] // part
            )
            span = pl.ds(pl.multiple_of(block * part, part), part)
            master_low[slot, span] = master_wide[slot, span].astype(BF16)

        loop(0, master_low.shape[0] * master_low.shape[1] // part, lower)

        def start(step):
            peer = lax.rem(here + step, total)
            loop(0, 2, lambda half: tile_copy(peer, here, half).start())

        loop(1, total, start)
        loop(1, seqs, lambda step: memory_copy(lax.rem(me + step, seqs), me).start())

        def keep_own(half):
            tile_rows, tile_columns = tile_of(here, planes, half, master_low.shape[1])
            tiles[here, half] = master_low[:, tile_rows, tile_columns]

        loop(0, 2, keep_own)
        memory_came[me] = memory_ref[...]
        norm_into(tokens_ref, vector(0), vector(1), h1_ref)

        def finish_memory(step):
            peer = lax.rem(me + step, seqs)
            memory_copy(peer, peer).wait()

        loop(1, seqs, finish_memory)

        def widen(j):
            span = pl.ds(pl.multiple_of(j * mem_rows, 8), mem_rows)
            memory_wide[span] = memory_came[j].astype(F32)[:mem_rows]

        loop(0, seqs, widen)

        def narrow(block):
            span = pl.ds(pl.multiple_of(block * part, part), part)
            memory_all[span] = memory_wide[span].astype(BF16)

        loop(0, memory_all.shape[0] // part, narrow)

        def finish(step):
            peer = lax.rem(here + total - step, total)
            loop(0, 2, lambda half: tile_copy(peer, peer, half).wait())

        loop(1, total, finish)

        def keep(unit):
            g, u = lax.div(unit, GROUP_UNITS), lax.rem(unit, GROUP_UNITS)
            for half in range(2):
                own[g, half, u] = tiles[holder_ref[unit], half, slot_ref[unit]]

        loop(0, holder_ref.shape[0], keep)

    def load(position, slot):
        return pltpu.make_async_copy(whole_ref.at[position], weights.at[slot], load_sem.at[slot])

    def outward(part, peer, slot):
        return remote(
            qkv_out.at[part, peer],
            qkv_all.at[part, slot],
            send_sem.at[part, peer],
            recv_sem.at[part, slot],
            (peer, z),
        )

    def backward_copy(peer, slot):
        return remote(
            rounded.at[peer],
            joined_ref.at[:, pl.ds(pl.multiple_of(slot * width, width), width)],
            back_send.at[peer],
            back_recv.at[slot],
            (peer, z),
        )

    def project(part):
        load(part, part).start()
        load(part, part).wait()
        bias_row = 6 + lax.div(part, 2)

        def emit(j, result):
            bias = vectors_ref[pl.ds(bias_row, 1), columns_of(j)]
            result = (result + jnp.where(part == 1, 0.0, bias)).astype(BF16)
            for piece in range(tile // width):
                qkv_out[part, j * (tile // width) + piece] = result[
                    :, piece * width : (piece + 1) * width
                ]

        dot_tiles(h1_ref[...], weights, part, emit, unrolled=True)
        loop(1, seqs, lambda step: outward(part, lax.rem(me + step, seqs), me).start())
        qkv_all[part, me] = qkv_out[part, me]

    head_count = width // HDIM

    def query_block(i):
        def arrive(ahead):
            @pl.when((lax.rem(i, 2) == 0) & (i + ahead != me))
            def _():
                loop(0, 3, lambda part: outward(part, i + ahead, i + ahead).wait_recv())

        loop(0, 2, arrive)
        rounded[i] = attend_pairs(i, rows, head_count, window_ref[0], qkv_all, log_ref).astype(BF16)

        @pl.when(i != me)
        def _():
            backward_copy(i, me).start()

        @pl.when(i == me)
        def _():
            joined_ref[:, pl.ds(pl.multiple_of(i * width, width), width)] = rounded[i]

    def after_self():
        def arrive(step):
            peer = lax.rem(me + step, seqs)
            backward_copy(peer, peer).wait_recv()

        loop(1, seqs, arrive)
        load(3, 0).wait()

        def emit(j, result):
            columns = columns_of(j)
            x2_ref[:, columns] = (
                tokens_ref[:, columns].astype(F32) + result + vectors_ref[8:9, columns]
            )

        dot_tiles(joined_ref[...], weights, 0, emit, unrolled=True)
        norm_into(x2_ref, vector(2), vector(3), h2_ref)
        load(6, 1).wait()

        def emit_query(j, result):
            columns = columns_of(j)
            cq_ref[:, columns] = (result + vectors_ref[9:10, columns]).astype(BF16)

        dot_tiles(h2_ref[...], weights, 1, emit_query, unrolled=True)

    def memory_rows(part):
        load(4 + part, part).start()
        load(4 + part, part).wait()

        def emit(j, result):
            columns = columns_of(j)
            bias = jnp.where(part == 1, vectors_ref[10:11, columns], 0.0)
            mem_ref[part, :, columns] = (result + bias).astype(BF16)

        dot_tiles(memory_all[...], weights, part, emit, unrolled=True)

    def cross_blocks(first, last):
        def one(j):
            columns = pl.ds(pl.multiple_of(j * LANES, LANES), LANES)
            crossed, logs = cross_attend(
                length_ref[0], cq_ref[:, columns], mem_ref[0, :, columns], mem_ref[1, :, columns]
            )
            for head in range(len(logs)):
                cross_log_ref[j, head : head + 1] = logs[head]
            crossed_low_ref[:, columns] = crossed.astype(BF16)

        loop(first, last, one)

    def after_cross():
        load(7, 2).wait()

        def emit(j, result):
            columns = columns_of(j)
            total = x2_ref[:, columns] + result + vectors_ref[11:12, columns]
            x3_ref[:, columns] = total
            down[:, columns] = total + vectors_ref[12 + FF // D : 13 + FF // D, columns]

        dot_tiles(crossed_low_ref[...], weights, 2, emit, unrolled=True)
        norm_into(x3_ref, vector(4), vector(5), h3_ref)

    def hidden_up(j):
        slot = lax.rem(j + 3, 4)
        load(8 + j, slot).wait()

        def emit(r, result):
            columns = columns_of(r)
            spread = pl.ds(pl.multiple_of(j * D + r * tile, tile), tile)
            pre = result + vectors_ref[pl.ds(12 + j, 1), columns]
            cumulative = 0.5 * (1.0 + lax.erf(pre * 0.5**0.5))
            density = jnp.exp(-0.5 * pre * pre) * (2.0 * jnp.pi) ** -0.5
            act_ref[:, spread] = (pre * cumulative).astype(BF16)
            slope_ref[:, spread] = (cumulative + pre * density).astype(BF16)

        dot_tiles(h3_ref[...], weights, slot, emit, turned=True, unrolled=True)

        @pl.when(j < 3)
        def _():
            load(12 + j, slot).start()

    def hidden_down(j):
        slot = lax.rem(j + 3, 4)
        load(12 + j, slot).wait()
        left = act_ref[:, pl.ds(pl.multiple_of(j * D, D), D)]

        def emit(r, result):
            columns = columns_of(r)
            down[:, columns] = down[:, columns] + result

        dot_tiles(left, weights, slot, emit, unrolled=True)

    arrived = gather.arrived

    def tick(t):
        gather.tick(t)

        @pl.when((t >= arrived) & (t < arrived + 3))
        def _():
            project(t - arrived)

        first_block = arrived + 3

        @pl.when((t >= first_block) & (t < first_block + seqs))
        def _():
            query_block(t - first_block)

        @pl.when((t >= arrived + 4) & (t < arrived + 6))
        def _():
            memory_rows(t - arrived - 4)

        early = arrived + 6
        for step, (position, slot) in enumerate(((3, 0), (6, 1), (7, 2), (8, 3))):

            @pl.when(t == early + step)
            def _(position=position, slot=slot):
                load(position, slot).start()

        late = first_block + seqs

        @pl.when(t == late)
        def _():
            after_self()
            load(9, 0).start()
            load(10, 1).start()

        @pl.when((t >= late) & (t < late + 2))
        def _():
            cross_blocks(4 * (t - late), 4 * (t - late) + 4)

        @pl.when(t == late + 1)
        def _():
            after_cross()
            load(11, 2).start()

        hidden = late + 2

        @pl.when((t >= hidden) & (t < hidden + 2))
        def _():
            loop(2 * (t - hidden), 2 * (t - hidden) + 2, hidden_up)

        @pl.when(t == hidden + 2)
        def _():
            load(15, 2).start()

        @pl.when(t > hidden)
        def _():
            loop(jnp.where(t == hidden + 1, 0, 1), jnp.where(t == hidden + 1, 1, 4), hidden_down)

    spread()
    loop(0, gather.groups + arrived, tick)

    def close(block):
        span = pl.ds(pl.multiple_of(block * NORM_ROWS, NORM_ROWS), NORM_ROWS)
        mixed_ref[span] = down[span].astype(BF16)

    loop(0, rows // NORM_ROWS, close)

    def finish(step):
        peer = lax.rem(me + step, seqs)
        loop(0, 3, lambda part: outward(part, peer, me).wait_send())
        backward_copy(peer, me).wait_send()

    loop(1, seqs, finish)
    gather.drain()


def forward_pass(
    seqs, planes, windows, lengths, holder, slot, master, tokens, memory, mem, vectors
):
    groups = holder.shape[0] // GROUP_UNITS
    slots, unit_rows = master.shape[:2]
    block = (unit_rows // 2 // planes, LANES)
    matrix = (2, D // LANES, planes, GROUP_UNITS) + block
    rows = tokens.shape[0]
    width = D // seqs
    dma = pltpu.SemaphoreType.DMA
    vmem = pl.BlockSpec(memory_space=pltpu.VMEM)
    smem = pl.BlockSpec(memory_space=pltpu.SMEM)
    anywhere = pl.BlockSpec(memory_space=pl.ANY)
    shape = jax.ShapeDtypeStruct
    by_head = (seqs, rows, width)
    outs = (
        shape((groups,) + matrix, BF16),
        shape((rows, D), BF16),
        shape((rows, D), BF16),
        shape((3,) + by_head, BF16),
        shape(by_head, BF16),
        shape((seqs, 8, rows), F32),
        shape((rows, D), F32),
        shape((rows, D), BF16),
        shape((rows, D), BF16),
        shape((2, mem, D), BF16),
        shape((rows, D), BF16),
        shape((D // LANES, 8, rows), F32),
        shape((rows, D), F32),
        shape((rows, D), BF16),
        shape((rows, FF), BF16),
        shape((rows, FF), BF16),
        shape((rows, D), BF16),
    )
    return pl.pallas_call(
        functools.partial(forward_kernel, seqs, planes),
        out_shape=outs,
        in_specs=[smem] * 4 + [anywhere, vmem, vmem, vmem],
        out_specs=(anywhere,) + (vmem,) * (len(outs) - 1),
        scratch_shapes=[
            pltpu.VMEM(master.shape, F32),
            pltpu.VMEM(master.shape, BF16),
            pltpu.VMEM((seqs * planes, 2, slots) + block, BF16),
            pltpu.VMEM((groups, 2, GROUP_UNITS) + block, BF16),
            pltpu.VMEM((seqs,) + memory.shape, BF16),
            pltpu.VMEM((mem, D), F32),
            pltpu.VMEM((mem, D), BF16),
            pltpu.VMEM((4,) + matrix, BF16),
            pltpu.VMEM((3,) + by_head, BF16),
            pltpu.VMEM((rows, D), F32),
        ]
        + gather_scratch(planes, groups)
        + [
            dma((4,)),
            dma(()),
            dma((seqs * planes, 2)),
            dma((seqs * planes, 2)),
            dma((seqs,)),
            dma((seqs,)),
        ]
        + [dma((3, seqs)), dma((3, seqs)), dma((seqs,)), dma((seqs,))],
        compiler_params=pltpu.CompilerParams(
            collective_id=2, has_side_effects=True, vmem_limit_bytes=56 * MIB
        ),
        name="forward_pass",
    )(windows, lengths, holder, slot, master, tokens, memory, vectors)


GRAD_SLOTS = 4
COLUMN_SLOTS = 8


class Reduce:
    def __init__(
        self,
        planes,
        made,
        theirs_far,
        wide_far,
        chain_far,
        sums_ref,
        theirs,
        wide_in,
        narrow_in,
        narrow_all,
        column,
        chain_in,
        light_in,
        load_sem,
        chain_sem,
        c_send,
        c_recv,
        p_send,
        p_recv,
        z_send,
        z_recv,
    ):
        self.place = Place(planes)
        self.planes = planes
        self.z = self.place.z
        self.made = made
        self.theirs_far, self.wide_far, self.chain_far = theirs_far, wide_far, chain_far
        self.sums_ref = sums_ref
        self.theirs, self.wide_in = theirs, wide_in
        self.narrow_in, self.column, self.chain_in = narrow_in, column, chain_in
        self.narrow_all, self.light_in = narrow_all, light_in
        self.load_sem, self.chain_sem = load_sem, chain_sem
        self.c_send, self.c_recv = c_send, c_recv
        self.p_send, self.p_recv = p_send, p_recv
        self.z_send, self.z_recv = z_send, z_recv
        self.groups = theirs_far.shape[0]
        self.enter = 3
        self.leave = self.enter + 2 * (planes - 1)
        self.last = self.leave + 1
        self.split = self.groups - REDUCE_LIGHT
        self.light_enter = self.enter + 2

    def to_sibling(self, g):
        src = self.made.at[lax.rem(g, GRAD_SLOTS), :, pl.ds((1 - self.place.core) * 4, 4)]
        return remote(
            src, self.theirs_far.at[g], self.c_send.at[g], self.c_recv.at[g], self.place.sibling()
        )

    def planar(self, g, half, order, light=False):
        place = self.place
        wide, narrow = place.bits(half)
        narrow_peer, wide_peer = place.peers(half)
        if order == 0:
            slot = lax.rem(g, GRAD_SLOTS)
            src = self.made.at[slot, half, pl.ds(place.core * 4 + (1 - wide) * 2, 2)]
            dst, target = self.wide_far.at[g, half], wide_peer
        elif light:
            src = self.column.at[lax.rem(g, COLUMN_SLOTS), :, half, 1 - narrow]
            dst, target = self.narrow_all.at[g - self.split, half], narrow_peer
        else:
            src = self.column.at[lax.rem(g, COLUMN_SLOTS), self.z, half, 1 - narrow]
            dst, target = self.narrow_in.at[g, half], narrow_peer
        return remote(
            src, dst, self.p_send.at[g, half, order], self.p_recv.at[g, half, order], target
        )

    def load(self, g, order):
        src, dst = ((self.theirs_far, self.theirs), (self.wide_far, self.wide_in))[order]
        return pltpu.make_async_copy(src.at[g], dst, self.load_sem.at[order])

    def plane_at(self, way, reach):
        return reach if way == 0 else self.planes - 1 - reach

    def chain(self, g, way, reach, light):
        src = self.column.at[lax.rem(g, COLUMN_SLOTS), self.plane_at(way, reach)]
        dst = self.chain_far.at[g, way, reach - 1]
        return remote(
            src.at[:, 0] if light else src,
            dst.at[:, 0] if light else dst,
            self.z_send.at[g, way, reach - 1],
            self.z_recv.at[g, way, reach - 1],
            self.place.above() if way == 0 else self.place.below(),
        )

    def chain_load(self, g, way, reach, light):
        src = self.chain_far.at[g, way, reach - 1]
        dst = self.light_in if light else self.chain_in
        return pltpu.make_async_copy(
            src.at[:, 0] if light else src,
            dst.at[way, reach - 1],
            self.chain_sem.at[1 if light else 0, way, reach - 1],
        )

    def chain_of(self, t, way, action):
        here = self.z if way == 0 else self.planes - 1 - self.z
        for light in (False, True):
            lag = self.light_enter + here if light else self.enter + 2 * here
            g = t - lag
            first, last = (self.split, self.groups) if light else (0, self.split)

            @pl.when((here > 0) & (g >= first) & (g < last))
            def _(light=light, g=g):
                loop(here, self.planes, lambda reach: action(g, way, reach, light))

    def chain_arrive(self, g, way, reach, light):
        self.chain(g, way, reach, light).wait_recv()
        self.chain_load(g, way, reach, light).start()

    def chain_pass(self, g, way, reach, light):
        here = self.z if way == 0 else self.planes - 1 - self.z
        slot, plane = lax.rem(g, COLUMN_SLOTS), self.plane_at(way, reach)
        self.chain_load(g, way, reach, light).wait()
        if light:
            for half in range(2):
                self.column[slot, plane, half, 0] = (
                    self.column[slot, plane, half, 0] + self.light_in[way, reach - 1, half]
                )
        else:
            self.column[slot, plane] = self.column[slot, plane] + self.chain_in[way, reach - 1]

        @pl.when(reach > here)
        def _():
            self.chain(g, way, reach, light).start()

    def start_chains(self, g, light):
        for way in range(2):

            @pl.when(self.z == (0 if way == 0 else self.planes - 1))
            def _(way=way):
                loop(1, self.planes, lambda reach: self.chain(g, way, reach, light).start())

    def enter_line(self, g):
        slot, spot = lax.rem(g, GRAD_SLOTS), lax.rem(g, COLUMN_SLOTS)
        self.load(g, 1).wait()
        for half in range(2):
            wide, narrow = self.place.bits(half)
            first = self.place.core * 4 + wide * 2
            for b in range(2):
                total = self.made[slot, half, first + b] + self.wide_in[half, b]
                for plane in range(self.planes):
                    self.column[spot, plane, half, b] = total[plane]

        @pl.when(g < self.split)
        def _():
            self.start_chains(g, False)

        @pl.when(g >= self.split)
        def _():
            for half in range(2):
                self.planar(g, half, 1, True).start()

    def enter_light(self, g):
        slot = lax.rem(g, COLUMN_SLOTS)
        for half in range(2):
            wide, narrow = self.place.bits(half)
            self.planar(g, half, 1, True).wait()

            def one(plane, half=half, narrow=narrow):
                self.column[slot, plane, half, 0] = (
                    self.column[slot, plane, half, narrow]
                    + self.narrow_all[g - self.split, half, plane]
                )

            loop(0, self.planes, one)
        self.start_chains(g, True)

    def finish_light(self, g):
        slot = lax.rem(g, COLUMN_SLOTS)
        for half in range(2):
            self.sums_ref[g, half] = self.column[slot, self.z, half, 0]

    def finish(self, g):
        for half in range(2):
            wide, narrow = self.place.bits(half)
            self.planar(g, half, 1).wait_recv()
            own = self.column[lax.rem(g, COLUMN_SLOTS), self.z, half, narrow].astype(F32)
            self.sums_ref[g, half] = (own + self.narrow_in[g, half].astype(F32)).astype(BF16)

    def arrive(self, g, order):
        if order == 0:
            self.to_sibling(g).wait_recv()
        else:
            for half in range(2):
                self.planar(g, half, 0).wait_recv()
        self.load(g, order).start()

    def add(self, g):
        slot = lax.rem(g, GRAD_SLOTS)
        self.load(g, 0).wait()
        first = self.place.core * 4
        for half in range(2):
            for b in range(4):
                self.made[slot, half, first + b] = (
                    self.made[slot, half, first + b] + self.theirs[half, b]
                )
            self.planar(g, half, 0).start()

    def leave_line(self, g):
        for half in range(2):
            self.planar(g, half, 1).start()

    def wait_column_sends(self, g, light=False):
        if not light:
            for half in range(2):
                self.planar(g, half, 1).wait_send()
        for way in range(2):
            here = self.z if way == 0 else self.planes - 1 - self.z
            loop(here + 1, self.planes, lambda reach: self.chain(g, way, reach, light).wait_send())

    def wait_made_sends(self, g):
        self.to_sibling(g).wait_send()
        for half in range(2):
            self.planar(g, half, 0).wait_send()

    def during(self, t, lag, action, first=0, last=None):
        g = t - lag

        @pl.when((g >= first) & (g < (self.groups if last is None else last)))
        def _():
            action(g)

    def receive(self, t):
        self.during(t, 1, lambda g: self.arrive(g, 0))
        self.during(t, self.enter, lambda g: self.arrive(g, 1))
        for way in range(2):
            self.chain_of(t, way, self.chain_arrive)
        self.during(t, self.last, self.finish, 0, self.split)

        @pl.when((t >= GRAD_SLOTS) & (t < self.groups))
        def _():
            self.wait_made_sends(t - GRAD_SLOTS)

    def advance(self, t):
        self.during(t, 0, lambda g: self.to_sibling(g).start())
        for way in range(2):
            self.chain_of(t, way, self.chain_pass)
        self.during(t, self.leave, self.leave_line, 0, self.split)
        self.during(t, self.light_enter + self.planes, self.finish_light, self.split)
        self.during(t, self.light_enter, self.enter_light, self.split)

        @pl.when((t >= self.enter + COLUMN_SLOTS) & (t < self.enter + self.groups))
        def _():
            self.wait_column_sends(t - self.enter - COLUMN_SLOTS)

        self.during(t, self.enter, self.enter_line)
        self.during(t, 1, self.add)

    def drain(self):
        loop(self.groups - GRAD_SLOTS, self.groups, self.wait_made_sends)
        loop(self.groups - COLUMN_SLOTS, self.split, self.wait_column_sends)
        loop(self.split, self.groups, lambda g: self.wait_column_sends(g, True))


BACKWARD_READS = (12, 8, 13, 9, 14, 10, 15, 11, 7, 6, 3, 4, 5, 0, 1, 2)
READ_SLOTS = 3


def backward_kernel(
    seqs,
    planes,
    window_ref,
    length_ref,
    group_ref,
    unit_ref,
    whole_ref,
    slope_ref,
    cotangent_ref,
    tokens_ref,
    x2_ref,
    x3_ref,
    h1_ref,
    h2_ref,
    h3_ref,
    act_ref,
    crossed_ref,
    cq_ref,
    mem_ref,
    cross_log_ref,
    joined_ref,
    attended_ref,
    qkv_all,
    log_ref,
    memory_ref,
    vectors_ref,
    theirs_far,
    wide_far,
    chain_far,
    slots_ref,
    grad_tokens_ref,
    grad_memory_ref,
    vec_sum_ref,
    sums_ref,
    vec_ref,
    vec_part,
    vec_came,
    vec_planes,
    made,
    theirs,
    wide_in,
    narrow_in,
    narrow_all,
    column,
    chain_in,
    light_in,
    weights,
    dx,
    dh,
    du,
    dx3_low,
    dx2_low,
    dco,
    dcq,
    mem_parts,
    mem_theirs,
    mem_came,
    mem_low,
    do_all,
    delta,
    dq_total,
    dk_total,
    dv_total,
    dq_low,
    dk_low,
    dv_low,
    dq_back,
    dk_back,
    dv_back,
    load_sem,
    chain_sem,
    c_send,
    c_recv,
    p_send,
    p_recv,
    z_send,
    z_recv,
    read_sem,
    slope_sem,
    fold_send,
    fold_recv,
    mem_send,
    mem_recv,
    do_send,
    do_recv,
    back_send,
    back_recv,
    vec_send,
    vec_recv,
    across_send,
    across_recv,
    slot_send,
    slot_recv,
    own_sem,
):
    reduce = Reduce(
        planes,
        made,
        theirs_far,
        wide_far,
        chain_far,
        sums_ref,
        theirs,
        wide_in,
        narrow_in,
        narrow_all,
        column,
        chain_in,
        light_in,
        load_sem,
        chain_sem,
        c_send,
        c_recv,
        p_send,
        p_recv,
        z_send,
        z_recv,
    )
    place = reduce.place
    me, z = place.seq, place.z
    rows = tokens_ref.shape[0]
    width = D // seqs
    tile = 2 * LANES
    head_count = width // HDIM
    mem_rows = mem_ref.shape[1] // seqs
    padded = memory_ref.shape[0]
    ups = FF // D

    total = seqs * planes
    here = me * planes + z

    def read(k):
        slot = k % READ_SLOTS
        return pltpu.make_async_copy(
            whole_ref.at[BACKWARD_READS[k]], weights.at[slot], read_sem.at[slot]
        )

    def using(k, work):
        read(k).wait()
        work(k % READ_SLOTS)
        if k + READ_SLOTS < len(BACKWARD_READS):
            read(k + READ_SLOTS).start()

    greet_all(here, total, lambda j: (lax.div(j, planes), lax.rem(j, planes)))

    slope_copy = pltpu.make_async_copy(slope_ref, du, slope_sem)
    slope_copy.start()
    for k in range(READ_SLOTS):
        read(k).start()

    def columns_of(j, count=tile):
        return pl.ds(pl.multiple_of(j * count, count), count)

    def vector(index):
        return vectors_ref[index : index + 1]

    def row_sum(values):
        return jnp.sum(values.astype(F32), axis=0, keepdims=True)

    def norm_back(stream_ref, gain_row, base, out_ref, low_ref):
        gain = vector(gain_row)
        part = rows // 4

        def one(block, sums):
            span = pl.ds(pl.multiple_of(block * part, part), part)
            _, form, inverse = norm_forward(stream_ref[span].astype(F32), 1.0, 0.0)
            upstream = dh[span]
            scaled = upstream * gain
            first = jnp.mean(scaled, axis=-1, keepdims=True)
            second = jnp.mean(scaled * form, axis=-1, keepdims=True)
            total = base(span) + inverse * (scaled - first - form * second)
            out_ref[span] = total
            gains, shifts, lows = sums
            if low_ref is not None:
                low = total.astype(BF16)
                low_ref[span] = low
                lows = lows + row_sum(low)
            return (gains + row_sum(upstream * form), shifts + row_sum(upstream), lows)

        zero = jnp.zeros((1, D), F32)
        gains, shifts, lows = lax.fori_loop(0, 4, one, (zero, zero, zero))
        vec_ref[gain_row : gain_row + 1] = gains
        vec_ref[gain_row + 1 : gain_row + 2] = shifts
        return lows

    def grad_matrix(slot, left_ref, first_column, right_ref):
        def one(r):
            first = first_column + r * tile
            left = left_ref[:, pl.ds(pl.multiple_of(first, tile), tile)]
            block = made.shape[5]
            for c in range(2):
                columns = slice(c * (D // 2), (c + 1) * (D // 2))
                result = dot_tn(left, right_ref[:, columns]).astype(BF16)
                for part in range(tile // block):
                    for b in range(D // 2 // LANES):
                        made[slot, part // planes, c * 4 + b, part % planes, r] = result[
                            part * block : (part + 1) * block, b * LANES : (b + 1) * LANES
                        ]

        def two(pair):
            one(2 * pair)
            one(2 * pair + 1)

        loop(0, GROUP_UNITS // 2, two)

    def hidden_back(j):
        if j == 0:
            dh[...] = jnp.zeros_like(dh)
            slope_copy.wait()
            vec_ref[...] = jnp.zeros_like(vec_ref)

        def slopes(slot):
            def emit(r, result):
                spread = pl.ds(pl.multiple_of(j * D + r * tile, tile), tile)
                low = (result * du[:, spread].astype(F32)).astype(BF16)
                du[:, spread] = low
                vec_ref[12 + j : 13 + j, columns_of(r)] = row_sum(low)

            dot_tiles(cotangent_ref[...], weights, slot, emit, turned=True, unrolled=True)

        def inner(slot):
            def emit(r, result):
                dh[:, columns_of(r)] = dh[:, columns_of(r)] + result

            dot_tiles(du[:, j * D : (j + 1) * D], weights, slot, emit, unrolled=True)

        using(2 * j, slopes)
        using(2 * j + 1, inner)

    def mem_fold():
        return remote(
            mem_parts.at[1 - place.core],
            mem_theirs,
            fold_send,
            fold_recv,
            place.sibling(),
        )

    chip = lax.div(me, 2)
    chips = seqs // 2

    def mem_copy(peer, slot):
        return remote(
            mem_parts.at[place.core, peer],
            mem_came.at[slot],
            mem_send.at[peer],
            mem_recv.at[slot],
            (2 * peer + place.core, z),
        )

    def cross_branch():
        vec_ref[12 + ups : 13 + ups] = row_sum(cotangent_ref[...])
        vec_ref[11:12] = norm_back(
            x3_ref, 4, lambda span: cotangent_ref[span].astype(F32), dx, dx3_low
        )

        def branch(slot):
            def emit(r, result):
                dco[:, columns_of(r)] = result.astype(BF16)

            dot_tiles(dx3_low[...], weights, slot, emit, turned=True, unrolled=True)

        using(8, branch)

    def cross_back(first, last):
        def one(j, carry):
            columns = columns_of(j, LANES)
            dq, dk, dv = cross_grads(
                length_ref[0],
                cq_ref[:, columns],
                mem_ref[0, :, columns],
                mem_ref[1, :, columns],
                dco[:, columns],
                crossed_ref[:, columns],
                [cross_log_ref[j, h : h + 1] for h in range(LANES // HDIM)],
            )
            dcq[:, columns] = dq.astype(BF16)
            fill = jnp.zeros((max(padded - mem_rows, 1), LANES), F32)
            for peer in range(seqs):
                span = slice(peer * mem_rows, (peer + 1) * mem_rows)
                for part, values in enumerate((dk, dv)):
                    block = values[span]
                    if padded > mem_rows:
                        block = jnp.concatenate([block, fill], axis=0)
                    mem_parts[peer % 2, peer // 2, part, :, columns] = block.astype(BF16)
            return carry

        lax.fori_loop(first, last, one, 0)

    def memory_send():
        mem_fold().wait()

        def send(step):
            peer = lax.rem(chip + step, chips)
            mem_parts[place.core, peer] = mem_parts[place.core, peer] + mem_theirs[peer]

            @pl.when(step < chips)
            def _():
                mem_copy(peer, chip).start()

            @pl.when(step == chips)
            def _():
                mem_came[chip] = mem_parts[place.core, peer]

        loop(1, chips + 1, send)

    def do_copy(peer, slot):
        return remote(
            dq_low.at[peer], do_all.at[slot], do_send.at[peer], do_recv.at[slot], (peer, z)
        )

    def before_self():
        def inner(slot):
            def emit(r, result):
                dh[:, columns_of(r)] = result

            dot_tiles(dcq[...], weights, slot, emit, turned=True, unrolled=True)

        using(9, inner)
        vec_ref[9:10] = row_sum(dcq[...])
        vec_ref[8:9] = norm_back(x2_ref, 2, lambda span: dx[span], dx, dx2_low)

        def branch(slot):
            def emit(r, result):
                low = result.astype(BF16)
                for piece in range(tile // width):
                    dq_low[r * (tile // width) + piece] = low[
                        :, piece * width : (piece + 1) * width
                    ]

            dot_tiles(dx2_low[...], weights, slot, emit, turned=True, unrolled=True)

        using(10, branch)

        def send(step, carry):
            do_copy(lax.rem(me + step, seqs), me).start()
            return carry

        lax.fori_loop(1, seqs, send, 0)
        do_all[me] = dq_low[me]

    def memory_back():
        def arrive(step):
            peer = lax.rem(chip + step, chips)
            mem_copy(peer, peer).wait_recv()

        loop(1, chips, arrive)
        for part in range(2):
            part_sum = mem_came[0, part].astype(F32)
            for j in range(1, chips):
                part_sum = part_sum + mem_came[j, part].astype(F32)
            mem_low[part] = part_sum.astype(BF16)
        vec_ref[10:11] = row_sum(mem_low[1])

        def keys(slot):
            def emit(r, result):
                grad_memory_ref[:, columns_of(r)] = result

            dot_tiles(mem_low[0], weights, slot, emit, turned=True, unrolled=True)

        def values(slot):
            def emit(r, result):
                grad_memory_ref[:, columns_of(r)] = grad_memory_ref[:, columns_of(r)] + result

            dot_tiles(mem_low[1], weights, slot, emit, turned=True, unrolled=True)

        using(11, keys)
        using(12, values)

    window = window_ref[0]
    outputs = ((dq_low, dq_back), (dk_low, dk_back), (dv_low, dv_back))

    def returned(peer, slot, part):
        src, dst = outputs[part]
        return remote(
            src.at[peer],
            dst.at[:, pl.ds(pl.multiple_of(slot * width, width), width)],
            back_send.at[part, peer],
            back_recv.at[part, slot],
            (peer, z),
        )

    def prepare():
        def one(i, carry):
            @pl.when(i != me)
            def _():
                do_copy(i, i).wait_recv()

            sums = head_sums(do_all[i].astype(F32) * attended_ref[i].astype(F32), head_count)
            for head in range(head_count):
                delta[i, head : head + 1] = sums[head]
            for total in (dq_total, dk_total, dv_total):
                total[i] = jnp.zeros((rows, width), F32)
            return carry

        lax.fori_loop(0, seqs, one, 0)

    span_rows = 2 * rows
    stacked_queries = head_count * span_rows

    def tile_grads(p):
        level = (
            jnp.where(p >= 2, 1, 0) + jnp.where(p >= 6, 1, 0) + jnp.where(p >= 12, 1, 0)
        ).astype(jnp.int32)
        rank = p - level * (level + 1)
        second = jnp.where(rank > level, 1, 0).astype(jnp.int32)
        b = seqs - 1 - 2 * level - second
        q2 = seqs // 2 - 1 - level + rank - second * (level + 1)
        pair = pl.ds(pl.multiple_of(q2 * 2, 2), 2)
        keys, values = qkv_all[1, b], qkv_all[2, b]
        scaled = qkv_all[0, pair].reshape(span_rows, width) * jnp.asarray(HDIM**-0.5, BF16)
        grads = do_all[pair].reshape(span_rows, width)
        queries = jnp.concatenate([only_head(scaled, h, head_count) for h in range(head_count)], 0)
        uppers = jnp.concatenate([only_head(grads, h, head_count) for h in range(head_count)], 0)

        def row_of(ref):
            return jnp.concatenate(
                [ref[q2 * 2 + k, h : h + 1] for h in range(head_count) for k in range(2)], 1
            )

        logs, deltas = row_of(log_ref), row_of(delta)
        shape = (rows, stacked_queries)
        key_row = lax.broadcasted_iota(jnp.int32, shape, 0)
        query_row = lax.rem(lax.broadcasted_iota(jnp.int32, (1, stacked_queries), 1), span_rows)
        reach = query_row + (q2 * 2 - b) * rows

        def work(diagonal):
            scores = dot_nt(keys, queries)
            allowed = key_row <= reach if diagonal else key_row > reach - window
            probs = jnp.exp(jnp.where(allowed, scores, NEG_FILL) - logs)
            grad_scores = (probs * (dot_nt(values, uppers) - deltas)).astype(BF16)
            dv_total[b] = dv_total[b] + dot_nn(probs.astype(BF16), uppers)
            dk_total[b] = dk_total[b] + dot_nn(grad_scores, queries)
            spread = dot_tn(grad_scores, keys)
            part = spread[:span_rows]
            lane = lax.broadcasted_iota(jnp.int32, part.shape, 1)
            for h in range(1, head_count):
                part = jnp.where(
                    lane >= h * HDIM, spread[h * span_rows : (h + 1) * span_rows], part
                )
            dq_total[pair] = dq_total[pair] + part.reshape(2, rows, width)

        diagonal = lax.div(b, 2) == q2

        @pl.when(diagonal)
        def _():
            work(True)

        @pl.when(jnp.logical_not(diagonal))
        def _():
            work(False)

        @pl.when(q2 == seqs // 2 - 1)
        def _():
            dk_low[b] = dk_total[b].astype(BF16)
            dv_low[b] = dv_total[b].astype(BF16)
            send_back(b, 1)
            send_back(b, 2)

    def send_back(i, part):
        low, rows_ref = outputs[part]

        @pl.when(i != me)
        def _():
            returned(i, me, part).start()

        @pl.when(i == me)
        def _():
            rows_ref[:, pl.ds(pl.multiple_of(i * width, width), width)] = low[i]

    def close_self():
        loop(1, seqs, lambda step: do_copy(lax.rem(me + step, seqs), me).wait_send())

        def one(i):
            dq_low[i] = (dq_total[i] * HDIM**-0.5).astype(BF16)
            send_back(i, 0)

        loop(0, seqs, one)

    def first_arrive():
        def arrive(step, carry):
            peer = lax.rem(me + step, seqs)
            for part in range(3):
                returned(peer, peer, part).wait_recv()
            return carry

        lax.fori_loop(1, seqs, arrive, 0)

    def first_back():
        for part in range(3):

            def inner(slot, part=part):
                def emit(r, result):
                    if part == 0:
                        dh[:, columns_of(r)] = result
                    else:
                        dh[:, columns_of(r)] = dh[:, columns_of(r)] + result

                dot_tiles(rows_of_part[part][...], weights, slot, emit, turned=True, unrolled=True)

            using(13 + part, inner)
        vec_ref[6:7] = row_sum(rows_of_part[0][...])
        vec_ref[7:8] = row_sum(rows_of_part[2][...])
        norm_back(tokens_ref, 0, lambda span: dx[span], grad_tokens_ref, None)

    rows_of_part = (dq_back, dk_back, dv_back)

    def fold_copy(order):
        target = (place.sibling(), place.x_peer(), place.y_peer())[order]
        return remote(
            vec_part.at[order],
            vec_came.at[order],
            vec_send.at[order],
            vec_recv.at[order],
            target,
        )

    def across_copy(peer, slot):
        return remote(
            vec_planes.at[slot],
            vec_planes.at[slot],
            across_send.at[peer],
            across_recv.at[slot],
            (me, peer),
        )

    def fold_vectors(order):
        if order == 0:
            vec_part[0] = vec_ref[...]
        else:
            fold_copy(order - 1).wait()
            folded = vec_part[order - 1] + vec_came[order - 1]
            if order < 3:
                vec_part[order] = folded
            else:
                vec_planes[z] = folded
        if order < 3:
            fold_copy(order).start()
        else:

            def send(step, carry):
                across_copy(lax.rem(z + step, planes), z).start()
                return carry

            lax.fori_loop(1, planes, send, 0)

    def close_vectors():
        def arrive(step, carry):
            peer = lax.rem(z + step, planes)
            across_copy(peer, peer).wait()
            return carry

        lax.fori_loop(1, planes, arrive, 0)
        vector_sum = vec_planes[0]
        for plane in range(1, planes):
            vector_sum = vector_sum + vec_planes[plane]
        vec_sum_ref[...] = vector_sum

    slot_count = slots_ref.shape[0]

    def slot_copy(peer, holder, half):
        slot_rows, slot_columns = tile_of(holder, planes, half, slots_ref.shape[1])
        return remote(
            made.at[0, half, lax.div(peer, planes), lax.rem(peer, planes), pl.ds(0, slot_count)],
            slots_ref.at[:, slot_rows, slot_columns],
            slot_send.at[peer, half],
            slot_recv.at[holder, half],
            (lax.div(peer, planes), lax.rem(peer, planes)),
        )

    def return_tiles():
        def fill(peer):
            for s in range(slot_count):
                group, unit = group_ref[peer * slot_count + s], unit_ref[peer * slot_count + s]
                for half in range(2):
                    block = sums_ref[jnp.maximum(group, 0), half, unit]
                    made[0, half, lax.div(peer, planes), lax.rem(peer, planes), s] = jnp.where(
                        group >= 0, block, jnp.zeros_like(block)
                    )

        def start(step, carry):
            peer = lax.rem(here + step, total)
            fill(peer)
            for half in range(2):
                slot_copy(peer, here, half).start()
            return carry

        lax.fori_loop(1, total, start, 0)
        fill(here)
        own = []
        for half in range(2):
            slot_rows, slot_columns = tile_of(here, planes, half, slots_ref.shape[1])
            own.append(
                pltpu.make_async_copy(
                    made.at[0, half, lax.div(here, planes), lax.rem(here, planes), pl.ds(0, slot_count)],
                    slots_ref.at[:, slot_rows, slot_columns],
                    own_sem.at[half],
                )
            )
            own[half].start()
        for copy in own:
            copy.wait()

        def finish_slots(step, carry):
            peer = lax.rem(here + total - step, total)
            for half in range(2):
                slot_copy(peer, peer, half).wait()
            return carry

        lax.fori_loop(1, total, finish_slots, 0)

    def tick(t, carry):
        reduce.receive(t)

        slot = lax.rem(t, GRAD_SLOTS)

        @pl.when(t < ups)
        def _():
            grad_matrix(slot, act_ref, t * D, cotangent_ref)

        @pl.when((t >= ups) & (t < 2 * ups))
        def _():
            grad_matrix(slot, du, (t - ups) * D, h3_ref)

        late = 2 * ups
        pieces = (
            (crossed_ref, dx3_low),
            (h2_ref, dcq),
            (joined_ref, dx2_low),
            (memory_ref, mem_low.at[0]),
            (memory_ref, mem_low.at[1]),
        )
        for step, (left, right) in enumerate(pieces):

            @pl.when(t == late + step)
            def _(left=left, right=right):
                grad_matrix(slot, left, 0, right)

        last = late + len(pieces)

        @pl.when(t == last)
        def _():
            first_arrive()

        for part in range(3):

            @pl.when(t == last + part)
            def _(part=part):
                grad_matrix(slot, h1_ref, 0, rows_of_part[part])

        reduce.advance(t)

        def at(step, work):
            @pl.when(t == step)
            def _():
                work()

        for j in range(ups):
            at(1 + j // 2, functools.partial(hidden_back, j))
        at(3, cross_branch)
        blocks = D // LANES
        at(4, functools.partial(cross_back, 0, blocks // 2))
        at(5, functools.partial(cross_back, blocks // 2, blocks))
        at(5, lambda: mem_fold().start())
        at(6, memory_send)
        at(6, before_self)
        at(7, prepare)

        @pl.when((t >= 7) & (t < 13))
        def _():
            loop(lax.div(10 * (t - 7), 3), lax.div(10 * (t - 6), 3), tile_grads)

        at(10, memory_back)
        at(12, close_self)
        at(last + 3, first_back)
        for order in range(4):
            at(last + 4 + order, functools.partial(fold_vectors, order))
        at(last + 9, close_vectors)
        return carry

    lax.fori_loop(0, reduce.groups + reduce.last, tick, 0)

    def finish(step, carry):
        peer = lax.rem(me + step, seqs)
        for part in range(3):
            returned(peer, me, part).wait_send()
        return carry

    lax.fori_loop(1, seqs, finish, 0)
    loop(1, chips, lambda step: mem_copy(lax.rem(chip + step, chips), chip).wait_send())
    reduce.drain()
    return_tiles()


def backward_pass(seqs, planes, windows, lengths, group, unit, whole, slope, arrays):
    groups, matrix = whole.shape[0], whole.shape[1:]
    column = matrix[2:]
    block = matrix[3:]
    cotangent, memory = arrays[0], arrays[-2]
    total = seqs * planes
    slots, unit_rows = group.shape[0] // total, 2 * planes * block[1]
    rows = cotangent.shape[0]
    width = D // seqs
    padded = memory.shape[0]
    dma = pltpu.SemaphoreType.DMA
    vmem = pl.BlockSpec(memory_space=pltpu.VMEM)
    smem = pl.BlockSpec(memory_space=pltpu.SMEM)
    anywhere = pl.BlockSpec(memory_space=pl.ANY)
    shape = jax.ShapeDtypeStruct
    by_head = (seqs, rows, width)
    outs = pl.pallas_call(
        functools.partial(backward_kernel, seqs, planes),
        out_shape=(
            shape((groups, 2, 4) + column, BF16),
            shape((groups, 2, 2) + column, BF16),
            shape((groups, 2, planes - 1, 2, 2) + block, BF16),
            shape((slots, unit_rows, D), BF16),
            shape((rows, D), F32),
            shape((padded, D), F32),
            shape((24, D), F32),
        ),
        in_specs=[smem] * 4 + [anywhere, anywhere] + [vmem] * len(arrays),
        out_specs=(anywhere, anywhere, anywhere, anywhere, vmem, vmem, vmem),
        scratch_shapes=[
            pltpu.VMEM((groups, 2) + block, BF16),
            pltpu.VMEM((24, D), F32),
            pltpu.VMEM((3, 24, D), F32),
            pltpu.VMEM((3, 24, D), F32),
            pltpu.VMEM((planes, 24, D), F32),
            pltpu.VMEM((GRAD_SLOTS,) + matrix, BF16),
            pltpu.VMEM((2, 4) + column, BF16),
            pltpu.VMEM((2, 2) + column, BF16),
            pltpu.VMEM((groups, 2) + block, BF16),
            pltpu.VMEM((REDUCE_LIGHT, 2) + column, BF16),
            pltpu.VMEM((COLUMN_SLOTS, planes, 2, 2) + block, BF16),
            pltpu.VMEM((2, planes - 1, 2, 2) + block, BF16),
            pltpu.VMEM((2, planes - 1, 2) + block, BF16),
            pltpu.VMEM((READ_SLOTS,) + matrix, BF16),
            pltpu.VMEM((rows, D), F32),
            pltpu.VMEM((rows, D), F32),
            pltpu.VMEM((rows, FF), BF16),
            pltpu.VMEM((rows, D), BF16),
            pltpu.VMEM((rows, D), BF16),
            pltpu.VMEM((rows, D), BF16),
            pltpu.VMEM((rows, D), BF16),
            pltpu.VMEM((2, seqs // 2, 2, padded, D), BF16),
            pltpu.VMEM((seqs // 2, 2, padded, D), BF16),
            pltpu.VMEM((seqs // 2, 2, padded, D), BF16),
            pltpu.VMEM((2, padded, D), BF16),
            pltpu.VMEM(by_head, BF16),
            pltpu.VMEM((seqs, 8, rows), F32),
            pltpu.VMEM(by_head, F32),
            pltpu.VMEM(by_head, F32),
            pltpu.VMEM(by_head, F32),
            pltpu.VMEM(by_head, BF16),
            pltpu.VMEM(by_head, BF16),
            pltpu.VMEM(by_head, BF16),
            pltpu.VMEM((rows, D), BF16),
            pltpu.VMEM((rows, D), BF16),
            pltpu.VMEM((rows, D), BF16),
            dma((2,)),
            dma((2, 2, planes - 1)),
            dma((groups,)),
            dma((groups,)),
            dma((groups, 2, 2)),
            dma((groups, 2, 2)),
            dma((groups, 2, planes - 1)),
            dma((groups, 2, planes - 1)),
            dma((READ_SLOTS,)),
            dma(()),
            dma(()),
            dma(()),
            dma((seqs // 2,)),
            dma((seqs // 2,)),
            dma((seqs,)),
            dma((seqs,)),
            dma((3, seqs)),
            dma((3, seqs)),
            dma((3,)),
            dma((3,)),
            dma((planes,)),
            dma((planes,)),
            dma((total, 2)),
            dma((total, 2)),
            dma((2,)),
        ],
        compiler_params=pltpu.CompilerParams(
            collective_id=3, has_side_effects=True, vmem_limit_bytes=60 * MIB
        ),
        name="backward_pass",
    )(windows, lengths, group, unit, whole, slope, *arrays)
    return outs[3:]


def dot_nt(left, right):
    return lax.dot_general(left, right, (((1,), (1,)), ((), ())), preferred_element_type=F32)


def dot_tn(left, right):
    return lax.dot_general(left, right, (((0,), (0,)), ((), ())), preferred_element_type=F32)


def dot_nn(left, right):
    return lax.dot_general(left, right, (((1,), (0,)), ((), ())), preferred_element_type=F32)


def only_head(values, head, head_count):
    if head_count == 1:
        return values
    lane = lax.broadcasted_iota(jnp.int32, values.shape, 1)
    inside = (lane >= head * HDIM) & (lane < (head + 1) * HDIM)
    return jnp.where(inside, values, jnp.zeros_like(values))


def stacked_heads(parts):
    whole = parts[0]
    row = lax.broadcasted_iota(jnp.int32, whole.shape, 0)
    for head in range(1, len(parts)):
        whole = jnp.where(row >= head * HDIM, parts[head], whole)
    return whole


def head_sums(values, head_count):
    turned = values.T
    return [
        jnp.sum(turned[head * HDIM : (head + 1) * HDIM], axis=0, keepdims=True)
        for head in range(head_count)
    ]


def attend_block(i, rows, head_count, offset, window, q_all, k_all, v_all, log_ref):
    scaled = q_all[i] * jnp.asarray(HDIM**-0.5, BF16)
    queries = [only_head(scaled, head, head_count) for head in range(head_count)]
    state = []
    for head in range(head_count):
        scores = dot_nt(k_all[i], queries[head])
        scores = jnp.where((offset <= 0) & (offset > -window), scores, NEG_FILL)
        best = jnp.max(scores, axis=0, keepdims=True)
        probs = jnp.exp(scores - best)
        state.append(
            (best, jnp.sum(probs, axis=0, keepdims=True), dot_tn(v_all[i], probs.astype(BF16)))
        )

    def key_block(b, running):
        keys, values = k_all[b], v_all[b]
        limit = (i - b) * rows - window
        renewed = []
        for head in range(head_count):
            best, total, gathered = running[head]
            scores = jnp.where(offset > limit, dot_nt(keys, queries[head]), NEG_FILL)
            new_best = jnp.maximum(best, jnp.max(scores, axis=0, keepdims=True))
            probs = jnp.exp(scores - new_best)
            keep = jnp.exp(best - new_best)
            renewed.append(
                (
                    new_best,
                    total * keep + jnp.sum(probs, axis=0, keepdims=True),
                    gathered * keep + dot_tn(values, probs.astype(BF16)),
                )
            )
        return tuple(renewed)

    state = lax.fori_loop(0, i, key_block, tuple(state))
    for head in range(head_count):
        best, total, _ = state[head]
        log_ref[i, head : head + 1] = best + jnp.log(total)
    return stacked_heads([gathered / total for _, total, gathered in state]).T


def attend_pairs(i, rows, head_count, window, qkv_all, log_ref):
    width = qkv_all.shape[3]
    scaled = qkv_all[0, i] * jnp.asarray(HDIM**-0.5, BF16)
    queries = jnp.concatenate([only_head(scaled, head, head_count) for head in range(head_count)], 0)
    columns = head_count * rows
    key_row = lax.broadcasted_iota(jnp.int32, (2 * rows, columns), 0)
    query_row = lax.rem(lax.broadcasted_iota(jnp.int32, (1, columns), 1), rows)
    last = lax.div(i, 2)

    def two_blocks(part, m):
        return qkv_all[part, pl.ds(pl.multiple_of(2 * m, 2), 2)].reshape(2 * rows, width)

    def one(step, running):
        m = last - step
        best, total, gathered = running
        reach = query_row + (i - 2 * m) * rows
        allowed = (key_row <= reach) & (key_row > reach - window)
        scores = jnp.where(allowed, dot_nt(two_blocks(1, m), queries), NEG_FILL)
        new_best = jnp.maximum(best, jnp.max(scores, axis=0, keepdims=True))
        probs = jnp.exp(scores - new_best)
        keep = jnp.exp(best - new_best)
        return (
            new_best,
            total * keep + jnp.sum(probs, axis=0, keepdims=True),
            gathered * keep + dot_tn(two_blocks(2, m), probs.astype(BF16)),
        )

    best, total, gathered = lax.fori_loop(
        0,
        last + 1,
        one,
        (
            jnp.full((1, columns), NEG_FILL, F32),
            jnp.zeros((1, columns), F32),
            jnp.zeros((width, columns), F32),
        ),
    )
    logs = best + jnp.log(total)
    gathered = gathered / total
    for head in range(head_count):
        log_ref[i, head : head + 1] = logs[:, head * rows : (head + 1) * rows]
    return stacked_heads(
        [gathered[:, head * rows : (head + 1) * rows] for head in range(head_count)]
    ).T


def cross_attend(length, query, keys, values):
    head_count = LANES // HDIM
    rows = query.shape[0]
    scaled = query * jnp.asarray(HDIM**-0.5, BF16)
    queries = jnp.concatenate([only_head(scaled, head, head_count) for head in range(head_count)], 0)
    scores = dot_nt(keys, queries)
    allowed = lax.broadcasted_iota(jnp.int32, scores.shape, 0) < length
    scores = jnp.where(allowed, scores, NEG_FILL)
    best = jnp.max(scores, axis=0, keepdims=True)
    probs = jnp.exp(scores - best)
    total = jnp.sum(probs, axis=0, keepdims=True)
    gathered = dot_tn(values, probs.astype(BF16)) / total
    logs = best + jnp.log(total)
    spans = [slice(head * rows, (head + 1) * rows) for head in range(head_count)]
    crossed = stacked_heads([gathered[:, span] for span in spans]).T
    return crossed, [logs[:, span] for span in spans]


def self_forward_kernel(
    seqs,
    window_ref,
    q_ref,
    k_ref,
    v_ref,
    joined_ref,
    q_all,
    k_all,
    v_all,
    attended_ref,
    log_ref,
    rounded,
    send_sem,
    recv_sem,
    back_send,
    back_recv,
):
    me, z = lax.axis_index("seq"), lax.axis_index("grp")
    rows, width = q_ref.shape[1], q_ref.shape[2]
    head_count = width // HDIM
    greet_all(me, seqs, lambda j: (j, z))
    pairs = ((q_ref, q_all), (k_ref, k_all), (v_ref, v_all))

    def outward(peer, slot, part):
        src, dst = pairs[part]
        return remote(
            src.at[peer], dst.at[slot], send_sem.at[part, peer], recv_sem.at[part, slot], (peer, z)
        )

    def start(step, carry):
        peer = lax.rem(me + step, seqs)
        for part in range(3):
            outward(peer, me, part).start()
        return carry

    lax.fori_loop(1, seqs, start, 0)
    for src, dst in pairs:
        dst[me] = src[me]
    window = window_ref[0]
    offset = lax.broadcasted_iota(jnp.int32, (rows, rows), 0) - lax.broadcasted_iota(
        jnp.int32, (rows, rows), 1
    )

    def backward_copy(peer, slot):
        return remote(
            rounded.at[peer], joined_ref.at[slot], back_send.at[peer], back_recv.at[slot], (peer, z)
        )

    def query_block(i, carry):
        @pl.when(i != me)
        def _():
            for part in range(3):
                outward(i, i, part).wait_recv()

        attended = attend_block(i, rows, head_count, offset, window, q_all, k_all, v_all, log_ref)
        attended_ref[i] = attended
        rounded[i] = attended.astype(BF16)

        @pl.when(i != me)
        def _():
            backward_copy(i, me).start()

        @pl.when(i == me)
        def _():
            joined_ref[i] = rounded[i]

        return carry

    lax.fori_loop(0, seqs, query_block, 0)

    def finish(step, carry):
        peer = lax.rem(me + step, seqs)
        for part in range(3):
            outward(peer, me, part).wait_send()
        backward_copy(peer, peer).wait()
        return carry

    lax.fori_loop(1, seqs, finish, 0)


def self_forward(seqs, windows, query, key, value):
    shape = query.shape
    head_count = shape[2] // HDIM
    dma = pltpu.SemaphoreType.DMA
    vmem = pl.BlockSpec(memory_space=pltpu.VMEM)
    return pl.pallas_call(
        functools.partial(self_forward_kernel, seqs),
        out_shape=(
            jax.ShapeDtypeStruct(shape, BF16),
            jax.ShapeDtypeStruct(shape, BF16),
            jax.ShapeDtypeStruct(shape, BF16),
            jax.ShapeDtypeStruct(shape, BF16),
            jax.ShapeDtypeStruct(shape, F32),
            jax.ShapeDtypeStruct((seqs, max(head_count, 8), shape[1]), F32),
        ),
        in_specs=[pl.BlockSpec(memory_space=pltpu.SMEM), vmem, vmem, vmem],
        out_specs=(vmem,) * 6,
        scratch_shapes=[
            pltpu.VMEM(shape, BF16),
            dma((3, seqs)),
            dma((3, seqs)),
            dma((seqs,)),
            dma((seqs,)),
        ],
        compiler_params=pltpu.CompilerParams(
            collective_id=5, has_side_effects=True, vmem_limit_bytes=40 * MIB
        ),
        name="self_forward",
    )(windows, query, key, value)


def key_grads(
    b, seqs, rows, head_count, offset, window,
    q_all, k_all, v_all, grad_all, log_ref, delta, dq_total,
):
    keys, values = k_all[b], v_all[b]
    width = keys.shape[1]
    scale = jnp.asarray(HDIM**-0.5, BF16)
    key_heads = [only_head(keys, head, head_count) for head in range(head_count)]

    def pair(i, sums, diagonal):
        dk, dv = sums
        scaled = q_all[i] * scale
        grads = grad_all[i]
        if diagonal:
            allowed = (offset <= 0) & (offset > -window)
        else:
            allowed = offset > (i - b) * rows - window
        dq = dq_total[i]
        for head in range(head_count):
            query = only_head(scaled, head, head_count)
            grad = only_head(grads, head, head_count)
            scores = jnp.where(allowed, dot_nt(keys, query), NEG_FILL)
            probs = jnp.exp(scores - log_ref[i, head : head + 1])
            spread = dot_nt(values, grad)
            grad_scores = (probs * (spread - delta[i, head : head + 1])).astype(BF16)
            dv = dv + dot_nn(probs.astype(BF16), grad)
            dk = dk + dot_nn(grad_scores, query)
            dq = dq + dot_tn(grad_scores, key_heads[head])
        dq_total[i] = dq
        return (dk, dv)

    zeros = jnp.zeros((rows, width), F32)
    sums = pair(b, (zeros, zeros), True)
    return lax.fori_loop(b + 1, seqs, lambda i, s: pair(i, s, False), sums)


def cross_grads(length, query, keys, values, grads, crossed, logs):
    head_count = LANES // HDIM
    rows = query.shape[0]
    scaled = query * jnp.asarray(HDIM**-0.5, BF16)
    queries = jnp.concatenate([only_head(scaled, head, head_count) for head in range(head_count)], 0)
    uppers = jnp.concatenate([only_head(grads, head, head_count) for head in range(head_count)], 0)
    deltas = jnp.concatenate(head_sums(grads.astype(F32) * crossed.astype(F32), head_count), 1)
    scores = dot_nt(keys, queries)
    allowed = lax.broadcasted_iota(jnp.int32, scores.shape, 0) < length
    probs = jnp.exp(jnp.where(allowed, scores, NEG_FILL) - jnp.concatenate(logs, 1))
    grad_scores = (probs * (dot_nt(values, uppers) - deltas)).astype(BF16)
    dv = dot_nn(probs.astype(BF16), uppers)
    dk = dot_nn(grad_scores, queries)
    spread = dot_tn(grad_scores, keys)
    dq = spread[:rows]
    lane = lax.broadcasted_iota(jnp.int32, dq.shape, 1)
    for head in range(1, head_count):
        dq = jnp.where(lane >= head * HDIM, spread[head * rows : (head + 1) * rows], dq)
    return dq * HDIM**-0.5, dk, dv


def self_backward_kernel(
    seqs,
    window_ref,
    grad_ref,
    q_all,
    k_all,
    v_all,
    attended_ref,
    log_ref,
    dq_ref,
    dk_ref,
    dv_ref,
    grad_all,
    delta,
    dq_total,
    dq_low,
    dk_low,
    dv_low,
    send_sem,
    recv_sem,
    back_send,
    back_recv,
):
    me, z = lax.axis_index("seq"), lax.axis_index("grp")
    rows, width = grad_ref.shape[1], grad_ref.shape[2]
    head_count = width // HDIM
    greet_all(me, seqs, lambda j: (j, z))

    def outward(peer, slot):
        return remote(
            grad_ref.at[peer], grad_all.at[slot], send_sem.at[peer], recv_sem.at[slot], (peer, z)
        )

    def start(step, carry):
        outward(lax.rem(me + step, seqs), me).start()
        return carry

    lax.fori_loop(1, seqs, start, 0)
    grad_all[me] = grad_ref[me]
    window = window_ref[0]
    offset = lax.broadcasted_iota(jnp.int32, (rows, rows), 0) - lax.broadcasted_iota(
        jnp.int32, (rows, rows), 1
    )

    def prepare(i, carry):
        @pl.when(i != me)
        def _():
            outward(i, i).wait_recv()

        sums = head_sums(grad_all[i].astype(F32) * attended_ref[i].astype(F32), head_count)
        for head in range(head_count):
            delta[i, head : head + 1] = sums[head]
        dq_total[i] = jnp.zeros((rows, width), F32)
        return carry

    lax.fori_loop(0, seqs, prepare, 0)
    outputs = ((dq_low, dq_ref), (dk_low, dk_ref), (dv_low, dv_ref))

    def returned(peer, slot, part):
        src, dst = outputs[part]
        return remote(
            src.at[peer], dst.at[slot], back_send.at[part, peer], back_recv.at[part, slot], (peer, z)
        )

    def key_block(step, carry):
        b = seqs - 1 - step
        dk, dv = key_grads(
            b, seqs, rows, head_count, offset, window,
            q_all, k_all, v_all, grad_all, log_ref, delta, dq_total,
        )
        dk_low[b] = dk.astype(BF16)
        dv_low[b] = dv.astype(BF16)

        @pl.when(b != me)
        def _():
            returned(b, me, 1).start()
            returned(b, me, 2).start()

        return carry

    lax.fori_loop(0, seqs, key_block, 0)

    def close(i, carry):
        dq_low[i] = (dq_total[i] * HDIM**-0.5).astype(BF16)

        @pl.when(i != me)
        def _():
            returned(i, me, 0).start()

        return carry

    lax.fori_loop(0, seqs, close, 0)
    for src, dst in outputs:
        dst[me] = src[me]

    def finish(step, carry):
        peer = lax.rem(me + step, seqs)
        outward(peer, me).wait_send()
        for part in range(3):
            returned(peer, peer, part).wait()
        return carry

    lax.fori_loop(1, seqs, finish, 0)


def self_backward(seqs, windows, grad, query_all, key_all, value_all, attended, logs):
    shape = grad.shape
    dma = pltpu.SemaphoreType.DMA
    vmem = pl.BlockSpec(memory_space=pltpu.VMEM)
    return pl.pallas_call(
        functools.partial(self_backward_kernel, seqs),
        out_shape=(jax.ShapeDtypeStruct(shape, BF16),) * 3,
        in_specs=[pl.BlockSpec(memory_space=pltpu.SMEM)] + [vmem] * 6,
        out_specs=(vmem,) * 3,
        scratch_shapes=[
            pltpu.VMEM(shape, BF16),
            pltpu.VMEM(logs.shape, F32),
            pltpu.VMEM(shape, F32),
            pltpu.VMEM(shape, BF16),
            pltpu.VMEM(shape, BF16),
            pltpu.VMEM(shape, BF16),
            dma((seqs,)),
            dma((seqs,)),
            dma((3, seqs)),
            dma((3, seqs)),
        ],
        compiler_params=pltpu.CompilerParams(
            collective_id=6, has_side_effects=True, vmem_limit_bytes=40 * MIB
        ),
        name="self_backward",
    )(windows, grad, query_all, key_all, value_all, attended, logs)


def cross_forward_kernel(length_ref, q_ref, k_ref, v_ref, crossed_ref, low_ref, log_ref):
    crossed, logs = cross_attend(length_ref[0], q_ref[...], k_ref[...], v_ref[...])
    for head in range(len(logs)):
        log_ref[0, head : head + 1] = logs[head]
    crossed_ref[...] = crossed
    low_ref[...] = crossed.astype(BF16)


def cross_forward(lengths, query, key, value):
    rows, width = query.shape
    blocks = width // LANES
    columns = lambda j: (0, j)
    return pl.pallas_call(
        cross_forward_kernel,
        grid=(blocks,),
        out_shape=(
            jax.ShapeDtypeStruct((rows, width), F32),
            jax.ShapeDtypeStruct((rows, width), BF16),
            jax.ShapeDtypeStruct((blocks, 8, rows), F32),
        ),
        in_specs=[
            pl.BlockSpec(memory_space=pltpu.SMEM),
            pl.BlockSpec((rows, LANES), columns),
            pl.BlockSpec((key.shape[0], LANES), columns),
            pl.BlockSpec((key.shape[0], LANES), columns),
        ],
        out_specs=(
            pl.BlockSpec((rows, LANES), columns),
            pl.BlockSpec((rows, LANES), columns),
            pl.BlockSpec((1, 8, rows), lambda j: (j, 0, 0)),
        ),
        name="cross_forward",
    )(lengths, query, key, value)


def cross_backward_kernel(
    length_ref, q_ref, k_ref, v_ref, grad_ref, crossed_ref, log_ref, dq_ref, dk_ref, dv_ref
):
    dq, dk, dv = cross_grads(
        length_ref[0],
        q_ref[...],
        k_ref[...],
        v_ref[...],
        grad_ref[...],
        crossed_ref[...],
        [log_ref[0, head : head + 1] for head in range(LANES // HDIM)],
    )
    dq_ref[...] = dq.astype(BF16)
    dk_ref[...] = dk.astype(BF16)
    dv_ref[...] = dv.astype(BF16)


def cross_backward(lengths, query, key, value, grad, crossed, logs):
    rows, width = query.shape
    keys = key.shape[0]
    columns = lambda j: (0, j)
    token_block = pl.BlockSpec((rows, LANES), columns)
    key_block = pl.BlockSpec((keys, LANES), columns)
    return pl.pallas_call(
        cross_backward_kernel,
        grid=(width // LANES,),
        out_shape=(
            jax.ShapeDtypeStruct((rows, width), BF16),
            jax.ShapeDtypeStruct((keys, width), BF16),
            jax.ShapeDtypeStruct((keys, width), BF16),
        ),
        in_specs=[
            pl.BlockSpec(memory_space=pltpu.SMEM),
            token_block,
            key_block,
            key_block,
            token_block,
            token_block,
            pl.BlockSpec((1, 8, rows), lambda j: (j, 0, 0)),
        ],
        out_specs=(token_block, key_block, key_block),
        name="cross_backward",
    )(lengths, query, key, value, grad, crossed, logs)


def memory_sum_kernel(seqs, parts_ref, total_ref, arrived, send_sem, recv_sem):
    me, z = lax.axis_index("seq"), lax.axis_index("grp")
    greet_all(me, seqs, lambda j: (j, z))

    def copy_of(peer, slot):
        return remote(
            parts_ref.at[peer], arrived.at[slot], send_sem.at[peer], recv_sem.at[slot], (peer, z)
        )

    def start(step, carry):
        copy_of(lax.rem(me + step, seqs), me).start()
        return carry

    def finish(step, carry):
        peer = lax.rem(me + step, seqs)
        copy_of(peer, peer).wait()
        return carry

    lax.fori_loop(1, seqs, start, 0)
    arrived[me] = parts_ref[me]
    lax.fori_loop(1, seqs, finish, 0)
    total = arrived[0].astype(F32)
    for j in range(1, seqs):
        total = total + arrived[j].astype(F32)
    total_ref[...] = total.astype(BF16)


def memory_sum(seqs, parts):
    dma = pltpu.SemaphoreType.DMA
    vmem = pl.BlockSpec(memory_space=pltpu.VMEM)
    return pl.pallas_call(
        functools.partial(memory_sum_kernel, seqs),
        out_shape=jax.ShapeDtypeStruct(parts.shape[1:], BF16),
        in_specs=[vmem],
        out_specs=vmem,
        scratch_shapes=[pltpu.VMEM(parts.shape, BF16), dma((seqs,)), dma((seqs,))],
        compiler_params=pltpu.CompilerParams(
            collective_id=7, has_side_effects=True, vmem_limit_bytes=32 * MIB
        ),
        name="memory_sum",
    )(parts)


def tiled_layer(
    tokens, memory, cotangent, windows, mem_lengths, owners, master, vectors
):
    rows = tokens.shape[1]
    mem_rows = memory.shape[1]
    seqs, planes = lax.axis_size("seq"), lax.axis_size("grp")
    holder, slot, group, unit = owner_tables(owners, master.shape[0], seqs * planes)
    memory_padded = jnp.pad(memory.reshape(mem_rows, D), ((0, -mem_rows % 16), (0, 0)))
    flat = tokens.reshape(rows, D)
    (
        whole,
        h1,
        joined,
        qkv,
        attended,
        logs,
        x2,
        h2,
        cross_queries,
        mem_acts,
        crossed,
        cross_logs,
        x3,
        h3,
        activation,
        slope,
        mixed,
    ) = forward_pass(
        seqs,
        planes,
        windows,
        mem_lengths,
        holder,
        slot,
        master,
        flat,
        memory_padded,
        seqs * mem_rows,
        vectors,
    )
    grad_slots, grad_tokens, grad_memory, vector_sums = backward_pass(
        seqs,
        planes,
        windows,
        mem_lengths,
        group,
        unit,
        whole,
        slope,
        (
            cotangent.reshape(rows, D),
            flat,
            x2,
            x3,
            h1,
            h2,
            h3,
            activation,
            crossed,
            cross_queries,
            mem_acts,
            cross_logs,
            joined,
            attended,
            qkv,
            logs,
            memory_padded,
            vectors,
        ),
    )
    return (
        mixed.reshape(tokens.shape),
        grad_tokens.reshape(tokens.shape),
        grad_memory[:mem_rows].reshape(memory.shape),
        grad_slots,
        vector_sums[: vectors.shape[0]],
    )


def plain_layer(
    tokens, memory, cotangent, windows, mem_lengths, owners, master, vectors
):
    rows = tokens.shape[1]
    seqs, planes = lax.axis_size("seq"), lax.axis_size("grp")
    units = owners.shape[0]
    slot_count, unit_rows = (master.shape[0], master.shape[1])
    bias_rows = FF // D
    placed, unit_at, occupied = slot_tables(owners, slot_count, seqs * planes)
    gathered = lax.all_gather(master.astype(BF16), ("seq", "grp"), axis=0, tiled=True)
    stacked = jnp.take(gathered, placed, axis=0).reshape(-1, D)
    memory_whole = lax.all_gather(memory[0], "seq", axis=0, tiled=True)
    self_query, self_key, self_value, self_out = (stacked[i * D : (i + 1) * D] for i in range(4))
    cross_query, cross_key, cross_value, cross_out = (
        stacked[i * D : (i + 1) * D] for i in range(4, 8)
    )
    hidden_in, hidden_out = stacked[8 * D : 8 * D + FF], stacked[8 * D + FF :]

    def by_device(tensor):
        return jnp.swapaxes(tensor.reshape(rows, seqs, D // seqs), 0, 1)

    def by_token(tensor):
        return jnp.swapaxes(tensor, 0, 1).reshape(rows, D)

    stream = tokens.astype(F32).reshape(rows, D)
    normed_one, form_one, inverse_one = norm_forward(stream, vectors[0], vectors[1])
    normed_self = normed_one.astype(BF16)
    query_act = (product(normed_self, self_query) + vectors[6]).astype(BF16)
    key_act = product(normed_self, self_key).astype(BF16)
    value_act = (product(normed_self, self_value) + vectors[7]).astype(BF16)
    joined, query_all, key_all, value_all, attended32, logs = self_forward(
        seqs, windows, by_device(query_act), by_device(key_act), by_device(value_act)
    )
    attended = by_token(joined)
    after_self = stream + product(attended, self_out) + vectors[8]
    normed_two, form_two, inverse_two = norm_forward(after_self, vectors[2], vectors[3])
    normed_cross = normed_two.astype(BF16)
    cross_queries = (product(normed_cross, cross_query) + vectors[9]).astype(BF16)
    mem_key_act = product(memory_whole, cross_key).astype(BF16)
    mem_value_act = (product(memory_whole, cross_value) + vectors[10]).astype(BF16)
    crossed32, crossed, cross_logs = cross_forward(
        mem_lengths, cross_queries, mem_key_act, mem_value_act
    )
    after_cross = after_self + product(crossed, cross_out) + vectors[11]
    normed_three, form_three, inverse_three = norm_forward(after_cross, vectors[4], vectors[5])
    normed_mlp = normed_three.astype(BF16)
    pre_act = product_nt(normed_mlp, hidden_in) + vectors[12 : 12 + bias_rows].reshape(FF)
    activation, slope = jax.jvp(gelu_exact, (pre_act,), (jnp.ones_like(pre_act),))
    activation_bf = activation.astype(BF16)
    result_rows = after_cross + product(activation_bf, hidden_out) + vectors[12 + bias_rows]
    mixed = result_rows.astype(BF16).reshape(tokens.shape)
    grad_out_bf = cotangent.reshape(rows, D)
    grad_stream = cotangent.astype(F32).reshape(rows, D)
    grad_hidden_out = product_tn(activation_bf, grad_out_bf)
    grad_down_bias = jnp.sum(grad_stream, axis=0)
    grad_activation = product_nt(grad_out_bf, hidden_out)
    grad_pre = (grad_activation * slope).astype(BF16)
    grad_hidden_in = product_tn(grad_pre, normed_mlp)
    grad_up_bias = jnp.sum(grad_pre.astype(F32), axis=0)
    grad_normed_mlp = product(grad_pre, hidden_in)
    back_three, grad_gain_three, grad_shift_three = norm_backward(
        grad_normed_mlp, form_three, inverse_three, vectors[4]
    )
    grad_after_cross = grad_stream + back_three
    grad_cross_branch = grad_after_cross.astype(BF16)
    grad_cross_out = product_tn(crossed, grad_cross_branch)
    grad_cross_out_bias = jnp.sum(grad_cross_branch.astype(F32), axis=0)
    grad_crossed = product_nt(grad_cross_branch, cross_out).astype(BF16)
    grad_cross_queries, part_mem_keys, part_mem_values = cross_backward(
        mem_lengths, cross_queries, mem_key_act, mem_value_act, grad_crossed, crossed32, cross_logs
    )
    mem_rows = memory.shape[1]
    mem_parts = jnp.concatenate(
        [part_mem_keys.reshape(seqs, mem_rows, D), part_mem_values.reshape(seqs, mem_rows, D)],
        axis=1,
    )
    mem_sums = memory_sum(seqs, mem_parts)
    mem_flat = memory.reshape(-1, D)
    mem_keys_flat = mem_sums[:mem_rows]
    mem_values_flat = mem_sums[mem_rows:]
    grad_cross_key = product_tn(mem_flat, mem_keys_flat)
    grad_cross_value = product_tn(mem_flat, mem_values_flat)
    grad_cross_value_bias = jnp.sum(mem_values_flat.astype(F32), axis=0)
    grad_memory = (
        product_nt(mem_keys_flat, cross_key) + product_nt(mem_values_flat, cross_value)
    ).reshape(memory.shape)
    grad_cross_query = product_tn(normed_cross, grad_cross_queries)
    grad_cross_query_bias = jnp.sum(grad_cross_queries.astype(F32), axis=0)
    grad_normed_cross = product_nt(grad_cross_queries, cross_query)
    back_two, grad_gain_two, grad_shift_two = norm_backward(
        grad_normed_cross, form_two, inverse_two, vectors[2]
    )
    grad_after_self = grad_after_cross + back_two
    grad_self_branch = grad_after_self.astype(BF16)
    grad_self_out = product_tn(attended, grad_self_branch)
    grad_self_out_bias = jnp.sum(grad_self_branch.astype(F32), axis=0)
    grad_attended = product_nt(grad_self_branch, self_out).astype(BF16)
    grad_queries, grad_keys, grad_values = (
        by_token(part)
        for part in self_backward(
            seqs, windows, by_device(grad_attended), query_all, key_all, value_all, attended32, logs
        )
    )
    grad_self_query = product_tn(normed_self, grad_queries)
    grad_self_key = product_tn(normed_self, grad_keys)
    grad_self_value = product_tn(normed_self, grad_values)
    grad_query_bias = jnp.sum(grad_queries.astype(F32), axis=0)
    grad_value_bias = jnp.sum(grad_values.astype(F32), axis=0)
    grad_normed_self = (
        product_nt(grad_queries, self_query)
        + product_nt(grad_keys, self_key)
        + product_nt(grad_values, self_value)
    )
    back_one, grad_gain_one, grad_shift_one = norm_backward(
        grad_normed_self, form_one, inverse_one, vectors[0]
    )
    grad_tokens = (grad_after_self + back_one).reshape(tokens.shape)
    grad_matrices = jnp.concatenate(
        [
            part.astype(BF16)
            for part in (
                grad_self_query,
                grad_self_key,
                grad_self_value,
                grad_self_out,
                grad_cross_query,
                grad_cross_key,
                grad_cross_value,
                grad_cross_out,
                grad_hidden_in,
                grad_hidden_out,
            )
        ],
        axis=0,
    )
    grad_units = grad_matrices.reshape(units, unit_rows, D)
    small_rows = jnp.stack(
        [
            grad_gain_one,
            grad_shift_one,
            grad_gain_two,
            grad_shift_two,
            grad_gain_three,
            grad_shift_three,
            grad_query_bias,
            grad_value_bias,
            grad_self_out_bias,
            grad_cross_query_bias,
            grad_cross_value_bias,
            grad_cross_out_bias,
        ]
    )
    grad_vectors = jnp.concatenate(
        [small_rows, grad_up_bias.reshape(bias_rows, D), grad_down_bias[None]], axis=0
    )
    grad_slots = lax.psum_scatter(
        jnp.where(
            occupied[:, None, None], jnp.take(grad_units, unit_at, axis=0), jnp.zeros((), BF16)
        ),
        ("seq", "grp"),
        scatter_dimension=0,
        tiled=True,
    )
    grad_vectors = lax.psum(grad_vectors, ("seq", "grp"))
    return mixed, grad_tokens, grad_memory, grad_slots, grad_vectors


def local(
    tokens,
    memory,
    cotangent,
    windows,
    mem_lengths,
    owners,
    master,
    first_moment,
    second_moment,
    vectors,
    vec_first,
    vec_second,
):
    tiled = lax.axis_size("seq") == 8 and master.shape[1] % (32 * lax.axis_size("grp")) == 0
    layer = tiled_layer if tiled else plain_layer
    mixed, grad_tokens, grad_memory, grad_slots, grad_vectors = layer(
        tokens, memory, cotangent, windows, mem_lengths, owners, master, vectors
    )
    grad_slots = grad_slots.astype(F32)
    new_first, new_second, new_master = adam_step(
        master, first_moment, second_moment, grad_slots, RATE_MATRIX, WEIGHT_DECAY
    )
    master_copy = new_master.astype(BF16)
    vec_first_out, vec_second_out, vectors_out = adam_step(
        vectors, vec_first, vec_second, grad_vectors, RATE_VECTOR, 0.0
    )
    grad_out_bias = grad_vectors[vectors.shape[0] - 1]
    return (
        mixed,
        grad_tokens,
        grad_memory,
        new_first,
        new_second,
        new_master,
        master_copy,
        vec_first_out,
        vec_second_out,
        vectors_out,
        grad_out_bias,
    )


def solution(mesh):
    placed = (
        P("grp", "seq", None),
        P("grp", "seq", None),
        P("grp", "seq", None),
        P("grp"),
        P("grp"),
        P(),
        P(("seq", "grp"), None, None),
        P(("seq", "grp"), None, None),
        P(("seq", "grp"), None, None),
        P(),
        P(),
        P(),
    )
    return jax.shard_map(
        local,
        mesh=mesh,
        in_specs=placed,
        out_specs=(
            P("grp", "seq", None),
            P("grp", "seq", None),
            P("grp", "seq", None),
            P(("seq", "grp"), None, None),
            P(("seq", "grp"), None, None),
            P(("seq", "grp"), None, None),
            P(("seq", "grp"), None, None),
            P(),
            P(),
            P(),
            P(),
        ),
        check_vma=False,
    )
```

```python
import functools

import jax
import jax.numpy as jnp
from jax import lax
from jax.experimental import pallas as pl
from jax.experimental.pallas import tpu as pltpu
from jax.sharding import PartitionSpec as P

D = 1024
FF = 4096
HEADS = 16
HDIM = 64
STEP = 10


NEG_FILL = -1e30
NORM_EPS = 1e-05
BETA_ONE = 0.5
BETA_TWO = 0.75
RATE_MATRIX = 0.03
RATE_VECTOR = 0.4
WEIGHT_DECAY = 0.01
ADAM_EPS = 1e-08

BF16 = jnp.bfloat16
F32 = jnp.float32
LANES = 128
GROUP_UNITS = 4
GATHER_LIGHT = 4
REDUCE_LIGHT = 4
MIB = 1 << 20


def product(left, right):
    return jnp.dot(left, right, preferred_element_type=F32)


def product_tn(left, right):
    return jnp.einsum("rd,re->de", left, right, preferred_element_type=F32)


def product_nt(left, right):
    return jnp.einsum("rd,ed->re", left, right, preferred_element_type=F32)


def slot_tables(owners, slot_count, holders):
    unit_count = owners.shape[0]
    positions = lax.iota(jnp.int32, unit_count)
    same_owner = owners[None, :] == owners[:, None]
    slot_rank = jnp.sum(
        (same_owner & (positions[None, :] < positions[:, None])).astype(jnp.int32), axis=1
    )
    placed = owners * slot_count + slot_rank
    slot_ids = lax.iota(jnp.int32, holders * slot_count)
    matches = slot_ids[:, None] == placed[None, :]
    occupied = jnp.sum(matches.astype(jnp.int32), axis=1) > 0
    unit_at = jnp.sum(jnp.where(matches, positions[None, :], 0), axis=1)
    return (placed, unit_at, occupied)


def norm_forward(stream, gain_row, shift_row):
    row_mean = jnp.mean(stream, axis=-1, keepdims=True)
    centered = stream - row_mean
    inverse = lax.rsqrt(jnp.mean(centered * centered, axis=-1, keepdims=True) + NORM_EPS)
    normal_form = centered * inverse
    return (normal_form * gain_row + shift_row, normal_form, inverse)


def norm_backward(upstream, normal_form, inverse, gain_row):
    scaled = upstream * gain_row
    first_term = jnp.mean(scaled, axis=-1, keepdims=True)
    second_term = jnp.mean(scaled * normal_form, axis=-1, keepdims=True)
    grad_in = inverse * (scaled - first_term - normal_form * second_term)
    return (grad_in, jnp.sum(upstream * normal_form, axis=0), jnp.sum(upstream, axis=0))


def gelu_exact(values):
    return jax.nn.gelu(values, approximate=False)


def adam_step(weight, first, second_in, upstream, rate, decay):
    first_new = BETA_ONE * first + (1.0 - BETA_ONE) * upstream
    second_new = BETA_TWO * second_in + (1.0 - BETA_TWO) * upstream * upstream
    first_hat = first_new / (1.0 - BETA_ONE**STEP)
    second_hat = second_new / (1.0 - BETA_TWO**STEP)
    weight_new = weight - rate * (first_hat / (jnp.sqrt(second_hat) + ADAM_EPS) + decay * weight)
    return (first_new, second_new, weight_new)


def remote(src, dst, send_sem, recv_sem, target):
    return pltpu.make_async_remote_copy(
        src_ref=src,
        dst_ref=dst,
        send_sem=send_sem,
        recv_sem=recv_sem,
        device_id=target,
        device_id_type=pl.DeviceIdType.MESH,
    )


def greet_all(me, total, target_of):
    barrier = pltpu.get_barrier_semaphore()

    def signal(step, carry):
        pl.semaphore_signal(
            barrier,
            inc=1,
            device_id=target_of(lax.rem(me + step, total)),
            device_id_type=pl.DeviceIdType.MESH,
        )
        return carry

    lax.fori_loop(1, total, signal, 0)
    pl.semaphore_wait(barrier, total - 1)


class Place:
    def __init__(self, planes):
        self.seq = lax.axis_index("seq")
        self.z = lax.axis_index("grp")
        self.planes = planes
        self.core = lax.rem(self.seq, 2)
        self.x = lax.rem(lax.div(self.seq, 2), 2)
        self.y = lax.div(self.seq, 4)

    def at(self, core, x, y, z):
        return (y * 4 + x * 2 + core, z)

    def sibling(self):
        return self.at(1 - self.core, self.x, self.y, self.z)

    def x_peer(self):
        return self.at(self.core, 1 - self.x, self.y, self.z)

    def y_peer(self):
        return self.at(self.core, self.x, 1 - self.y, self.z)

    def above(self):
        return (self.seq, self.z + 1)

    def below(self):
        return (self.seq, self.z - 1)

    def peers(self, half):
        return (self.x_peer(), self.y_peer()) if half == 0 else (self.y_peer(), self.x_peer())

    def bits(self, half):
        return (self.y, self.x) if half == 0 else (self.x, self.y)


def tile_of(device, planes, half, unit_rows):
    seq, z = lax.div(device, planes), lax.rem(device, planes)
    core, x, y = lax.rem(seq, 2), lax.rem(lax.div(seq, 2), 2), lax.div(seq, 4)
    wide, narrow = jnp.where(half == 0, y, x), jnp.where(half == 0, x, y)
    half_rows = unit_rows // 2
    block = half_rows // planes
    first_row = pl.multiple_of(half * half_rows + z * block, block)
    first_column = pl.multiple_of((core * 4 + wide * 2 + narrow) * LANES, LANES)
    return (pl.ds(first_row, block), pl.ds(first_column, LANES))


def loop(first, last, work):
    def one(index, carry):
        work(index)
        return carry

    lax.fori_loop(first, last, one, 0)


class Gather:
    def __init__(self, planes, own_ref, whole_ref, own_sem, z_send, z_recv, p_send, p_recv):
        self.place = Place(planes)
        self.planes = planes
        self.z = self.place.z
        self.own_ref, self.whole_ref = own_ref, whole_ref
        self.own_sem = own_sem
        self.z_send, self.z_recv = z_send, z_recv
        self.p_send, self.p_recv = p_send, p_recv
        self.groups = whole_ref.shape[0]
        self.split = GATHER_LIGHT
        self.leave = 1 + 2 * (planes - 1)
        self.arrived = self.leave + 3

    def block(self, g, half, plane):
        wide, narrow = self.place.bits(half)
        first = self.place.core * 4 + wide * 2 + narrow
        return self.whole_ref.at[g, half, first, plane]

    def pair(self, g, half, plane):
        wide, narrow = self.place.bits(half)
        return self.whole_ref.at[g, half, pl.ds(self.place.core * 4 + wide * 2, 2), plane]

    def line(self, g, half, way, hop, plane, light):
        ref = self.block(g, half, plane) if light else self.pair(g, half, plane)
        return remote(
            self.own_ref.at[g, half] if light and hop == 0 else ref,
            ref,
            self.z_send.at[g, half, way, hop],
            self.z_recv.at[g, half, way, hop],
            self.place.above() if way == 0 else self.place.below(),
        )

    def planar(self, g, half, order, light, arriving=False):
        wide, narrow = self.place.bits(half)
        core = self.place.core
        if order == 0:
            first = core * 4 + wide * 2 + (1 - narrow if arriving else narrow)
            if light:
                ref = src = self.whole_ref.at[g, half, first]
            else:
                ref = self.whole_ref.at[g, half, first, self.z]
                src = self.own_ref.at[g, half]
        else:
            if order == 1:
                first, columns = core * 4 + (1 - wide if arriving else wide) * 2, 2
            else:
                first, columns = (1 - core if arriving else core) * 4, 4
            ref = src = self.whole_ref.at[g, half, pl.ds(first, columns)]
        target = self.place.peers(half)[order] if order < 2 else self.place.sibling()
        return remote(
            src, ref, self.p_send.at[g, half, order], self.p_recv.at[g, half, order], target
        )

    def own_copy(self, g, half):
        return pltpu.make_async_copy(
            self.own_ref.at[g, half],
            self.block(g, half, self.z),
            self.own_sem.at[g, half],
        )

    def enter_line(self, g, half, light):
        z = self.z

        @pl.when(z < self.planes - 1)
        def _():
            self.line(g, half, 0, 0, z, light).start()

        @pl.when(z > 0)
        def _():
            self.line(g, half, 1, 0, z, light).start()

    def hop(self, g, half, k, light):
        z, planes = self.z, self.planes

        @pl.when(z >= k)
        def _():
            self.line(g, half, 0, k - 1, z - k, light).wait_recv()

        if k < planes - 1:

            @pl.when((z >= k) & (z < planes - 1))
            def _():
                self.line(g, half, 0, k, z - k, light).start()

        @pl.when(z + k < planes)
        def _():
            self.line(g, half, 1, k - 1, z + k, light).wait_recv()

        if k < planes - 1:

            @pl.when((z + k < planes) & (z > 0))
            def _():
                self.line(g, half, 1, k, z + k, light).start()

    def exchange(self, g, half, order, light):
        self.planar(g, half, order, light, arriving=True).wait_recv()
        if order < 2:
            self.planar(g, half, order + 1, light).start()

    def heavy_start(self, g, half):
        self.own_copy(g, half).start()
        self.planar(g, half, 0, False).start()

    def heavy_enter(self, g, half):
        self.own_copy(g, half).wait()
        self.planar(g, half, 0, False, arriving=True).wait_recv()
        self.enter_line(g, half, False)

    def heavy_leave(self, g, half):
        self.hop(g, half, self.planes - 1, False)
        self.planar(g, half, 1, False).start()

    def light_start(self, g, half):
        self.own_copy(g, half).start()
        self.enter_line(g, half, True)

    def light_leave(self, g, half):
        self.hop(g, half, self.planes - 1, True)
        self.own_copy(g, half).wait()
        self.planar(g, half, 0, True).start()

    def tick(self, t):
        planes, leave = self.planes, self.leave

        def during(lag, action, first, last):
            g = t - lag

            @pl.when((g >= first) & (g < last))
            def _():
                for half in range(2):
                    action(g, half)

        def heavy(lag, action):
            during(lag, action, self.split, self.groups)

        def light(lag, action):
            during(lag, action, 0, self.split)

        during(leave + 3, lambda g, half: self.exchange(g, half, 2, False), 0, self.groups)
        during(leave + 2, lambda g, half: self.exchange(g, half, 1, False), 0, self.groups)
        heavy(leave, self.heavy_leave)
        light(leave, lambda g, half: self.exchange(g, half, 0, True))
        for k in reversed(range(1, planes - 1)):
            heavy(1 + 2 * k, lambda g, half, k=k: self.hop(g, half, k, False))
        light(leave - 2, self.light_leave)
        for k in reversed(range(1, planes - 1)):
            light(1 + k, lambda g, half, k=k: self.hop(g, half, k, True))
        heavy(1, self.heavy_enter)
        heavy(0, self.heavy_start)
        light(0, self.light_start)

    def drain(self):
        z, planes = self.z, self.planes

        def one(g, light):
            for half in range(2):
                for k in range(planes - 1):

                    @pl.when((z >= k) & (z < planes - 1))
                    def _(half=half, k=k):
                        self.line(g, half, 0, k, z - k, light).wait_send()

                    @pl.when((z + k < planes) & (z > 0))
                    def _(half=half, k=k):
                        self.line(g, half, 1, k, z + k, light).wait_send()

                for order in range(3):
                    self.planar(g, half, order, light).wait_send()

        loop(0, self.split, lambda g: one(g, True))
        loop(self.split, self.groups, lambda g: one(g, False))


def gather_scratch(planes, groups):
    dma = pltpu.SemaphoreType.DMA
    return [
        dma((groups, 2)),
        dma((groups, 2, 2, planes - 1)),
        dma((groups, 2, 2, planes - 1)),
        dma((groups, 2, 3)),
        dma((groups, 2, 3)),
    ]


NORM_ROWS = 32


def norm_into(stream_ref, gain_row, shift_row, out_ref):
    def one(block):
        span = pl.ds(pl.multiple_of(block * NORM_ROWS, NORM_ROWS), NORM_ROWS)
        normed = norm_forward(stream_ref[span].astype(F32), gain_row, shift_row)[0]
        out_ref[span] = normed.astype(BF16)

    loop(0, out_ref.shape[0] // NORM_ROWS, one)


def weight_block(weight_ref, slot, block, unit):
    halves, planes = weight_ref.shape[1], weight_ref.shape[3]
    return [weight_ref[slot, h, block, p, unit] for h in range(halves) for p in range(planes)]


def dot_tiles(left, weight_ref, slot, emit, turned=False, unrolled=False):
    blocks, units = weight_ref.shape[2], weight_ref.shape[4]

    def one(j, carry):
        if turned:
            weight = jnp.concatenate(
                [jnp.concatenate(weight_block(weight_ref, slot, b, j), 0) for b in range(blocks)], 1
            )
            emit(j, dot_nt(left, weight))
        else:
            weight = jnp.concatenate(
                [
                    jnp.concatenate(
                        sum(
                            (weight_block(weight_ref, slot, 2 * j + b, u) for u in range(units)),
                            [],
                        ),
                        0,
                    )
                    for b in range(2)
                ],
                1,
            )
            emit(j, dot_nn(left, weight))
        return carry

    if unrolled:
        for j in range(4):
            one(j, 0)
    else:
        lax.fori_loop(0, 4, one, 0)


TRAVEL = (0, 1, 2, 3, 5, 6, 4, 7, 8, 9, 10, 11, 12, 13, 14, 15)
REDUCE = (12, 13, 14, 15, 8, 9, 10, 11, 7, 4, 3, 5, 6, 0, 1, 2)


def tables_kernel(slots, owners_ref, holder_ref, slot_ref, group_ref, unit_ref, count):
    holders = count.shape[0]

    def clear(n, carry):
        count[n] = 0
        for s in range(slots):
            group_ref[n * slots + s] = -1
            unit_ref[n * slots + s] = 0
        return carry

    lax.fori_loop(0, holders, clear, 0)
    for unit in range(owners_ref.shape[0]):
        matrix, part = divmod(unit, GROUP_UNITS)
        owner = owners_ref[unit]
        slot = count[owner]
        count[owner] = slot + 1
        travel = TRAVEL.index(matrix) * GROUP_UNITS + part
        holder_ref[travel] = owner
        slot_ref[travel] = slot
        group_ref[owner * slots + slot] = REDUCE.index(matrix)
        unit_ref[owner * slots + slot] = part


def owner_tables(owners, slots, holders):
    units = owners.shape[0]
    smem = pl.BlockSpec(memory_space=pltpu.SMEM)
    return pl.pallas_call(
        functools.partial(tables_kernel, slots),
        out_shape=(jax.ShapeDtypeStruct((units,), jnp.int32),) * 2
        + (jax.ShapeDtypeStruct((holders * slots,), jnp.int32),) * 2,
        in_specs=[smem],
        out_specs=(smem,) * 4,
        scratch_shapes=[pltpu.SMEM((holders,), jnp.int32)],
        name="owner_tables",
    )(owners)


def forward_kernel(
    seqs,
    planes,
    window_ref,
    length_ref,
    holder_ref,
    slot_ref,
    master_ref,
    tokens_ref,
    memory_ref,
    vectors_ref,
    whole_ref,
    h1_ref,
    joined_ref,
    qkv_all,
    rounded,
    log_ref,
    x2_ref,
    h2_ref,
    cq_ref,
    mem_ref,
    crossed_low_ref,
    cross_log_ref,
    x3_ref,
    h3_ref,
    act_ref,
    slope_ref,
    mixed_ref,
    padded_ref,
    master_wide,
    master_low,
    tiles,
    own,
    memory_came,
    memory_wide,
    memory_all,
    weights,
    qkv_out,
    down,
    own_sem,
    z_send,
    z_recv,
    p_send,
    p_recv,
    load_sem,
    master_sem,
    tile_send,
    tile_recv,
    memory_send,
    memory_recv,
    send_sem,
    recv_sem,
    back_send,
    back_recv,
):
    fetch = pltpu.make_async_copy(master_ref, master_wide, master_sem)
    fetch.start()
    gather = Gather(planes, own, whole_ref, own_sem, z_send, z_recv, p_send, p_recv)
    place = gather.place
    me, z = place.seq, place.z
    rows = tokens_ref.shape[0]
    width = D // seqs
    tile = 2 * LANES
    total = seqs * planes
    here = me * planes + z
    mem_rows = memory_all.shape[0] // seqs
    greet_all(here, total, lambda j: (lax.div(j, planes), lax.rem(j, planes)))

    def vector(index):
        return vectors_ref[index : index + 1]

    def columns_of(j):
        return pl.ds(pl.multiple_of(j * tile, tile), tile)

    def tile_copy(peer, slot, half):
        tile_rows, tile_columns = tile_of(peer, planes, half, master_low.shape[1])
        return remote(
            master_low.at[:, tile_rows, tile_columns],
            tiles.at[slot, half],
            tile_send.at[peer, half],
            tile_recv.at[slot, half],
            (lax.div(peer, planes), lax.rem(peer, planes)),
        )

    def memory_copy(peer, slot):
        return remote(
            padded_ref, memory_came.at[slot], memory_send.at[peer], memory_recv.at[slot], (peer, z)
        )

    def spread():
        own_memory = memory_ref[...].astype(F32)
        if padded_ref.shape[0] > mem_rows:
            fill = jnp.zeros((padded_ref.shape[0] - mem_rows, D), F32)
            own_memory = jnp.concatenate([own_memory, fill], 0)
        padded_ref[...] = own_memory.astype(BF16)
        fetch.wait()
        part = 64

        def lower(index):
            slot, block = lax.div(index, master_low.shape[1] // part), lax.rem(
                index, master_low.shape[1] // part
            )
            span = pl.ds(pl.multiple_of(block * part, part), part)
            master_low[slot, span] = master_wide[slot, span].astype(BF16)

        loop(0, master_low.shape[0] * master_low.shape[1] // part, lower)

        def start(step):
            peer = lax.rem(here + step, total)
            loop(0, 2, lambda half: tile_copy(peer, here, half).start())

        loop(1, total, start)
        loop(1, seqs, lambda step: memory_copy(lax.rem(me + step, seqs), me).start())

        def keep_own(half):
            tile_rows, tile_columns = tile_of(here, planes, half, master_low.shape[1])
            tiles[here, half] = master_low[:, tile_rows, tile_columns]

        loop(0, 2, keep_own)
        memory_came[me] = padded_ref[...]
        norm_into(tokens_ref, vector(0), vector(1), h1_ref)

        def finish_memory(step):
            peer = lax.rem(me + step, seqs)
            memory_copy(peer, peer).wait()

        loop(1, seqs, finish_memory)

        def widen(j):
            span = pl.ds(pl.multiple_of(j * mem_rows, 8), mem_rows)
            memory_wide[span] = memory_came[j].astype(F32)[:mem_rows]

        loop(0, seqs, widen)

        def narrow(block):
            span = pl.ds(pl.multiple_of(block * part, part), part)
            memory_all[span] = memory_wide[span].astype(BF16)

        loop(0, memory_all.shape[0] // part, narrow)

        def finish(step):
            peer = lax.rem(here + total - step, total)
            loop(0, 2, lambda half: tile_copy(peer, peer, half).wait())

        loop(1, total, finish)

        def keep(unit):
            g, u = lax.div(unit, GROUP_UNITS), lax.rem(unit, GROUP_UNITS)
            for half in range(2):
                own[g, half, u] = tiles[holder_ref[unit], half, slot_ref[unit]]

        loop(0, holder_ref.shape[0], keep)

    def load(position, slot):
        return pltpu.make_async_copy(whole_ref.at[position], weights.at[slot], load_sem.at[slot])

    def outward(part, peer, slot):
        return remote(
            qkv_out.at[part, peer],
            qkv_all.at[part, slot],
            send_sem.at[part, peer],
            recv_sem.at[part, slot],
            (peer, z),
        )

    def backward_copy(peer, slot):
        return remote(
            rounded.at[peer],
            joined_ref.at[:, pl.ds(pl.multiple_of(slot * width, width), width)],
            back_send.at[peer],
            back_recv.at[slot],
            (peer, z),
        )

    def project(part):
        load(part, part).start()
        load(part, part).wait()
        bias_row = 6 + lax.div(part, 2)

        def emit(j, result):
            bias = vectors_ref[pl.ds(bias_row, 1), columns_of(j)]
            result = (result + jnp.where(part == 1, 0.0, bias)).astype(BF16)
            for piece in range(tile // width):
                qkv_out[part, j * (tile // width) + piece] = result[
                    :, piece * width : (piece + 1) * width
                ]

        dot_tiles(h1_ref[...], weights, part, emit, unrolled=True)
        loop(1, seqs, lambda step: outward(part, lax.rem(me + step, seqs), me).start())
        qkv_all[part, me] = qkv_out[part, me]

    head_count = width // HDIM

    def query_block(i):
        def arrive(ahead):
            @pl.when((lax.rem(i, 2) == 0) & (i + ahead != me))
            def _():
                loop(0, 3, lambda part: outward(part, i + ahead, i + ahead).wait_recv())

        loop(0, 2, arrive)
        rounded[i] = attend_pairs(i, rows, head_count, window_ref[0], qkv_all, log_ref).astype(BF16)

        @pl.when(i != me)
        def _():
            backward_copy(i, me).start()

        @pl.when(i == me)
        def _():
            joined_ref[:, pl.ds(pl.multiple_of(i * width, width), width)] = rounded[i]

    def after_self():
        def arrive(step):
            peer = lax.rem(me + step, seqs)
            backward_copy(peer, peer).wait_recv()

        loop(1, seqs, arrive)
        load(3, 0).wait()

        def emit(j, result):
            columns = columns_of(j)
            x2_ref[:, columns] = (
                tokens_ref[:, columns].astype(F32) + result + vectors_ref[8:9, columns]
            )

        dot_tiles(joined_ref[...], weights, 0, emit, unrolled=True)
        norm_into(x2_ref, vector(2), vector(3), h2_ref)
        load(6, 1).wait()

        def emit_query(j, result):
            columns = columns_of(j)
            cq_ref[:, columns] = (result + vectors_ref[9:10, columns]).astype(BF16)

        dot_tiles(h2_ref[...], weights, 1, emit_query, unrolled=True)

    def memory_rows(part):
        load(4 + part, part).start()
        load(4 + part, part).wait()

        def emit(j, result):
            columns = columns_of(j)
            bias = jnp.where(part == 1, vectors_ref[10:11, columns], 0.0)
            mem_ref[part, :, columns] = (result + bias).astype(BF16)

        dot_tiles(memory_all[...], weights, part, emit, unrolled=True)

    def cross_blocks(first, last):
        def one(j):
            columns = pl.ds(pl.multiple_of(j * LANES, LANES), LANES)
            crossed, logs = cross_attend(
                length_ref[0], cq_ref[:, columns], mem_ref[0, :, columns], mem_ref[1, :, columns]
            )
            for head in range(len(logs)):
                cross_log_ref[j, head : head + 1] = logs[head]
            crossed_low_ref[:, columns] = crossed.astype(BF16)

        loop(first, last, one)

    def after_cross():
        load(7, 2).wait()

        def emit(j, result):
            columns = columns_of(j)
            total = x2_ref[:, columns] + result + vectors_ref[11:12, columns]
            x3_ref[:, columns] = total
            down[:, columns] = total + vectors_ref[12 + FF // D : 13 + FF // D, columns]

        dot_tiles(crossed_low_ref[...], weights, 2, emit, unrolled=True)
        norm_into(x3_ref, vector(4), vector(5), h3_ref)

    def hidden_up(j):
        slot = lax.rem(j + 3, 4)
        load(8 + j, slot).wait()

        def emit(r, result):
            columns = columns_of(r)
            spread = pl.ds(pl.multiple_of(j * D + r * tile, tile), tile)
            pre = result + vectors_ref[pl.ds(12 + j, 1), columns]
            cumulative = 0.5 * (1.0 + lax.erf(pre * 0.5**0.5))
            density = jnp.exp(-0.5 * pre * pre) * (2.0 * jnp.pi) ** -0.5
            act_ref[:, spread] = (pre * cumulative).astype(BF16)
            slope_ref[:, spread] = (cumulative + pre * density).astype(BF16)

        dot_tiles(h3_ref[...], weights, slot, emit, turned=True, unrolled=True)

        @pl.when(j < 3)
        def _():
            load(12 + j, slot).start()

    def hidden_down(j):
        slot = lax.rem(j + 3, 4)
        load(12 + j, slot).wait()
        left = act_ref[:, pl.ds(pl.multiple_of(j * D, D), D)]

        def emit(r, result):
            columns = columns_of(r)
            down[:, columns] = down[:, columns] + result

        dot_tiles(left, weights, slot, emit, unrolled=True)

    arrived = gather.arrived

    def tick(t):
        gather.tick(t)

        @pl.when((t >= arrived) & (t < arrived + 3))
        def _():
            project(t - arrived)

        first_block = arrived + 3

        @pl.when((t >= first_block) & (t < first_block + seqs))
        def _():
            query_block(t - first_block)

        @pl.when((t >= arrived + 4) & (t < arrived + 6))
        def _():
            memory_rows(t - arrived - 4)

        early = arrived + 6
        for step, (position, slot) in enumerate(((3, 0), (6, 1), (7, 2), (8, 3))):

            @pl.when(t == early + step)
            def _(position=position, slot=slot):
                load(position, slot).start()

        late = first_block + seqs

        @pl.when(t == late)
        def _():
            after_self()
            load(9, 0).start()
            load(10, 1).start()

        @pl.when((t >= late) & (t < late + 2))
        def _():
            cross_blocks(4 * (t - late), 4 * (t - late) + 4)

        @pl.when(t == late + 1)
        def _():
            after_cross()
            load(11, 2).start()

        hidden = late + 2

        @pl.when((t >= hidden) & (t < hidden + 2))
        def _():
            loop(2 * (t - hidden), 2 * (t - hidden) + 2, hidden_up)

        @pl.when(t == hidden + 2)
        def _():
            load(15, 2).start()

        @pl.when(t > hidden)
        def _():
            loop(jnp.where(t == hidden + 1, 0, 1), jnp.where(t == hidden + 1, 1, 4), hidden_down)

    spread()
    loop(0, gather.groups + arrived, tick)

    def close(block):
        span = pl.ds(pl.multiple_of(block * NORM_ROWS, NORM_ROWS), NORM_ROWS)
        mixed_ref[span] = down[span].astype(BF16)

    loop(0, rows // NORM_ROWS, close)

    def finish(step):
        peer = lax.rem(me + step, seqs)
        loop(0, 3, lambda part: outward(part, peer, me).wait_send())
        backward_copy(peer, me).wait_send()

    loop(1, seqs, finish)
    gather.drain()


def forward_pass(
    seqs, planes, windows, lengths, holder, slot, master, tokens, memory, vectors
):
    mem = seqs * memory.shape[0]
    padded = memory.shape[0] + -memory.shape[0] % 16
    groups = holder.shape[0] // GROUP_UNITS
    slots, unit_rows = master.shape[:2]
    block = (unit_rows // 2 // planes, LANES)
    matrix = (2, D // LANES, planes, GROUP_UNITS) + block
    rows = tokens.shape[0]
    width = D // seqs
    dma = pltpu.SemaphoreType.DMA
    vmem = pl.BlockSpec(memory_space=pltpu.VMEM)
    smem = pl.BlockSpec(memory_space=pltpu.SMEM)
    anywhere = pl.BlockSpec(memory_space=pl.ANY)
    shape = jax.ShapeDtypeStruct
    by_head = (seqs, rows, width)
    outs = (
        shape((groups,) + matrix, BF16),
        shape((rows, D), BF16),
        shape((rows, D), BF16),
        shape((3,) + by_head, BF16),
        shape(by_head, BF16),
        shape((seqs, 8, rows), F32),
        shape((rows, D), F32),
        shape((rows, D), BF16),
        shape((rows, D), BF16),
        shape((2, mem, D), BF16),
        shape((rows, D), BF16),
        shape((D // LANES, 8, rows), F32),
        shape((rows, D), F32),
        shape((rows, D), BF16),
        shape((rows, FF), BF16),
        shape((rows, FF), BF16),
        shape((rows, D), BF16),
        shape((padded, D), BF16),
    )
    return pl.pallas_call(
        functools.partial(forward_kernel, seqs, planes),
        out_shape=outs,
        in_specs=[smem] * 4 + [anywhere, vmem, vmem, vmem],
        out_specs=(anywhere,) + (vmem,) * (len(outs) - 1),
        scratch_shapes=[
            pltpu.VMEM(master.shape, F32),
            pltpu.VMEM(master.shape, BF16),
            pltpu.VMEM((seqs * planes, 2, slots) + block, BF16),
            pltpu.VMEM((groups, 2, GROUP_UNITS) + block, BF16),
            pltpu.VMEM((seqs, padded, D), BF16),
            pltpu.VMEM((mem, D), F32),
            pltpu.VMEM((mem, D), BF16),
            pltpu.VMEM((4,) + matrix, BF16),
            pltpu.VMEM((3,) + by_head, BF16),
            pltpu.VMEM((rows, D), F32),
        ]
        + gather_scratch(planes, groups)
        + [
            dma((4,)),
            dma(()),
            dma((seqs * planes, 2)),
            dma((seqs * planes, 2)),
            dma((seqs,)),
            dma((seqs,)),
        ]
        + [dma((3, seqs)), dma((3, seqs)), dma((seqs,)), dma((seqs,))],
        compiler_params=pltpu.CompilerParams(
            collective_id=2,
            has_side_effects=True,
            vmem_limit_bytes=56 * MIB,
        ),
        name="forward_pass",
    )(windows, lengths, holder, slot, master, tokens, memory, vectors)


GRAD_SLOTS = 4
COLUMN_SLOTS = 8


class Reduce:
    def __init__(
        self,
        planes,
        made,
        theirs_far,
        wide_far,
        chain_far,
        sums_ref,
        theirs,
        wide_in,
        narrow_in,
        narrow_all,
        column,
        chain_in,
        light_in,
        load_sem,
        chain_sem,
        c_send,
        c_recv,
        p_send,
        p_recv,
        z_send,
        z_recv,
    ):
        self.place = Place(planes)
        self.planes = planes
        self.z = self.place.z
        self.made = made
        self.theirs_far, self.wide_far, self.chain_far = theirs_far, wide_far, chain_far
        self.sums_ref = sums_ref
        self.theirs, self.wide_in = theirs, wide_in
        self.narrow_in, self.column, self.chain_in = narrow_in, column, chain_in
        self.narrow_all, self.light_in = narrow_all, light_in
        self.load_sem, self.chain_sem = load_sem, chain_sem
        self.c_send, self.c_recv = c_send, c_recv
        self.p_send, self.p_recv = p_send, p_recv
        self.z_send, self.z_recv = z_send, z_recv
        self.groups = theirs_far.shape[0]
        self.enter = 3
        self.leave = self.enter + 2 * (planes - 1)
        self.last = self.leave + 1
        self.split = self.groups - REDUCE_LIGHT
        self.light_enter = self.enter + 2

    def to_sibling(self, g):
        src = self.made.at[lax.rem(g, GRAD_SLOTS), :, pl.ds((1 - self.place.core) * 4, 4)]
        return remote(
            src, self.theirs_far.at[g], self.c_send.at[g], self.c_recv.at[g], self.place.sibling()
        )

    def planar(self, g, half, order, light=False):
        place = self.place
        wide, narrow = place.bits(half)
        narrow_peer, wide_peer = place.peers(half)
        if order == 0:
            slot = lax.rem(g, GRAD_SLOTS)
            src = self.made.at[slot, half, pl.ds(place.core * 4 + (1 - wide) * 2, 2)]
            dst, target = self.wide_far.at[g, half], wide_peer
        elif light:
            src = self.column.at[lax.rem(g, COLUMN_SLOTS), :, half, 1 - narrow]
            dst, target = self.narrow_all.at[g - self.split, half], narrow_peer
        else:
            src = self.column.at[lax.rem(g, COLUMN_SLOTS), self.z, half, 1 - narrow]
            dst, target = self.narrow_in.at[g, half], narrow_peer
        return remote(
            src, dst, self.p_send.at[g, half, order], self.p_recv.at[g, half, order], target
        )

    def load(self, g, order):
        src, dst = ((self.theirs_far, self.theirs), (self.wide_far, self.wide_in))[order]
        return pltpu.make_async_copy(src.at[g], dst, self.load_sem.at[order])

    def plane_at(self, way, reach):
        return reach if way == 0 else self.planes - 1 - reach

    def chain(self, g, way, reach, light):
        src = self.column.at[lax.rem(g, COLUMN_SLOTS), self.plane_at(way, reach)]
        dst = self.chain_far.at[g, way, reach - 1]
        return remote(
            src.at[:, 0] if light else src,
            dst.at[:, 0] if light else dst,
            self.z_send.at[g, way, reach - 1],
            self.z_recv.at[g, way, reach - 1],
            self.place.above() if way == 0 else self.place.below(),
        )

    def chain_load(self, g, way, reach, light):
        src = self.chain_far.at[g, way, reach - 1]
        dst = self.light_in if light else self.chain_in
        return pltpu.make_async_copy(
            src.at[:, 0] if light else src,
            dst.at[way, reach - 1],
            self.chain_sem.at[1 if light else 0, way, reach - 1],
        )

    def chain_of(self, t, way, action):
        here = self.z if way == 0 else self.planes - 1 - self.z
        for light in (False, True):
            lag = self.light_enter + here if light else self.enter + 2 * here
            g = t - lag
            first, last = (self.split, self.groups) if light else (0, self.split)

            @pl.when((here > 0) & (g >= first) & (g < last))
            def _(light=light, g=g):
                loop(here, self.planes, lambda reach: action(g, way, reach, light))

    def chain_arrive(self, g, way, reach, light):
        self.chain(g, way, reach, light).wait_recv()
        self.chain_load(g, way, reach, light).start()

    def chain_pass(self, g, way, reach, light):
        here = self.z if way == 0 else self.planes - 1 - self.z
        slot, plane = lax.rem(g, COLUMN_SLOTS), self.plane_at(way, reach)
        self.chain_load(g, way, reach, light).wait()
        if light:
            for half in range(2):
                self.column[slot, plane, half, 0] = (
                    self.column[slot, plane, half, 0] + self.light_in[way, reach - 1, half]
                )
        else:
            self.column[slot, plane] = self.column[slot, plane] + self.chain_in[way, reach - 1]

        @pl.when(reach > here)
        def _():
            self.chain(g, way, reach, light).start()

    def start_chains(self, g, light):
        for way in range(2):

            @pl.when(self.z == (0 if way == 0 else self.planes - 1))
            def _(way=way):
                loop(1, self.planes, lambda reach: self.chain(g, way, reach, light).start())

    def enter_line(self, g):
        slot, spot = lax.rem(g, GRAD_SLOTS), lax.rem(g, COLUMN_SLOTS)
        self.load(g, 1).wait()
        for half in range(2):
            wide, narrow = self.place.bits(half)
            first = self.place.core * 4 + wide * 2
            for b in range(2):
                total = self.made[slot, half, first + b] + self.wide_in[half, b]
                for plane in range(self.planes):
                    self.column[spot, plane, half, b] = total[plane]

        @pl.when(g < self.split)
        def _():
            self.start_chains(g, False)

        @pl.when(g >= self.split)
        def _():
            for half in range(2):
                self.planar(g, half, 1, True).start()

    def enter_light(self, g):
        slot = lax.rem(g, COLUMN_SLOTS)
        for half in range(2):
            wide, narrow = self.place.bits(half)
            self.planar(g, half, 1, True).wait()

            def one(plane, half=half, narrow=narrow):
                self.column[slot, plane, half, 0] = (
                    self.column[slot, plane, half, narrow]
                    + self.narrow_all[g - self.split, half, plane]
                )

            loop(0, self.planes, one)
        self.start_chains(g, True)

    def finish_light(self, g):
        slot = lax.rem(g, COLUMN_SLOTS)
        for half in range(2):
            self.sums_ref[g, half] = self.column[slot, self.z, half, 0]

    def finish(self, g):
        for half in range(2):
            wide, narrow = self.place.bits(half)
            self.planar(g, half, 1).wait_recv()
            own = self.column[lax.rem(g, COLUMN_SLOTS), self.z, half, narrow].astype(F32)
            self.sums_ref[g, half] = (own + self.narrow_in[g, half].astype(F32)).astype(BF16)

    def arrive(self, g, order):
        if order == 0:
            self.to_sibling(g).wait_recv()
        else:
            for half in range(2):
                self.planar(g, half, 0).wait_recv()
        self.load(g, order).start()

    def add(self, g):
        slot = lax.rem(g, GRAD_SLOTS)
        self.load(g, 0).wait()
        first = self.place.core * 4
        for half in range(2):
            for b in range(4):
                self.made[slot, half, first + b] = (
                    self.made[slot, half, first + b] + self.theirs[half, b]
                )
            self.planar(g, half, 0).start()

    def leave_line(self, g):
        for half in range(2):
            self.planar(g, half, 1).start()

    def wait_column_sends(self, g, light=False):
        if not light:
            for half in range(2):
                self.planar(g, half, 1).wait_send()
        for way in range(2):
            here = self.z if way == 0 else self.planes - 1 - self.z
            loop(here + 1, self.planes, lambda reach: self.chain(g, way, reach, light).wait_send())

    def wait_made_sends(self, g):
        self.to_sibling(g).wait_send()
        for half in range(2):
            self.planar(g, half, 0).wait_send()

    def during(self, t, lag, action, first=0, last=None):
        g = t - lag

        @pl.when((g >= first) & (g < (self.groups if last is None else last)))
        def _():
            action(g)

    def receive(self, t):
        self.during(t, 1, lambda g: self.arrive(g, 0))
        self.during(t, self.enter, lambda g: self.arrive(g, 1))
        for way in range(2):
            self.chain_of(t, way, self.chain_arrive)
        self.during(t, self.last, self.finish, 0, self.split)

        @pl.when((t >= GRAD_SLOTS) & (t < self.groups))
        def _():
            self.wait_made_sends(t - GRAD_SLOTS)

    def advance(self, t):
        self.during(t, 0, lambda g: self.to_sibling(g).start())
        for way in range(2):
            self.chain_of(t, way, self.chain_pass)
        self.during(t, self.leave, self.leave_line, 0, self.split)
        self.during(t, self.light_enter + self.planes, self.finish_light, self.split)
        self.during(t, self.light_enter, self.enter_light, self.split)

        @pl.when((t >= self.enter + COLUMN_SLOTS) & (t < self.enter + self.groups))
        def _():
            self.wait_column_sends(t - self.enter - COLUMN_SLOTS)

        self.during(t, self.enter, self.enter_line)
        self.during(t, 1, self.add)

    def drain(self):
        loop(self.groups - GRAD_SLOTS, self.groups, self.wait_made_sends)
        loop(self.groups - COLUMN_SLOTS, self.split, self.wait_column_sends)
        loop(self.split, self.groups, lambda g: self.wait_column_sends(g, True))


BACKWARD_READS = (12, 8, 13, 9, 14, 10, 15, 11, 7, 6, 3, 4, 5, 0, 1, 2)
READ_SLOTS = 3


def backward_kernel(
    seqs,
    planes,
    window_ref,
    length_ref,
    group_ref,
    unit_ref,
    whole_ref,
    slope_ref,
    cotangent_ref,
    tokens_ref,
    x2_ref,
    x3_ref,
    h1_ref,
    h2_ref,
    h3_ref,
    act_ref,
    crossed_ref,
    cq_ref,
    mem_ref,
    cross_log_ref,
    joined_ref,
    attended_ref,
    qkv_all,
    log_ref,
    memory_ref,
    vectors_ref,
    theirs_far,
    wide_far,
    chain_far,
    slots_ref,
    grad_tokens_ref,
    grad_memory_ref,
    vec_sum_ref,
    sums_ref,
    vec_ref,
    vec_part,
    vec_came,
    vec_planes,
    made,
    theirs,
    wide_in,
    narrow_in,
    narrow_all,
    column,
    chain_in,
    light_in,
    weights,
    dx,
    dh,
    du,
    dx3_low,
    dx2_low,
    dco,
    dcq,
    mem_parts,
    mem_theirs,
    mem_came,
    mem_low,
    do_all,
    delta,
    dq_total,
    dk_total,
    dv_total,
    dq_low,
    dk_low,
    dv_low,
    dq_back,
    dk_back,
    dv_back,
    load_sem,
    chain_sem,
    c_send,
    c_recv,
    p_send,
    p_recv,
    z_send,
    z_recv,
    read_sem,
    slope_sem,
    fold_send,
    fold_recv,
    mem_send,
    mem_recv,
    do_send,
    do_recv,
    back_send,
    back_recv,
    vec_send,
    vec_recv,
    across_send,
    across_recv,
    slot_send,
    slot_recv,
    own_sem,
):
    reduce = Reduce(
        planes,
        made,
        theirs_far,
        wide_far,
        chain_far,
        sums_ref,
        theirs,
        wide_in,
        narrow_in,
        narrow_all,
        column,
        chain_in,
        light_in,
        load_sem,
        chain_sem,
        c_send,
        c_recv,
        p_send,
        p_recv,
        z_send,
        z_recv,
    )
    place = reduce.place
    me, z = place.seq, place.z
    rows = tokens_ref.shape[0]
    width = D // seqs
    tile = 2 * LANES
    head_count = width // HDIM
    mem_rows = mem_ref.shape[1] // seqs
    padded = memory_ref.shape[0]
    ups = FF // D

    total = seqs * planes
    here = me * planes + z

    def read(k):
        slot = k % READ_SLOTS
        return pltpu.make_async_copy(
            whole_ref.at[BACKWARD_READS[k]], weights.at[slot], read_sem.at[slot]
        )

    def using(k, work):
        read(k).wait()
        work(k % READ_SLOTS)
        if k + READ_SLOTS < len(BACKWARD_READS):
            read(k + READ_SLOTS).start()

    greet_all(here, total, lambda j: (lax.div(j, planes), lax.rem(j, planes)))

    slope_copy = pltpu.make_async_copy(slope_ref, du, slope_sem)
    slope_copy.start()
    for k in range(READ_SLOTS):
        read(k).start()

    def columns_of(j, count=tile):
        return pl.ds(pl.multiple_of(j * count, count), count)

    def vector(index):
        return vectors_ref[index : index + 1]

    def row_sum(values):
        return jnp.sum(values.astype(F32), axis=0, keepdims=True)

    def norm_back(stream_ref, gain_row, base, out_ref, low_ref):
        gain = vector(gain_row)
        part = rows // 4

        def one(block, sums):
            span = pl.ds(pl.multiple_of(block * part, part), part)
            _, form, inverse = norm_forward(stream_ref[span].astype(F32), 1.0, 0.0)
            upstream = dh[span]
            scaled = upstream * gain
            first = jnp.mean(scaled, axis=-1, keepdims=True)
            second = jnp.mean(scaled * form, axis=-1, keepdims=True)
            total = base(span) + inverse * (scaled - first - form * second)
            out_ref[span] = total
            gains, shifts, lows = sums
            if low_ref is not None:
                low = total.astype(BF16)
                low_ref[span] = low
                lows = lows + row_sum(low)
            return (gains + row_sum(upstream * form), shifts + row_sum(upstream), lows)

        zero = jnp.zeros((1, D), F32)
        gains, shifts, lows = lax.fori_loop(0, 4, one, (zero, zero, zero))
        vec_ref[gain_row : gain_row + 1] = gains
        vec_ref[gain_row + 1 : gain_row + 2] = shifts
        return lows

    def grad_matrix(slot, left_ref, first_column, right_ref):
        def one(r):
            first = first_column + r * tile
            left = left_ref[:, pl.ds(pl.multiple_of(first, tile), tile)]
            block = made.shape[5]
            for c in range(2):
                columns = slice(c * (D // 2), (c + 1) * (D // 2))
                result = dot_tn(left, right_ref[:, columns]).astype(BF16)
                for part in range(tile // block):
                    for b in range(D // 2 // LANES):
                        made[slot, part // planes, c * 4 + b, part % planes, r] = result[
                            part * block : (part + 1) * block, b * LANES : (b + 1) * LANES
                        ]

        def two(pair):
            one(2 * pair)
            one(2 * pair + 1)

        loop(0, GROUP_UNITS // 2, two)

    def hidden_back(j):
        if j == 0:
            dh[...] = jnp.zeros_like(dh)
            slope_copy.wait()
            vec_ref[...] = jnp.zeros_like(vec_ref)

        def slopes(slot):
            def emit(r, result):
                spread = pl.ds(pl.multiple_of(j * D + r * tile, tile), tile)
                low = (result * du[:, spread].astype(F32)).astype(BF16)
                du[:, spread] = low
                vec_ref[12 + j : 13 + j, columns_of(r)] = row_sum(low)

            dot_tiles(cotangent_ref[...], weights, slot, emit, turned=True, unrolled=True)

        def inner(slot):
            def emit(r, result):
                dh[:, columns_of(r)] = dh[:, columns_of(r)] + result

            dot_tiles(du[:, j * D : (j + 1) * D], weights, slot, emit, unrolled=True)

        using(2 * j, slopes)
        using(2 * j + 1, inner)

    def mem_fold():
        return remote(
            mem_parts.at[1 - place.core],
            mem_theirs,
            fold_send,
            fold_recv,
            place.sibling(),
        )

    chip = lax.div(me, 2)
    chips = seqs // 2

    def mem_copy(peer, slot):
        return remote(
            mem_parts.at[place.core, peer],
            mem_came.at[slot],
            mem_send.at[peer],
            mem_recv.at[slot],
            (2 * peer + place.core, z),
        )

    def cross_branch():
        vec_ref[12 + ups : 13 + ups] = row_sum(cotangent_ref[...])
        vec_ref[11:12] = norm_back(
            x3_ref, 4, lambda span: cotangent_ref[span].astype(F32), dx, dx3_low
        )

        def branch(slot):
            def emit(r, result):
                dco[:, columns_of(r)] = result.astype(BF16)

            dot_tiles(dx3_low[...], weights, slot, emit, turned=True, unrolled=True)

        using(8, branch)

    def cross_back(first, last):
        def one(j, carry):
            columns = columns_of(j, LANES)
            dq, dk, dv = cross_grads(
                length_ref[0],
                cq_ref[:, columns],
                mem_ref[0, :, columns],
                mem_ref[1, :, columns],
                dco[:, columns],
                crossed_ref[:, columns],
                [cross_log_ref[j, h : h + 1] for h in range(LANES // HDIM)],
            )
            dcq[:, columns] = dq.astype(BF16)
            fill = jnp.zeros((max(padded - mem_rows, 1), LANES), F32)
            for peer in range(seqs):
                span = slice(peer * mem_rows, (peer + 1) * mem_rows)
                for part, values in enumerate((dk, dv)):
                    block = values[span]
                    if padded > mem_rows:
                        block = jnp.concatenate([block, fill], axis=0)
                    mem_parts[peer % 2, peer // 2, part, :, columns] = block.astype(BF16)
            return carry

        lax.fori_loop(first, last, one, 0)

    def memory_send():
        mem_fold().wait()

        def send(step):
            peer = lax.rem(chip + step, chips)
            mem_parts[place.core, peer] = mem_parts[place.core, peer] + mem_theirs[peer]

            @pl.when(step < chips)
            def _():
                mem_copy(peer, chip).start()

            @pl.when(step == chips)
            def _():
                mem_came[chip] = mem_parts[place.core, peer]

        loop(1, chips + 1, send)

    def do_copy(peer, slot):
        return remote(
            dq_low.at[peer], do_all.at[slot], do_send.at[peer], do_recv.at[slot], (peer, z)
        )

    def before_self():
        def inner(slot):
            def emit(r, result):
                dh[:, columns_of(r)] = result

            dot_tiles(dcq[...], weights, slot, emit, turned=True, unrolled=True)

        using(9, inner)
        vec_ref[9:10] = row_sum(dcq[...])
        vec_ref[8:9] = norm_back(x2_ref, 2, lambda span: dx[span], dx, dx2_low)

        def branch(slot):
            def emit(r, result):
                low = result.astype(BF16)
                for piece in range(tile // width):
                    dq_low[r * (tile // width) + piece] = low[
                        :, piece * width : (piece + 1) * width
                    ]

            dot_tiles(dx2_low[...], weights, slot, emit, turned=True, unrolled=True)

        using(10, branch)

        def send(step, carry):
            do_copy(lax.rem(me + step, seqs), me).start()
            return carry

        lax.fori_loop(1, seqs, send, 0)
        do_all[me] = dq_low[me]

    def memory_back():
        def arrive(step):
            peer = lax.rem(chip + step, chips)
            mem_copy(peer, peer).wait_recv()

        loop(1, chips, arrive)
        for part in range(2):
            part_sum = mem_came[0, part].astype(F32)
            for j in range(1, chips):
                part_sum = part_sum + mem_came[j, part].astype(F32)
            mem_low[part] = part_sum.astype(BF16)
        vec_ref[10:11] = row_sum(mem_low[1])

        def keys(slot):
            def emit(r, result):
                grad_memory_ref[:, columns_of(r)] = result

            dot_tiles(mem_low[0], weights, slot, emit, turned=True, unrolled=True)

        def values(slot):
            def emit(r, result):
                grad_memory_ref[:, columns_of(r)] = grad_memory_ref[:, columns_of(r)] + result

            dot_tiles(mem_low[1], weights, slot, emit, turned=True, unrolled=True)

        using(11, keys)
        using(12, values)

    window = window_ref[0]
    outputs = ((dq_low, dq_back), (dk_low, dk_back), (dv_low, dv_back))

    def returned(peer, slot, part):
        src, dst = outputs[part]
        return remote(
            src.at[peer],
            dst.at[:, pl.ds(pl.multiple_of(slot * width, width), width)],
            back_send.at[part, peer],
            back_recv.at[part, slot],
            (peer, z),
        )

    def prepare():
        def one(i, carry):
            @pl.when(i != me)
            def _():
                do_copy(i, i).wait_recv()

            sums = head_sums(do_all[i].astype(F32) * attended_ref[i].astype(F32), head_count)
            for head in range(head_count):
                delta[i, head : head + 1] = sums[head]
            for total in (dq_total, dk_total, dv_total):
                total[i] = jnp.zeros((rows, width), F32)
            return carry

        lax.fori_loop(0, seqs, one, 0)

    span_rows = 2 * rows
    stacked_queries = head_count * span_rows

    def tile_grads(p):
        level = (
            jnp.where(p >= 2, 1, 0) + jnp.where(p >= 6, 1, 0) + jnp.where(p >= 12, 1, 0)
        ).astype(jnp.int32)
        rank = p - level * (level + 1)
        second = jnp.where(rank > level, 1, 0).astype(jnp.int32)
        b = seqs - 1 - 2 * level - second
        q2 = seqs // 2 - 1 - level + rank - second * (level + 1)
        pair = pl.ds(pl.multiple_of(q2 * 2, 2), 2)
        keys, values = qkv_all[1, b], qkv_all[2, b]
        scaled = qkv_all[0, pair].reshape(span_rows, width) * jnp.asarray(HDIM**-0.5, BF16)
        grads = do_all[pair].reshape(span_rows, width)
        queries = jnp.concatenate([only_head(scaled, h, head_count) for h in range(head_count)], 0)
        uppers = jnp.concatenate([only_head(grads, h, head_count) for h in range(head_count)], 0)

        def row_of(ref):
            return jnp.concatenate(
                [ref[q2 * 2 + k, h : h + 1] for h in range(head_count) for k in range(2)], 1
            )

        logs, deltas = row_of(log_ref), row_of(delta)
        shape = (rows, stacked_queries)
        key_row = lax.broadcasted_iota(jnp.int32, shape, 0)
        query_row = lax.rem(lax.broadcasted_iota(jnp.int32, (1, stacked_queries), 1), span_rows)
        reach = query_row + (q2 * 2 - b) * rows

        def work(diagonal):
            scores = dot_nt(keys, queries)
            allowed = key_row <= reach if diagonal else key_row > reach - window
            probs = jnp.exp(jnp.where(allowed, scores, NEG_FILL) - logs)
            grad_scores = (probs * (dot_nt(values, uppers) - deltas)).astype(BF16)
            dv_total[b] = dv_total[b] + dot_nn(probs.astype(BF16), uppers)
            dk_total[b] = dk_total[b] + dot_nn(grad_scores, queries)
            spread = dot_tn(grad_scores, keys)
            part = spread[:span_rows]
            lane = lax.broadcasted_iota(jnp.int32, part.shape, 1)
            for h in range(1, head_count):
                part = jnp.where(
                    lane >= h * HDIM, spread[h * span_rows : (h + 1) * span_rows], part
                )
            dq_total[pair] = dq_total[pair] + part.reshape(2, rows, width)

        diagonal = lax.div(b, 2) == q2

        @pl.when(diagonal)
        def _():
            work(True)

        @pl.when(jnp.logical_not(diagonal))
        def _():
            work(False)

        @pl.when(q2 == seqs // 2 - 1)
        def _():
            dk_low[b] = dk_total[b].astype(BF16)
            dv_low[b] = dv_total[b].astype(BF16)
            send_back(b, 1)
            send_back(b, 2)

    def send_back(i, part):
        low, rows_ref = outputs[part]

        @pl.when(i != me)
        def _():
            returned(i, me, part).start()

        @pl.when(i == me)
        def _():
            rows_ref[:, pl.ds(pl.multiple_of(i * width, width), width)] = low[i]

    def close_self():
        loop(1, seqs, lambda step: do_copy(lax.rem(me + step, seqs), me).wait_send())

        def one(i):
            dq_low[i] = (dq_total[i] * HDIM**-0.5).astype(BF16)
            send_back(i, 0)

        loop(0, seqs, one)

    def first_arrive():
        def arrive(step, carry):
            peer = lax.rem(me + step, seqs)
            for part in range(3):
                returned(peer, peer, part).wait_recv()
            return carry

        lax.fori_loop(1, seqs, arrive, 0)

    def first_back():
        for part in range(3):

            def inner(slot, part=part):
                def emit(r, result):
                    if part == 0:
                        dh[:, columns_of(r)] = result
                    else:
                        dh[:, columns_of(r)] = dh[:, columns_of(r)] + result

                dot_tiles(rows_of_part[part][...], weights, slot, emit, turned=True, unrolled=True)

            using(13 + part, inner)
        vec_ref[6:7] = row_sum(rows_of_part[0][...])
        vec_ref[7:8] = row_sum(rows_of_part[2][...])
        norm_back(tokens_ref, 0, lambda span: dx[span], grad_tokens_ref, None)

    rows_of_part = (dq_back, dk_back, dv_back)

    def fold_copy(order):
        target = (place.sibling(), place.x_peer(), place.y_peer())[order]
        return remote(
            vec_part.at[order],
            vec_came.at[order],
            vec_send.at[order],
            vec_recv.at[order],
            target,
        )

    def across_copy(peer, slot):
        return remote(
            vec_planes.at[slot],
            vec_planes.at[slot],
            across_send.at[peer],
            across_recv.at[slot],
            (me, peer),
        )

    def fold_vectors(order):
        if order == 0:
            vec_part[0] = vec_ref[...]
        else:
            fold_copy(order - 1).wait()
            folded = vec_part[order - 1] + vec_came[order - 1]
            if order < 3:
                vec_part[order] = folded
            else:
                vec_planes[z] = folded
        if order < 3:
            fold_copy(order).start()
        else:

            def send(step, carry):
                across_copy(lax.rem(z + step, planes), z).start()
                return carry

            lax.fori_loop(1, planes, send, 0)

    def close_vectors():
        def arrive(step, carry):
            peer = lax.rem(z + step, planes)
            across_copy(peer, peer).wait()
            return carry

        lax.fori_loop(1, planes, arrive, 0)
        vector_sum = vec_planes[0]
        for plane in range(1, planes):
            vector_sum = vector_sum + vec_planes[plane]
        vec_sum_ref[...] = vector_sum

    slot_count = slots_ref.shape[0]

    def slot_copy(peer, holder, half):
        slot_rows, slot_columns = tile_of(holder, planes, half, slots_ref.shape[1])
        return remote(
            made.at[0, half, lax.div(peer, planes), lax.rem(peer, planes), pl.ds(0, slot_count)],
            slots_ref.at[:, slot_rows, slot_columns],
            slot_send.at[peer, half],
            slot_recv.at[holder, half],
            (lax.div(peer, planes), lax.rem(peer, planes)),
        )

    def return_tiles():
        def fill(peer):
            for s in range(slot_count):
                group, unit = group_ref[peer * slot_count + s], unit_ref[peer * slot_count + s]
                for half in range(2):
                    block = sums_ref[jnp.maximum(group, 0), half, unit]
                    made[0, half, lax.div(peer, planes), lax.rem(peer, planes), s] = jnp.where(
                        group >= 0, block, jnp.zeros_like(block)
                    )

        def start(step, carry):
            peer = lax.rem(here + step, total)
            fill(peer)
            for half in range(2):
                slot_copy(peer, here, half).start()
            return carry

        lax.fori_loop(1, total, start, 0)
        fill(here)
        own = []
        for half in range(2):
            slot_rows, slot_columns = tile_of(here, planes, half, slots_ref.shape[1])
            own.append(
                pltpu.make_async_copy(
                    made.at[0, half, lax.div(here, planes), lax.rem(here, planes), pl.ds(0, slot_count)],
                    slots_ref.at[:, slot_rows, slot_columns],
                    own_sem.at[half],
                )
            )
            own[half].start()
        for copy in own:
            copy.wait()

        def finish_slots(step, carry):
            peer = lax.rem(here + total - step, total)
            for half in range(2):
                slot_copy(peer, peer, half).wait()
            return carry

        lax.fori_loop(1, total, finish_slots, 0)

    def tick(t, carry):
        reduce.receive(t)

        slot = lax.rem(t, GRAD_SLOTS)

        @pl.when(t < ups)
        def _():
            grad_matrix(slot, act_ref, t * D, cotangent_ref)

        @pl.when((t >= ups) & (t < 2 * ups))
        def _():
            grad_matrix(slot, du, (t - ups) * D, h3_ref)

        late = 2 * ups
        pieces = (
            (crossed_ref, dx3_low),
            (h2_ref, dcq),
            (joined_ref, dx2_low),
            (memory_ref, mem_low.at[0]),
            (memory_ref, mem_low.at[1]),
        )
        for step, (left, right) in enumerate(pieces):

            @pl.when(t == late + step)
            def _(left=left, right=right):
                grad_matrix(slot, left, 0, right)

        last = late + len(pieces)

        @pl.when(t == last)
        def _():
            first_arrive()

        for part in range(3):

            @pl.when(t == last + part)
            def _(part=part):
                grad_matrix(slot, h1_ref, 0, rows_of_part[part])

        reduce.advance(t)

        def at(step, work):
            @pl.when(t == step)
            def _():
                work()

        for j in range(ups):
            at(1 + j // 2, functools.partial(hidden_back, j))
        at(3, cross_branch)
        blocks = D // LANES
        at(4, functools.partial(cross_back, 0, blocks // 2))
        at(5, functools.partial(cross_back, blocks // 2, blocks))
        at(5, lambda: mem_fold().start())
        at(6, memory_send)
        at(6, before_self)
        at(7, prepare)

        @pl.when((t >= 7) & (t < 13))
        def _():
            loop(lax.div(10 * (t - 7), 3), lax.div(10 * (t - 6), 3), tile_grads)

        at(10, memory_back)
        at(12, close_self)
        at(last + 3, first_back)
        for order in range(4):
            at(last + 4 + order, functools.partial(fold_vectors, order))
        at(last + 9, close_vectors)
        return carry

    lax.fori_loop(0, reduce.groups + reduce.last, tick, 0)

    def finish(step, carry):
        peer = lax.rem(me + step, seqs)
        for part in range(3):
            returned(peer, me, part).wait_send()
        return carry

    lax.fori_loop(1, seqs, finish, 0)
    loop(1, chips, lambda step: mem_copy(lax.rem(chip + step, chips), chip).wait_send())
    reduce.drain()
    return_tiles()


def backward_pass(seqs, planes, windows, lengths, group, unit, whole, slope, arrays):
    groups, matrix = whole.shape[0], whole.shape[1:]
    column = matrix[2:]
    block = matrix[3:]
    cotangent, memory = arrays[0], arrays[-2]
    total = seqs * planes
    slots, unit_rows = group.shape[0] // total, 2 * planes * block[1]
    rows = cotangent.shape[0]
    width = D // seqs
    padded = memory.shape[0]
    dma = pltpu.SemaphoreType.DMA
    vmem = pl.BlockSpec(memory_space=pltpu.VMEM)
    smem = pl.BlockSpec(memory_space=pltpu.SMEM)
    anywhere = pl.BlockSpec(memory_space=pl.ANY)
    shape = jax.ShapeDtypeStruct
    by_head = (seqs, rows, width)
    outs = pl.pallas_call(
        functools.partial(backward_kernel, seqs, planes),
        out_shape=(
            shape((groups, 2, 4) + column, BF16),
            shape((groups, 2, 2) + column, BF16),
            shape((groups, 2, planes - 1, 2, 2) + block, BF16),
            shape((slots, unit_rows, D), BF16),
            shape((rows, D), F32),
            shape((padded, D), F32),
            shape((24, D), F32),
        ),
        in_specs=[smem] * 4 + [anywhere, anywhere] + [vmem] * len(arrays),
        out_specs=(anywhere, anywhere, anywhere, anywhere, vmem, vmem, vmem),
        scratch_shapes=[
            pltpu.VMEM((groups, 2) + block, BF16),
            pltpu.VMEM((24, D), F32),
            pltpu.VMEM((3, 24, D), F32),
            pltpu.VMEM((3, 24, D), F32),
            pltpu.VMEM((planes, 24, D), F32),
            pltpu.VMEM((GRAD_SLOTS,) + matrix, BF16),
            pltpu.VMEM((2, 4) + column, BF16),
            pltpu.VMEM((2, 2) + column, BF16),
            pltpu.VMEM((groups, 2) + block, BF16),
            pltpu.VMEM((REDUCE_LIGHT, 2) + column, BF16),
            pltpu.VMEM((COLUMN_SLOTS, planes, 2, 2) + block, BF16),
            pltpu.VMEM((2, planes - 1, 2, 2) + block, BF16),
            pltpu.VMEM((2, planes - 1, 2) + block, BF16),
            pltpu.VMEM((READ_SLOTS,) + matrix, BF16),
            pltpu.VMEM((rows, D), F32),
            pltpu.VMEM((rows, D), F32),
            pltpu.VMEM((rows, FF), BF16),
            pltpu.VMEM((rows, D), BF16),
            pltpu.VMEM((rows, D), BF16),
            pltpu.VMEM((rows, D), BF16),
            pltpu.VMEM((rows, D), BF16),
            pltpu.VMEM((2, seqs // 2, 2, padded, D), BF16),
            pltpu.VMEM((seqs // 2, 2, padded, D), BF16),
            pltpu.VMEM((seqs // 2, 2, padded, D), BF16),
            pltpu.VMEM((2, padded, D), BF16),
            pltpu.VMEM(by_head, BF16),
            pltpu.VMEM((seqs, 8, rows), F32),
            pltpu.VMEM(by_head, F32),
            pltpu.VMEM(by_head, F32),
            pltpu.VMEM(by_head, F32),
            pltpu.VMEM(by_head, BF16),
            pltpu.VMEM(by_head, BF16),
            pltpu.VMEM(by_head, BF16),
            pltpu.VMEM((rows, D), BF16),
            pltpu.VMEM((rows, D), BF16),
            pltpu.VMEM((rows, D), BF16),
            dma((2,)),
            dma((2, 2, planes - 1)),
            dma((groups,)),
            dma((groups,)),
            dma((groups, 2, 2)),
            dma((groups, 2, 2)),
            dma((groups, 2, planes - 1)),
            dma((groups, 2, planes - 1)),
            dma((READ_SLOTS,)),
            dma(()),
            dma(()),
            dma(()),
            dma((seqs // 2,)),
            dma((seqs // 2,)),
            dma((seqs,)),
            dma((seqs,)),
            dma((3, seqs)),
            dma((3, seqs)),
            dma((3,)),
            dma((3,)),
            dma((planes,)),
            dma((planes,)),
            dma((total, 2)),
            dma((total, 2)),
            dma((2,)),
        ],
        compiler_params=pltpu.CompilerParams(
            collective_id=3,
            has_side_effects=True,
            vmem_limit_bytes=60 * MIB,
        ),
        name="backward_pass",
    )(windows, lengths, group, unit, whole, slope, *arrays)
    return outs[3:]


def dot_nt(left, right):
    return lax.dot_general(left, right, (((1,), (1,)), ((), ())), preferred_element_type=F32)


def dot_tn(left, right):
    return lax.dot_general(left, right, (((0,), (0,)), ((), ())), preferred_element_type=F32)


def dot_nn(left, right):
    return lax.dot_general(left, right, (((1,), (0,)), ((), ())), preferred_element_type=F32)


def only_head(values, head, head_count):
    if head_count == 1:
        return values
    lane = lax.broadcasted_iota(jnp.int32, values.shape, 1)
    inside = (lane >= head * HDIM) & (lane < (head + 1) * HDIM)
    return jnp.where(inside, values, jnp.zeros_like(values))


def stacked_heads(parts):
    whole = parts[0]
    row = lax.broadcasted_iota(jnp.int32, whole.shape, 0)
    for head in range(1, len(parts)):
        whole = jnp.where(row >= head * HDIM, parts[head], whole)
    return whole


def head_sums(values, head_count):
    turned = values.T
    return [
        jnp.sum(turned[head * HDIM : (head + 1) * HDIM], axis=0, keepdims=True)
        for head in range(head_count)
    ]


def attend_block(i, rows, head_count, offset, window, q_all, k_all, v_all, log_ref):
    scaled = q_all[i] * jnp.asarray(HDIM**-0.5, BF16)
    queries = [only_head(scaled, head, head_count) for head in range(head_count)]
    state = []
    for head in range(head_count):
        scores = dot_nt(k_all[i], queries[head])
        scores = jnp.where((offset <= 0) & (offset > -window), scores, NEG_FILL)
        best = jnp.max(scores, axis=0, keepdims=True)
        probs = jnp.exp(scores - best)
        state.append(
            (best, jnp.sum(probs, axis=0, keepdims=True), dot_tn(v_all[i], probs.astype(BF16)))
        )

    def key_block(b, running):
        keys, values = k_all[b], v_all[b]
        limit = (i - b) * rows - window
        renewed = []
        for head in range(head_count):
            best, total, gathered = running[head]
            scores = jnp.where(offset > limit, dot_nt(keys, queries[head]), NEG_FILL)
            new_best = jnp.maximum(best, jnp.max(scores, axis=0, keepdims=True))
            probs = jnp.exp(scores - new_best)
            keep = jnp.exp(best - new_best)
            renewed.append(
                (
                    new_best,
                    total * keep + jnp.sum(probs, axis=0, keepdims=True),
                    gathered * keep + dot_tn(values, probs.astype(BF16)),
                )
            )
        return tuple(renewed)

    state = lax.fori_loop(0, i, key_block, tuple(state))
    for head in range(head_count):
        best, total, _ = state[head]
        log_ref[i, head : head + 1] = best + jnp.log(total)
    return stacked_heads([gathered / total for _, total, gathered in state]).T


def attend_pairs(i, rows, head_count, window, qkv_all, log_ref):
    width = qkv_all.shape[3]
    scaled = qkv_all[0, i] * jnp.asarray(HDIM**-0.5, BF16)
    queries = jnp.concatenate([only_head(scaled, head, head_count) for head in range(head_count)], 0)
    columns = head_count * rows
    key_row = lax.broadcasted_iota(jnp.int32, (2 * rows, columns), 0)
    query_row = lax.rem(lax.broadcasted_iota(jnp.int32, (1, columns), 1), rows)
    last = lax.div(i, 2)

    def two_blocks(part, m):
        return qkv_all[part, pl.ds(pl.multiple_of(2 * m, 2), 2)].reshape(2 * rows, width)

    def one(step, running):
        m = last - step
        best, total, gathered = running
        reach = query_row + (i - 2 * m) * rows
        allowed = (key_row <= reach) & (key_row > reach - window)
        scores = jnp.where(allowed, dot_nt(two_blocks(1, m), queries), NEG_FILL)
        new_best = jnp.maximum(best, jnp.max(scores, axis=0, keepdims=True))
        probs = jnp.exp(scores - new_best)
        keep = jnp.exp(best - new_best)
        return (
            new_best,
            total * keep + jnp.sum(probs, axis=0, keepdims=True),
            gathered * keep + dot_tn(two_blocks(2, m), probs.astype(BF16)),
        )

    best, total, gathered = lax.fori_loop(
        0,
        last + 1,
        one,
        (
            jnp.full((1, columns), NEG_FILL, F32),
            jnp.zeros((1, columns), F32),
            jnp.zeros((width, columns), F32),
        ),
    )
    logs = best + jnp.log(total)
    gathered = gathered / total
    for head in range(head_count):
        log_ref[i, head : head + 1] = logs[:, head * rows : (head + 1) * rows]
    return stacked_heads(
        [gathered[:, head * rows : (head + 1) * rows] for head in range(head_count)]
    ).T


def cross_attend(length, query, keys, values):
    head_count = LANES // HDIM
    rows = query.shape[0]
    scaled = query * jnp.asarray(HDIM**-0.5, BF16)
    queries = jnp.concatenate([only_head(scaled, head, head_count) for head in range(head_count)], 0)
    scores = dot_nt(keys, queries)
    allowed = lax.broadcasted_iota(jnp.int32, scores.shape, 0) < length
    scores = jnp.where(allowed, scores, NEG_FILL)
    best = jnp.max(scores, axis=0, keepdims=True)
    probs = jnp.exp(scores - best)
    total = jnp.sum(probs, axis=0, keepdims=True)
    gathered = dot_tn(values, probs.astype(BF16)) / total
    logs = best + jnp.log(total)
    spans = [slice(head * rows, (head + 1) * rows) for head in range(head_count)]
    crossed = stacked_heads([gathered[:, span] for span in spans]).T
    return crossed, [logs[:, span] for span in spans]


def self_forward_kernel(
    seqs,
    window_ref,
    q_ref,
    k_ref,
    v_ref,
    joined_ref,
    q_all,
    k_all,
    v_all,
    attended_ref,
    log_ref,
    rounded,
    send_sem,
    recv_sem,
    back_send,
    back_recv,
):
    me, z = lax.axis_index("seq"), lax.axis_index("grp")
    rows, width = q_ref.shape[1], q_ref.shape[2]
    head_count = width // HDIM
    greet_all(me, seqs, lambda j: (j, z))
    pairs = ((q_ref, q_all), (k_ref, k_all), (v_ref, v_all))

    def outward(peer, slot, part):
        src, dst = pairs[part]
        return remote(
            src.at[peer], dst.at[slot], send_sem.at[part, peer], recv_sem.at[part, slot], (peer, z)
        )

    def start(step, carry):
        peer = lax.rem(me + step, seqs)
        for part in range(3):
            outward(peer, me, part).start()
        return carry

    lax.fori_loop(1, seqs, start, 0)
    for src, dst in pairs:
        dst[me] = src[me]
    window = window_ref[0]
    offset = lax.broadcasted_iota(jnp.int32, (rows, rows), 0) - lax.broadcasted_iota(
        jnp.int32, (rows, rows), 1
    )

    def backward_copy(peer, slot):
        return remote(
            rounded.at[peer], joined_ref.at[slot], back_send.at[peer], back_recv.at[slot], (peer, z)
        )

    def query_block(i, carry):
        @pl.when(i != me)
        def _():
            for part in range(3):
                outward(i, i, part).wait_recv()

        attended = attend_block(i, rows, head_count, offset, window, q_all, k_all, v_all, log_ref)
        attended_ref[i] = attended
        rounded[i] = attended.astype(BF16)

        @pl.when(i != me)
        def _():
            backward_copy(i, me).start()

        @pl.when(i == me)
        def _():
            joined_ref[i] = rounded[i]

        return carry

    lax.fori_loop(0, seqs, query_block, 0)

    def finish(step, carry):
        peer = lax.rem(me + step, seqs)
        for part in range(3):
            outward(peer, me, part).wait_send()
        backward_copy(peer, peer).wait()
        return carry

    lax.fori_loop(1, seqs, finish, 0)


def self_forward(seqs, windows, query, key, value):
    shape = query.shape
    head_count = shape[2] // HDIM
    dma = pltpu.SemaphoreType.DMA
    vmem = pl.BlockSpec(memory_space=pltpu.VMEM)
    return pl.pallas_call(
        functools.partial(self_forward_kernel, seqs),
        out_shape=(
            jax.ShapeDtypeStruct(shape, BF16),
            jax.ShapeDtypeStruct(shape, BF16),
            jax.ShapeDtypeStruct(shape, BF16),
            jax.ShapeDtypeStruct(shape, BF16),
            jax.ShapeDtypeStruct(shape, F32),
            jax.ShapeDtypeStruct((seqs, max(head_count, 8), shape[1]), F32),
        ),
        in_specs=[pl.BlockSpec(memory_space=pltpu.SMEM), vmem, vmem, vmem],
        out_specs=(vmem,) * 6,
        scratch_shapes=[
            pltpu.VMEM(shape, BF16),
            dma((3, seqs)),
            dma((3, seqs)),
            dma((seqs,)),
            dma((seqs,)),
        ],
        compiler_params=pltpu.CompilerParams(
            collective_id=5, has_side_effects=True, vmem_limit_bytes=40 * MIB
        ),
        name="self_forward",
    )(windows, query, key, value)


def key_grads(
    b, seqs, rows, head_count, offset, window,
    q_all, k_all, v_all, grad_all, log_ref, delta, dq_total,
):
    keys, values = k_all[b], v_all[b]
    width = keys.shape[1]
    scale = jnp.asarray(HDIM**-0.5, BF16)
    key_heads = [only_head(keys, head, head_count) for head in range(head_count)]

    def pair(i, sums, diagonal):
        dk, dv = sums
        scaled = q_all[i] * scale
        grads = grad_all[i]
        if diagonal:
            allowed = (offset <= 0) & (offset > -window)
        else:
            allowed = offset > (i - b) * rows - window
        dq = dq_total[i]
        for head in range(head_count):
            query = only_head(scaled, head, head_count)
            grad = only_head(grads, head, head_count)
            scores = jnp.where(allowed, dot_nt(keys, query), NEG_FILL)
            probs = jnp.exp(scores - log_ref[i, head : head + 1])
            spread = dot_nt(values, grad)
            grad_scores = (probs * (spread - delta[i, head : head + 1])).astype(BF16)
            dv = dv + dot_nn(probs.astype(BF16), grad)
            dk = dk + dot_nn(grad_scores, query)
            dq = dq + dot_tn(grad_scores, key_heads[head])
        dq_total[i] = dq
        return (dk, dv)

    zeros = jnp.zeros((rows, width), F32)
    sums = pair(b, (zeros, zeros), True)
    return lax.fori_loop(b + 1, seqs, lambda i, s: pair(i, s, False), sums)


def cross_grads(length, query, keys, values, grads, crossed, logs):
    head_count = LANES // HDIM
    rows = query.shape[0]
    scaled = query * jnp.asarray(HDIM**-0.5, BF16)
    queries = jnp.concatenate([only_head(scaled, head, head_count) for head in range(head_count)], 0)
    uppers = jnp.concatenate([only_head(grads, head, head_count) for head in range(head_count)], 0)
    deltas = jnp.concatenate(head_sums(grads.astype(F32) * crossed.astype(F32), head_count), 1)
    scores = dot_nt(keys, queries)
    allowed = lax.broadcasted_iota(jnp.int32, scores.shape, 0) < length
    probs = jnp.exp(jnp.where(allowed, scores, NEG_FILL) - jnp.concatenate(logs, 1))
    grad_scores = (probs * (dot_nt(values, uppers) - deltas)).astype(BF16)
    dv = dot_nn(probs.astype(BF16), uppers)
    dk = dot_nn(grad_scores, queries)
    spread = dot_tn(grad_scores, keys)
    dq = spread[:rows]
    lane = lax.broadcasted_iota(jnp.int32, dq.shape, 1)
    for head in range(1, head_count):
        dq = jnp.where(lane >= head * HDIM, spread[head * rows : (head + 1) * rows], dq)
    return dq * HDIM**-0.5, dk, dv


def self_backward_kernel(
    seqs,
    window_ref,
    grad_ref,
    q_all,
    k_all,
    v_all,
    attended_ref,
    log_ref,
    dq_ref,
    dk_ref,
    dv_ref,
    grad_all,
    delta,
    dq_total,
    dq_low,
    dk_low,
    dv_low,
    send_sem,
    recv_sem,
    back_send,
    back_recv,
):
    me, z = lax.axis_index("seq"), lax.axis_index("grp")
    rows, width = grad_ref.shape[1], grad_ref.shape[2]
    head_count = width // HDIM
    greet_all(me, seqs, lambda j: (j, z))

    def outward(peer, slot):
        return remote(
            grad_ref.at[peer], grad_all.at[slot], send_sem.at[peer], recv_sem.at[slot], (peer, z)
        )

    def start(step, carry):
        outward(lax.rem(me + step, seqs), me).start()
        return carry

    lax.fori_loop(1, seqs, start, 0)
    grad_all[me] = grad_ref[me]
    window = window_ref[0]
    offset = lax.broadcasted_iota(jnp.int32, (rows, rows), 0) - lax.broadcasted_iota(
        jnp.int32, (rows, rows), 1
    )

    def prepare(i, carry):
        @pl.when(i != me)
        def _():
            outward(i, i).wait_recv()

        sums = head_sums(grad_all[i].astype(F32) * attended_ref[i].astype(F32), head_count)
        for head in range(head_count):
            delta[i, head : head + 1] = sums[head]
        dq_total[i] = jnp.zeros((rows, width), F32)
        return carry

    lax.fori_loop(0, seqs, prepare, 0)
    outputs = ((dq_low, dq_ref), (dk_low, dk_ref), (dv_low, dv_ref))

    def returned(peer, slot, part):
        src, dst = outputs[part]
        return remote(
            src.at[peer], dst.at[slot], back_send.at[part, peer], back_recv.at[part, slot], (peer, z)
        )

    def key_block(step, carry):
        b = seqs - 1 - step
        dk, dv = key_grads(
            b, seqs, rows, head_count, offset, window,
            q_all, k_all, v_all, grad_all, log_ref, delta, dq_total,
        )
        dk_low[b] = dk.astype(BF16)
        dv_low[b] = dv.astype(BF16)

        @pl.when(b != me)
        def _():
            returned(b, me, 1).start()
            returned(b, me, 2).start()

        return carry

    lax.fori_loop(0, seqs, key_block, 0)

    def close(i, carry):
        dq_low[i] = (dq_total[i] * HDIM**-0.5).astype(BF16)

        @pl.when(i != me)
        def _():
            returned(i, me, 0).start()

        return carry

    lax.fori_loop(0, seqs, close, 0)
    for src, dst in outputs:
        dst[me] = src[me]

    def finish(step, carry):
        peer = lax.rem(me + step, seqs)
        outward(peer, me).wait_send()
        for part in range(3):
            returned(peer, peer, part).wait()
        return carry

    lax.fori_loop(1, seqs, finish, 0)


def self_backward(seqs, windows, grad, query_all, key_all, value_all, attended, logs):
    shape = grad.shape
    dma = pltpu.SemaphoreType.DMA
    vmem = pl.BlockSpec(memory_space=pltpu.VMEM)
    return pl.pallas_call(
        functools.partial(self_backward_kernel, seqs),
        out_shape=(jax.ShapeDtypeStruct(shape, BF16),) * 3,
        in_specs=[pl.BlockSpec(memory_space=pltpu.SMEM)] + [vmem] * 6,
        out_specs=(vmem,) * 3,
        scratch_shapes=[
            pltpu.VMEM(shape, BF16),
            pltpu.VMEM(logs.shape, F32),
            pltpu.VMEM(shape, F32),
            pltpu.VMEM(shape, BF16),
            pltpu.VMEM(shape, BF16),
            pltpu.VMEM(shape, BF16),
            dma((seqs,)),
            dma((seqs,)),
            dma((3, seqs)),
            dma((3, seqs)),
        ],
        compiler_params=pltpu.CompilerParams(
            collective_id=6, has_side_effects=True, vmem_limit_bytes=40 * MIB
        ),
        name="self_backward",
    )(windows, grad, query_all, key_all, value_all, attended, logs)


def cross_forward_kernel(length_ref, q_ref, k_ref, v_ref, crossed_ref, low_ref, log_ref):
    crossed, logs = cross_attend(length_ref[0], q_ref[...], k_ref[...], v_ref[...])
    for head in range(len(logs)):
        log_ref[0, head : head + 1] = logs[head]
    crossed_ref[...] = crossed
    low_ref[...] = crossed.astype(BF16)


def cross_forward(lengths, query, key, value):
    rows, width = query.shape
    blocks = width // LANES
    columns = lambda j: (0, j)
    return pl.pallas_call(
        cross_forward_kernel,
        grid=(blocks,),
        out_shape=(
            jax.ShapeDtypeStruct((rows, width), F32),
            jax.ShapeDtypeStruct((rows, width), BF16),
            jax.ShapeDtypeStruct((blocks, 8, rows), F32),
        ),
        in_specs=[
            pl.BlockSpec(memory_space=pltpu.SMEM),
            pl.BlockSpec((rows, LANES), columns),
            pl.BlockSpec((key.shape[0], LANES), columns),
            pl.BlockSpec((key.shape[0], LANES), columns),
        ],
        out_specs=(
            pl.BlockSpec((rows, LANES), columns),
            pl.BlockSpec((rows, LANES), columns),
            pl.BlockSpec((1, 8, rows), lambda j: (j, 0, 0)),
        ),
        name="cross_forward",
    )(lengths, query, key, value)


def cross_backward_kernel(
    length_ref, q_ref, k_ref, v_ref, grad_ref, crossed_ref, log_ref, dq_ref, dk_ref, dv_ref
):
    dq, dk, dv = cross_grads(
        length_ref[0],
        q_ref[...],
        k_ref[...],
        v_ref[...],
        grad_ref[...],
        crossed_ref[...],
        [log_ref[0, head : head + 1] for head in range(LANES // HDIM)],
    )
    dq_ref[...] = dq.astype(BF16)
    dk_ref[...] = dk.astype(BF16)
    dv_ref[...] = dv.astype(BF16)


def cross_backward(lengths, query, key, value, grad, crossed, logs):
    rows, width = query.shape
    keys = key.shape[0]
    columns = lambda j: (0, j)
    token_block = pl.BlockSpec((rows, LANES), columns)
    key_block = pl.BlockSpec((keys, LANES), columns)
    return pl.pallas_call(
        cross_backward_kernel,
        grid=(width // LANES,),
        out_shape=(
            jax.ShapeDtypeStruct((rows, width), BF16),
            jax.ShapeDtypeStruct((keys, width), BF16),
            jax.ShapeDtypeStruct((keys, width), BF16),
        ),
        in_specs=[
            pl.BlockSpec(memory_space=pltpu.SMEM),
            token_block,
            key_block,
            key_block,
            token_block,
            token_block,
            pl.BlockSpec((1, 8, rows), lambda j: (j, 0, 0)),
        ],
        out_specs=(token_block, key_block, key_block),
        name="cross_backward",
    )(lengths, query, key, value, grad, crossed, logs)


def memory_sum_kernel(seqs, parts_ref, total_ref, arrived, send_sem, recv_sem):
    me, z = lax.axis_index("seq"), lax.axis_index("grp")
    greet_all(me, seqs, lambda j: (j, z))

    def copy_of(peer, slot):
        return remote(
            parts_ref.at[peer], arrived.at[slot], send_sem.at[peer], recv_sem.at[slot], (peer, z)
        )

    def start(step, carry):
        copy_of(lax.rem(me + step, seqs), me).start()
        return carry

    def finish(step, carry):
        peer = lax.rem(me + step, seqs)
        copy_of(peer, peer).wait()
        return carry

    lax.fori_loop(1, seqs, start, 0)
    arrived[me] = parts_ref[me]
    lax.fori_loop(1, seqs, finish, 0)
    total = arrived[0].astype(F32)
    for j in range(1, seqs):
        total = total + arrived[j].astype(F32)
    total_ref[...] = total.astype(BF16)


def memory_sum(seqs, parts):
    dma = pltpu.SemaphoreType.DMA
    vmem = pl.BlockSpec(memory_space=pltpu.VMEM)
    return pl.pallas_call(
        functools.partial(memory_sum_kernel, seqs),
        out_shape=jax.ShapeDtypeStruct(parts.shape[1:], BF16),
        in_specs=[vmem],
        out_specs=vmem,
        scratch_shapes=[pltpu.VMEM(parts.shape, BF16), dma((seqs,)), dma((seqs,))],
        compiler_params=pltpu.CompilerParams(
            collective_id=7, has_side_effects=True, vmem_limit_bytes=32 * MIB
        ),
        name="memory_sum",
    )(parts)


def tiled_layer(
    tokens, memory, cotangent, windows, mem_lengths, owners, master, vectors
):
    rows = tokens.shape[1]
    mem_rows = memory.shape[1]
    seqs, planes = lax.axis_size("seq"), lax.axis_size("grp")
    holder, slot, group, unit = owner_tables(owners, master.shape[0], seqs * planes)
    flat = tokens.reshape(rows, D)
    (
        whole,
        h1,
        joined,
        qkv,
        attended,
        logs,
        x2,
        h2,
        cross_queries,
        mem_acts,
        crossed,
        cross_logs,
        x3,
        h3,
        activation,
        slope,
        mixed,
        memory_padded,
    ) = forward_pass(
        seqs,
        planes,
        windows,
        mem_lengths,
        holder,
        slot,
        master,
        flat,
        memory.reshape(mem_rows, D),
        vectors,
    )
    grad_slots, grad_tokens, grad_memory, vector_sums = backward_pass(
        seqs,
        planes,
        windows,
        mem_lengths,
        group,
        unit,
        whole,
        slope,
        (
            cotangent.reshape(rows, D),
            flat,
            x2,
            x3,
            h1,
            h2,
            h3,
            activation,
            crossed,
            cross_queries,
            mem_acts,
            cross_logs,
            joined,
            attended,
            qkv,
            logs,
            memory_padded,
            vectors,
        ),
    )
    return mixed.reshape(tokens.shape), grad_tokens.reshape(tokens.shape), grad_memory, grad_slots, vector_sums


def plain_layer(
    tokens, memory, cotangent, windows, mem_lengths, owners, master, vectors
):
    rows = tokens.shape[1]
    seqs, planes = lax.axis_size("seq"), lax.axis_size("grp")
    units = owners.shape[0]
    slot_count, unit_rows = (master.shape[0], master.shape[1])
    bias_rows = FF // D
    placed, unit_at, occupied = slot_tables(owners, slot_count, seqs * planes)
    gathered = lax.all_gather(master.astype(BF16), ("seq", "grp"), axis=0, tiled=True)
    stacked = jnp.take(gathered, placed, axis=0).reshape(-1, D)
    memory_whole = lax.all_gather(memory[0], "seq", axis=0, tiled=True)
    self_query, self_key, self_value, self_out = (stacked[i * D : (i + 1) * D] for i in range(4))
    cross_query, cross_key, cross_value, cross_out = (
        stacked[i * D : (i + 1) * D] for i in range(4, 8)
    )
    hidden_in, hidden_out = stacked[8 * D : 8 * D + FF], stacked[8 * D + FF :]

    def by_device(tensor):
        return jnp.swapaxes(tensor.reshape(rows, seqs, D // seqs), 0, 1)

    def by_token(tensor):
        return jnp.swapaxes(tensor, 0, 1).reshape(rows, D)

    stream = tokens.astype(F32).reshape(rows, D)
    normed_one, form_one, inverse_one = norm_forward(stream, vectors[0], vectors[1])
    normed_self = normed_one.astype(BF16)
    query_act = (product(normed_self, self_query) + vectors[6]).astype(BF16)
    key_act = product(normed_self, self_key).astype(BF16)
    value_act = (product(normed_self, self_value) + vectors[7]).astype(BF16)
    joined, query_all, key_all, value_all, attended32, logs = self_forward(
        seqs, windows, by_device(query_act), by_device(key_act), by_device(value_act)
    )
    attended = by_token(joined)
    after_self = stream + product(attended, self_out) + vectors[8]
    normed_two, form_two, inverse_two = norm_forward(after_self, vectors[2], vectors[3])
    normed_cross = normed_two.astype(BF16)
    cross_queries = (product(normed_cross, cross_query) + vectors[9]).astype(BF16)
    mem_key_act = product(memory_whole, cross_key).astype(BF16)
    mem_value_act = (product(memory_whole, cross_value) + vectors[10]).astype(BF16)
    crossed32, crossed, cross_logs = cross_forward(
        mem_lengths, cross_queries, mem_key_act, mem_value_act
    )
    after_cross = after_self + product(crossed, cross_out) + vectors[11]
    normed_three, form_three, inverse_three = norm_forward(after_cross, vectors[4], vectors[5])
    normed_mlp = normed_three.astype(BF16)
    pre_act = product_nt(normed_mlp, hidden_in) + vectors[12 : 12 + bias_rows].reshape(FF)
    activation, slope = jax.jvp(gelu_exact, (pre_act,), (jnp.ones_like(pre_act),))
    activation_bf = activation.astype(BF16)
    result_rows = after_cross + product(activation_bf, hidden_out) + vectors[12 + bias_rows]
    mixed = result_rows.astype(BF16).reshape(tokens.shape)
    grad_out_bf = cotangent.reshape(rows, D)
    grad_stream = cotangent.astype(F32).reshape(rows, D)
    grad_hidden_out = product_tn(activation_bf, grad_out_bf)
    grad_down_bias = jnp.sum(grad_stream, axis=0)
    grad_activation = product_nt(grad_out_bf, hidden_out)
    grad_pre = (grad_activation * slope).astype(BF16)
    grad_hidden_in = product_tn(grad_pre, normed_mlp)
    grad_up_bias = jnp.sum(grad_pre.astype(F32), axis=0)
    grad_normed_mlp = product(grad_pre, hidden_in)
    back_three, grad_gain_three, grad_shift_three = norm_backward(
        grad_normed_mlp, form_three, inverse_three, vectors[4]
    )
    grad_after_cross = grad_stream + back_three
    grad_cross_branch = grad_after_cross.astype(BF16)
    grad_cross_out = product_tn(crossed, grad_cross_branch)
    grad_cross_out_bias = jnp.sum(grad_cross_branch.astype(F32), axis=0)
    grad_crossed = product_nt(grad_cross_branch, cross_out).astype(BF16)
    grad_cross_queries, part_mem_keys, part_mem_values = cross_backward(
        mem_lengths, cross_queries, mem_key_act, mem_value_act, grad_crossed, crossed32, cross_logs
    )
    mem_rows = memory.shape[1]
    mem_parts = jnp.concatenate(
        [part_mem_keys.reshape(seqs, mem_rows, D), part_mem_values.reshape(seqs, mem_rows, D)],
        axis=1,
    )
    mem_sums = memory_sum(seqs, mem_parts)
    mem_flat = memory.reshape(-1, D)
    mem_keys_flat = mem_sums[:mem_rows]
    mem_values_flat = mem_sums[mem_rows:]
    grad_cross_key = product_tn(mem_flat, mem_keys_flat)
    grad_cross_value = product_tn(mem_flat, mem_values_flat)
    grad_cross_value_bias = jnp.sum(mem_values_flat.astype(F32), axis=0)
    grad_memory = (
        product_nt(mem_keys_flat, cross_key) + product_nt(mem_values_flat, cross_value)
    ).reshape(memory.shape)
    grad_cross_query = product_tn(normed_cross, grad_cross_queries)
    grad_cross_query_bias = jnp.sum(grad_cross_queries.astype(F32), axis=0)
    grad_normed_cross = product_nt(grad_cross_queries, cross_query)
    back_two, grad_gain_two, grad_shift_two = norm_backward(
        grad_normed_cross, form_two, inverse_two, vectors[2]
    )
    grad_after_self = grad_after_cross + back_two
    grad_self_branch = grad_after_self.astype(BF16)
    grad_self_out = product_tn(attended, grad_self_branch)
    grad_self_out_bias = jnp.sum(grad_self_branch.astype(F32), axis=0)
    grad_attended = product_nt(grad_self_branch, self_out).astype(BF16)
    grad_queries, grad_keys, grad_values = (
        by_token(part)
        for part in self_backward(
            seqs, windows, by_device(grad_attended), query_all, key_all, value_all, attended32, logs
        )
    )
    grad_self_query = product_tn(normed_self, grad_queries)
    grad_self_key = product_tn(normed_self, grad_keys)
    grad_self_value = product_tn(normed_self, grad_values)
    grad_query_bias = jnp.sum(grad_queries.astype(F32), axis=0)
    grad_value_bias = jnp.sum(grad_values.astype(F32), axis=0)
    grad_normed_self = (
        product_nt(grad_queries, self_query)
        + product_nt(grad_keys, self_key)
        + product_nt(grad_values, self_value)
    )
    back_one, grad_gain_one, grad_shift_one = norm_backward(
        grad_normed_self, form_one, inverse_one, vectors[0]
    )
    grad_tokens = (grad_after_self + back_one).reshape(tokens.shape)
    grad_matrices = jnp.concatenate(
        [
            part.astype(BF16)
            for part in (
                grad_self_query,
                grad_self_key,
                grad_self_value,
                grad_self_out,
                grad_cross_query,
                grad_cross_key,
                grad_cross_value,
                grad_cross_out,
                grad_hidden_in,
                grad_hidden_out,
            )
        ],
        axis=0,
    )
    grad_units = grad_matrices.reshape(units, unit_rows, D)
    small_rows = jnp.stack(
        [
            grad_gain_one,
            grad_shift_one,
            grad_gain_two,
            grad_shift_two,
            grad_gain_three,
            grad_shift_three,
            grad_query_bias,
            grad_value_bias,
            grad_self_out_bias,
            grad_cross_query_bias,
            grad_cross_value_bias,
            grad_cross_out_bias,
        ]
    )
    grad_vectors = jnp.concatenate(
        [small_rows, grad_up_bias.reshape(bias_rows, D), grad_down_bias[None]], axis=0
    )
    grad_slots = lax.psum_scatter(
        jnp.where(
            occupied[:, None, None], jnp.take(grad_units, unit_at, axis=0), jnp.zeros((), BF16)
        ),
        ("seq", "grp"),
        scatter_dimension=0,
        tiled=True,
    )
    grad_vectors = lax.psum(grad_vectors, ("seq", "grp"))
    return mixed, grad_tokens, grad_memory, grad_slots, grad_vectors


def update_kernel(
    master_ref,
    first_ref,
    second_ref,
    grad_ref,
    vectors_ref,
    vec_first_ref,
    vec_second_ref,
    vec_grad_ref,
    memory_ref,
    first_out,
    second_out,
    master_out,
    low_out,
    vec_first_out,
    vec_second_out,
    vectors_out,
    memory_out,
    bias_out,
):
    first, second, weight = adam_step(
        master_ref[...],
        first_ref[...],
        second_ref[...],
        grad_ref[...].astype(F32),
        RATE_MATRIX,
        WEIGHT_DECAY,
    )
    first_out[...] = first
    second_out[...] = second
    master_out[...] = weight
    low_out[...] = weight.astype(BF16)

    @pl.when((pl.program_id(0) == 0) & (pl.program_id(1) == 0))
    def _():
        rows = vectors_ref.shape[0]
        sums = vec_grad_ref[...][:rows]
        vec_first_out[...], vec_second_out[...], vectors_out[...] = adam_step(
            vectors_ref[...], vec_first_ref[...], vec_second_ref[...], sums, RATE_VECTOR, 0.0
        )
        memory_out[...] = memory_ref[...][: memory_out.shape[0]]
        bias_out[...] = sums[rows - 1 :]


def update(master, first, second, grad, vectors, vec_first, vec_second, vec_grad, grad_memory, mem):
    slots, rows, width = master.shape
    part = rows // 2
    block = pl.BlockSpec((1, part, width), lambda s, p: (s, p, 0))

    def whole(shape):
        return pl.BlockSpec(shape, lambda s, p: (0, 0))

    shape = jax.ShapeDtypeStruct
    vec = whole(vectors.shape)
    return pl.pallas_call(
        update_kernel,
        grid=(slots, rows // part),
        out_shape=(shape(master.shape, F32),) * 3
        + (shape(master.shape, BF16),)
        + (shape(vectors.shape, F32),) * 3
        + (shape((mem, width), F32), shape((1, width), F32)),
        in_specs=[block] * 4 + [vec] * 3 + [whole(vec_grad.shape), whole(grad_memory.shape)],
        out_specs=(block,) * 4 + (vec,) * 3 + (whole((mem, width)), whole((1, width))),
        compiler_params=pltpu.CompilerParams(vmem_limit_bytes=60 * MIB),
        name="update",
    )(master, first, second, grad, vectors, vec_first, vec_second, vec_grad, grad_memory)


def local(
    tokens,
    memory,
    cotangent,
    windows,
    mem_lengths,
    owners,
    master,
    first_moment,
    second_moment,
    vectors,
    vec_first,
    vec_second,
):
    tiled = lax.axis_size("seq") == 8 and master.shape[1] % (32 * lax.axis_size("grp")) == 0
    layer = tiled_layer if tiled else plain_layer
    mixed, grad_tokens, grad_memory, grad_slots, grad_vectors = layer(
        tokens, memory, cotangent, windows, mem_lengths, owners, master, vectors
    )
    if tiled:
        (
            new_first,
            new_second,
            new_master,
            master_copy,
            vec_first_out,
            vec_second_out,
            vectors_out,
            grad_memory,
            grad_out_bias,
        ) = update(
            master,
            first_moment,
            second_moment,
            grad_slots,
            vectors,
            vec_first,
            vec_second,
            grad_vectors,
            grad_memory,
            memory.shape[1],
        )
        grad_memory = grad_memory.reshape(memory.shape)
        grad_out_bias = grad_out_bias.reshape(D)
    else:
        new_first, new_second, new_master = adam_step(
            master,
            first_moment,
            second_moment,
            grad_slots.astype(F32),
            RATE_MATRIX,
            WEIGHT_DECAY,
        )
        master_copy = new_master.astype(BF16)
        vec_first_out, vec_second_out, vectors_out = adam_step(
            vectors, vec_first, vec_second, grad_vectors, RATE_VECTOR, 0.0
        )
        grad_out_bias = grad_vectors[vectors.shape[0] - 1]
    return (
        mixed,
        grad_tokens,
        grad_memory,
        new_first,
        new_second,
        new_master,
        master_copy,
        vec_first_out,
        vec_second_out,
        vectors_out,
        grad_out_bias,
    )


def solution(mesh):
    placed = (
        P("grp", "seq", None),
        P("grp", "seq", None),
        P("grp", "seq", None),
        P("grp"),
        P("grp"),
        P(),
        P(("seq", "grp"), None, None),
        P(("seq", "grp"), None, None),
        P(("seq", "grp"), None, None),
        P(),
        P(),
        P(),
    )
    return jax.shard_map(
        local,
        mesh=mesh,
        in_specs=placed,
        out_specs=(
            P("grp", "seq", None),
            P("grp", "seq", None),
            P("grp", "seq", None),
            P(("seq", "grp"), None, None),
            P(("seq", "grp"), None, None),
            P(("seq", "grp"), None, None),
            P(("seq", "grp"), None, None),
            P(),
            P(),
            P(),
            P(),
        ),
        check_vma=False,
    )
```

```python
import functools

import jax
import jax.numpy as jnp
from jax import lax
from jax.experimental import pallas as pl
from jax.experimental.pallas import tpu as pltpu
from jax.sharding import PartitionSpec as P

D = 1024
FF = 4096
HEADS = 16
HDIM = 64
STEP = 10


NEG_FILL = -1e30
NORM_EPS = 1e-05
BETA_ONE = 0.5
BETA_TWO = 0.75
RATE_MATRIX = 0.03
RATE_VECTOR = 0.4
WEIGHT_DECAY = 0.01
ADAM_EPS = 1e-08

BF16 = jnp.bfloat16
F32 = jnp.float32
LANES = 128
GROUP_UNITS = 4
GATHER_LIGHT = 4
REDUCE_LIGHT = 4
MIB = 1 << 20


def product(left, right):
    return jnp.dot(left, right, preferred_element_type=F32)


def product_tn(left, right):
    return jnp.einsum("rd,re->de", left, right, preferred_element_type=F32)


def product_nt(left, right):
    return jnp.einsum("rd,ed->re", left, right, preferred_element_type=F32)


def slot_tables(owners, slot_count, holders):
    unit_count = owners.shape[0]
    positions = lax.iota(jnp.int32, unit_count)
    same_owner = owners[None, :] == owners[:, None]
    slot_rank = jnp.sum(
        (same_owner & (positions[None, :] < positions[:, None])).astype(jnp.int32), axis=1
    )
    placed = owners * slot_count + slot_rank
    slot_ids = lax.iota(jnp.int32, holders * slot_count)
    matches = slot_ids[:, None] == placed[None, :]
    occupied = jnp.sum(matches.astype(jnp.int32), axis=1) > 0
    unit_at = jnp.sum(jnp.where(matches, positions[None, :], 0), axis=1)
    return (placed, unit_at, occupied)


def norm_forward(stream, gain_row, shift_row):
    row_mean = jnp.mean(stream, axis=-1, keepdims=True)
    centered = stream - row_mean
    inverse = lax.rsqrt(jnp.mean(centered * centered, axis=-1, keepdims=True) + NORM_EPS)
    normal_form = centered * inverse
    return (normal_form * gain_row + shift_row, normal_form, inverse)


def norm_backward(upstream, normal_form, inverse, gain_row):
    scaled = upstream * gain_row
    first_term = jnp.mean(scaled, axis=-1, keepdims=True)
    second_term = jnp.mean(scaled * normal_form, axis=-1, keepdims=True)
    grad_in = inverse * (scaled - first_term - normal_form * second_term)
    return (grad_in, jnp.sum(upstream * normal_form, axis=0), jnp.sum(upstream, axis=0))


def gelu_exact(values):
    return jax.nn.gelu(values, approximate=False)


def adam_step(weight, first, second_in, upstream, rate, decay):
    first_new = BETA_ONE * first + (1.0 - BETA_ONE) * upstream
    second_new = BETA_TWO * second_in + (1.0 - BETA_TWO) * upstream * upstream
    first_hat = first_new / (1.0 - BETA_ONE**STEP)
    second_hat = second_new / (1.0 - BETA_TWO**STEP)
    weight_new = weight - rate * (first_hat / (jnp.sqrt(second_hat) + ADAM_EPS) + decay * weight)
    return (first_new, second_new, weight_new)


def remote(src, dst, send_sem, recv_sem, target):
    return pltpu.make_async_remote_copy(
        src_ref=src,
        dst_ref=dst,
        send_sem=send_sem,
        recv_sem=recv_sem,
        device_id=target,
        device_id_type=pl.DeviceIdType.MESH,
    )


def greet_all(me, total, target_of):
    barrier = pltpu.get_barrier_semaphore()

    def signal(step, carry):
        pl.semaphore_signal(
            barrier,
            inc=1,
            device_id=target_of(lax.rem(me + step, total)),
            device_id_type=pl.DeviceIdType.MESH,
        )
        return carry

    lax.fori_loop(1, total, signal, 0)
    pl.semaphore_wait(barrier, total - 1)


class Place:
    def __init__(self, planes):
        self.seq = lax.axis_index("seq")
        self.z = lax.axis_index("grp")
        self.planes = planes
        self.core = lax.rem(self.seq, 2)
        self.x = lax.rem(lax.div(self.seq, 2), 2)
        self.y = lax.div(self.seq, 4)

    def at(self, core, x, y, z):
        return (y * 4 + x * 2 + core, z)

    def sibling(self):
        return self.at(1 - self.core, self.x, self.y, self.z)

    def x_peer(self):
        return self.at(self.core, 1 - self.x, self.y, self.z)

    def y_peer(self):
        return self.at(self.core, self.x, 1 - self.y, self.z)

    def above(self):
        return (self.seq, self.z + 1)

    def below(self):
        return (self.seq, self.z - 1)

    def peers(self, half):
        return (self.x_peer(), self.y_peer()) if half == 0 else (self.y_peer(), self.x_peer())

    def bits(self, half):
        return (self.y, self.x) if half == 0 else (self.x, self.y)


def tile_of(device, planes, half, unit_rows):
    seq, z = lax.div(device, planes), lax.rem(device, planes)
    core, x, y = lax.rem(seq, 2), lax.rem(lax.div(seq, 2), 2), lax.div(seq, 4)
    wide, narrow = jnp.where(half == 0, y, x), jnp.where(half == 0, x, y)
    half_rows = unit_rows // 2
    block = half_rows // planes
    first_row = pl.multiple_of(half * half_rows + z * block, block)
    first_column = pl.multiple_of((core * 4 + wide * 2 + narrow) * LANES, LANES)
    return (pl.ds(first_row, block), pl.ds(first_column, LANES))


def loop(first, last, work):
    def one(index, carry):
        work(index)
        return carry

    lax.fori_loop(first, last, one, 0)


class Gather:
    def __init__(self, planes, own_ref, whole_ref, own_sem, z_send, z_recv, p_send, p_recv):
        self.place = Place(planes)
        self.planes = planes
        self.z = self.place.z
        self.own_ref, self.whole_ref = own_ref, whole_ref
        self.own_sem = own_sem
        self.z_send, self.z_recv = z_send, z_recv
        self.p_send, self.p_recv = p_send, p_recv
        self.groups = whole_ref.shape[0]
        self.split = GATHER_LIGHT
        self.leave = 1 + 2 * (planes - 1)
        self.arrived = self.leave + 3

    def block(self, g, half, plane):
        wide, narrow = self.place.bits(half)
        first = self.place.core * 4 + wide * 2 + narrow
        return self.whole_ref.at[g, half, first, plane]

    def pair(self, g, half, plane):
        wide, narrow = self.place.bits(half)
        return self.whole_ref.at[g, half, pl.ds(self.place.core * 4 + wide * 2, 2), plane]

    def line(self, g, half, way, hop, plane, light):
        ref = self.block(g, half, plane) if light else self.pair(g, half, plane)
        return remote(
            self.own_ref.at[g, half] if light and hop == 0 else ref,
            ref,
            self.z_send.at[g, half, way, hop],
            self.z_recv.at[g, half, way, hop],
            self.place.above() if way == 0 else self.place.below(),
        )

    def planar(self, g, half, order, light, arriving=False):
        wide, narrow = self.place.bits(half)
        core = self.place.core
        if order == 0:
            first = core * 4 + wide * 2 + (1 - narrow if arriving else narrow)
            if light:
                ref = src = self.whole_ref.at[g, half, first]
            else:
                ref = self.whole_ref.at[g, half, first, self.z]
                src = self.own_ref.at[g, half]
        else:
            if order == 1:
                first, columns = core * 4 + (1 - wide if arriving else wide) * 2, 2
            else:
                first, columns = (1 - core if arriving else core) * 4, 4
            ref = src = self.whole_ref.at[g, half, pl.ds(first, columns)]
        target = self.place.peers(half)[order] if order < 2 else self.place.sibling()
        return remote(
            src, ref, self.p_send.at[g, half, order], self.p_recv.at[g, half, order], target
        )

    def own_copy(self, g, half):
        return pltpu.make_async_copy(
            self.own_ref.at[g, half],
            self.block(g, half, self.z),
            self.own_sem.at[g, half],
        )

    def enter_line(self, g, half, light):
        z = self.z

        @pl.when(z < self.planes - 1)
        def _():
            self.line(g, half, 0, 0, z, light).start()

        @pl.when(z > 0)
        def _():
            self.line(g, half, 1, 0, z, light).start()

    def hop(self, g, half, k, light):
        z, planes = self.z, self.planes

        @pl.when(z >= k)
        def _():
            self.line(g, half, 0, k - 1, z - k, light).wait_recv()

        if k < planes - 1:

            @pl.when((z >= k) & (z < planes - 1))
            def _():
                self.line(g, half, 0, k, z - k, light).start()

        @pl.when(z + k < planes)
        def _():
            self.line(g, half, 1, k - 1, z + k, light).wait_recv()

        if k < planes - 1:

            @pl.when((z + k < planes) & (z > 0))
            def _():
                self.line(g, half, 1, k, z + k, light).start()

    def exchange(self, g, half, order, light):
        self.planar(g, half, order, light, arriving=True).wait_recv()
        if order < 2:
            self.planar(g, half, order + 1, light).start()

    def heavy_start(self, g, half):
        self.own_copy(g, half).start()
        self.planar(g, half, 0, False).start()

    def heavy_enter(self, g, half):
        self.own_copy(g, half).wait()
        self.planar(g, half, 0, False, arriving=True).wait_recv()
        self.enter_line(g, half, False)

    def heavy_leave(self, g, half):
        self.hop(g, half, self.planes - 1, False)
        self.planar(g, half, 1, False).start()

    def light_start(self, g, half):
        self.own_copy(g, half).start()
        self.enter_line(g, half, True)

    def light_leave(self, g, half):
        self.hop(g, half, self.planes - 1, True)
        self.own_copy(g, half).wait()
        self.planar(g, half, 0, True).start()

    def tick(self, t):
        planes, leave = self.planes, self.leave

        def during(lag, action, first, last):
            g = t - lag

            @pl.when((g >= first) & (g < last))
            def _():
                for half in range(2):
                    action(g, half)

        def heavy(lag, action):
            during(lag, action, self.split, self.groups)

        def light(lag, action):
            during(lag, action, 0, self.split)

        during(leave + 3, lambda g, half: self.exchange(g, half, 2, False), 0, self.groups)
        during(leave + 2, lambda g, half: self.exchange(g, half, 1, False), 0, self.groups)
        heavy(leave, self.heavy_leave)
        light(leave, lambda g, half: self.exchange(g, half, 0, True))
        for k in reversed(range(1, planes - 1)):
            heavy(1 + 2 * k, lambda g, half, k=k: self.hop(g, half, k, False))
        light(leave - 2, self.light_leave)
        for k in reversed(range(1, planes - 1)):
            light(1 + k, lambda g, half, k=k: self.hop(g, half, k, True))
        heavy(1, self.heavy_enter)
        heavy(0, self.heavy_start)
        light(0, self.light_start)

    def drain(self):
        z, planes = self.z, self.planes

        def one(g, light):
            for half in range(2):
                for k in range(planes - 1):

                    @pl.when((z >= k) & (z < planes - 1))
                    def _(half=half, k=k):
                        self.line(g, half, 0, k, z - k, light).wait_send()

                    @pl.when((z + k < planes) & (z > 0))
                    def _(half=half, k=k):
                        self.line(g, half, 1, k, z + k, light).wait_send()

                for order in range(3):
                    self.planar(g, half, order, light).wait_send()

        loop(0, self.split, lambda g: one(g, True))
        loop(self.split, self.groups, lambda g: one(g, False))


def gather_scratch(planes, groups):
    dma = pltpu.SemaphoreType.DMA
    return [
        dma((groups, 2)),
        dma((groups, 2, 2, planes - 1)),
        dma((groups, 2, 2, planes - 1)),
        dma((groups, 2, 3)),
        dma((groups, 2, 3)),
    ]


NORM_ROWS = 32


def norm_into(stream_ref, gain_row, shift_row, out_ref):
    def one(block):
        span = pl.ds(pl.multiple_of(block * NORM_ROWS, NORM_ROWS), NORM_ROWS)
        normed = norm_forward(stream_ref[span].astype(F32), gain_row, shift_row)[0]
        out_ref[span] = normed.astype(BF16)

    loop(0, out_ref.shape[0] // NORM_ROWS, one)


def weight_block(weight_ref, slot, block, unit):
    halves, planes = weight_ref.shape[1], weight_ref.shape[3]
    return [weight_ref[slot, h, block, p, unit] for h in range(halves) for p in range(planes)]


def dot_tiles(left, weight_ref, slot, emit, turned=False, unrolled=False):
    blocks, units = weight_ref.shape[2], weight_ref.shape[4]

    def one(j, carry):
        if turned:
            weight = jnp.concatenate(
                [jnp.concatenate(weight_block(weight_ref, slot, b, j), 0) for b in range(blocks)], 1
            )
            emit(j, dot_nt(left, weight))
        else:
            weight = jnp.concatenate(
                [
                    jnp.concatenate(
                        sum(
                            (weight_block(weight_ref, slot, 2 * j + b, u) for u in range(units)),
                            [],
                        ),
                        0,
                    )
                    for b in range(2)
                ],
                1,
            )
            emit(j, dot_nn(left, weight))
        return carry

    if unrolled:
        for j in range(4):
            one(j, 0)
    else:
        lax.fori_loop(0, 4, one, 0)


TRAVEL = (0, 1, 2, 3, 5, 6, 4, 7, 8, 9, 10, 11, 12, 13, 14, 15)
REDUCE = (12, 13, 14, 15, 8, 9, 10, 11, 7, 4, 3, 5, 6, 0, 1, 2)


def tables_kernel(slots, owners_ref, holder_ref, slot_ref, group_ref, unit_ref, count):
    holders = count.shape[0]

    def clear(n, carry):
        count[n] = 0
        for s in range(slots):
            group_ref[n * slots + s] = -1
            unit_ref[n * slots + s] = 0
        return carry

    lax.fori_loop(0, holders, clear, 0)
    for unit in range(owners_ref.shape[0]):
        matrix, part = divmod(unit, GROUP_UNITS)
        owner = owners_ref[unit]
        slot = count[owner]
        count[owner] = slot + 1
        travel = TRAVEL.index(matrix) * GROUP_UNITS + part
        holder_ref[travel] = owner
        slot_ref[travel] = slot
        group_ref[owner * slots + slot] = REDUCE.index(matrix)
        unit_ref[owner * slots + slot] = part


def owner_tables(owners, slots, holders):
    units = owners.shape[0]
    smem = pl.BlockSpec(memory_space=pltpu.SMEM)
    return pl.pallas_call(
        functools.partial(tables_kernel, slots),
        out_shape=(jax.ShapeDtypeStruct((units,), jnp.int32),) * 2
        + (jax.ShapeDtypeStruct((holders * slots,), jnp.int32),) * 2,
        in_specs=[smem],
        out_specs=(smem,) * 4,
        scratch_shapes=[pltpu.SMEM((holders,), jnp.int32)],
        name="owner_tables",
    )(owners)


def forward_kernel(
    seqs,
    planes,
    window_ref,
    length_ref,
    holder_ref,
    slot_ref,
    master_ref,
    tokens_ref,
    memory_ref,
    vectors_ref,
    whole_ref,
    h1_ref,
    joined_ref,
    qkv_all,
    rounded,
    log_ref,
    x2_ref,
    h2_ref,
    cq_ref,
    mem_ref,
    crossed_low_ref,
    cross_log_ref,
    x3_ref,
    h3_ref,
    act_ref,
    slope_ref,
    mixed_ref,
    padded_ref,
    master_wide,
    master_low,
    tiles,
    own,
    memory_came,
    memory_wide,
    memory_all,
    weights,
    qkv_out,
    down,
    own_sem,
    z_send,
    z_recv,
    p_send,
    p_recv,
    load_sem,
    master_sem,
    tile_send,
    tile_recv,
    memory_send,
    memory_recv,
    send_sem,
    recv_sem,
    back_send,
    back_recv,
):
    fetch = pltpu.make_async_copy(master_ref, master_wide, master_sem)
    fetch.start()
    gather = Gather(planes, own, whole_ref, own_sem, z_send, z_recv, p_send, p_recv)
    place = gather.place
    me, z = place.seq, place.z
    rows = tokens_ref.shape[0]
    width = D // seqs
    tile = 2 * LANES
    total = seqs * planes
    here = me * planes + z
    mem_rows = memory_all.shape[0] // seqs
    greet_all(here, total, lambda j: (lax.div(j, planes), lax.rem(j, planes)))

    def vector(index):
        return vectors_ref[index : index + 1]

    def columns_of(j):
        return pl.ds(pl.multiple_of(j * tile, tile), tile)

    def tile_copy(peer, slot, half):
        tile_rows, tile_columns = tile_of(peer, planes, half, master_low.shape[1])
        return remote(
            master_low.at[:, tile_rows, tile_columns],
            tiles.at[slot, half],
            tile_send.at[peer, half],
            tile_recv.at[slot, half],
            (lax.div(peer, planes), lax.rem(peer, planes)),
        )

    def memory_copy(peer, slot):
        return remote(
            padded_ref, memory_came.at[slot], memory_send.at[peer], memory_recv.at[slot], (peer, z)
        )

    def spread():
        own_memory = memory_ref[...].astype(F32)
        if padded_ref.shape[0] > mem_rows:
            fill = jnp.zeros((padded_ref.shape[0] - mem_rows, D), F32)
            own_memory = jnp.concatenate([own_memory, fill], 0)
        padded_ref[...] = own_memory.astype(BF16)
        fetch.wait()
        part = 64

        def lower(index):
            slot, block = lax.div(index, master_low.shape[1] // part), lax.rem(
                index, master_low.shape[1] // part
            )
            span = pl.ds(pl.multiple_of(block * part, part), part)
            master_low[slot, span] = master_wide[slot, span].astype(BF16)

        loop(0, master_low.shape[0] * master_low.shape[1] // part, lower)

        def start(step):
            peer = lax.rem(here + step, total)
            loop(0, 2, lambda half: tile_copy(peer, here, half).start())

        loop(1, total, start)
        loop(1, seqs, lambda step: memory_copy(lax.rem(me + step, seqs), me).start())

        def keep_own(half):
            tile_rows, tile_columns = tile_of(here, planes, half, master_low.shape[1])
            tiles[here, half] = master_low[:, tile_rows, tile_columns]

        loop(0, 2, keep_own)
        memory_came[me] = padded_ref[...]
        norm_into(tokens_ref, vector(0), vector(1), h1_ref)

        def finish_memory(step):
            peer = lax.rem(me + step, seqs)
            memory_copy(peer, peer).wait()

        loop(1, seqs, finish_memory)

        def widen(j):
            span = pl.ds(pl.multiple_of(j * mem_rows, 8), mem_rows)
            memory_wide[span] = memory_came[j].astype(F32)[:mem_rows]

        loop(0, seqs, widen)

        def narrow(block):
            span = pl.ds(pl.multiple_of(block * part, part), part)
            memory_all[span] = memory_wide[span].astype(BF16)

        loop(0, memory_all.shape[0] // part, narrow)

        def finish(step):
            peer = lax.rem(here + total - step, total)
            loop(0, 2, lambda half: tile_copy(peer, peer, half).wait())

        loop(1, total, finish)

        def keep(unit):
            g, u = lax.div(unit, GROUP_UNITS), lax.rem(unit, GROUP_UNITS)
            for half in range(2):
                own[g, half, u] = tiles[holder_ref[unit], half, slot_ref[unit]]

        loop(0, holder_ref.shape[0], keep)

    def load(position, slot):
        return pltpu.make_async_copy(whole_ref.at[position], weights.at[slot], load_sem.at[slot])

    def outward(part, peer, slot):
        return remote(
            qkv_out.at[part, peer],
            qkv_all.at[part, slot],
            send_sem.at[part, peer],
            recv_sem.at[part, slot],
            (peer, z),
        )

    def backward_copy(peer, slot):
        return remote(
            rounded.at[peer],
            joined_ref.at[:, pl.ds(pl.multiple_of(slot * width, width), width)],
            back_send.at[peer],
            back_recv.at[slot],
            (peer, z),
        )

    def project(part):
        load(part, part).start()
        load(part, part).wait()
        bias_row = 6 + lax.div(part, 2)

        def emit(j, result):
            bias = vectors_ref[pl.ds(bias_row, 1), columns_of(j)]
            result = (result + jnp.where(part == 1, 0.0, bias)).astype(BF16)
            for piece in range(tile // width):
                qkv_out[part, j * (tile // width) + piece] = result[
                    :, piece * width : (piece + 1) * width
                ]

        dot_tiles(h1_ref[...], weights, part, emit, unrolled=True)
        loop(1, seqs, lambda step: outward(part, lax.rem(me + step, seqs), me).start())
        qkv_all[part, me] = qkv_out[part, me]

    head_count = width // HDIM

    def query_block(i):
        def arrive(ahead):
            @pl.when((lax.rem(i, 2) == 0) & (i + ahead != me))
            def _():
                loop(0, 3, lambda part: outward(part, i + ahead, i + ahead).wait_recv())

        loop(0, 2, arrive)
        rounded[i] = attend_pairs(i, rows, head_count, window_ref[0], qkv_all, log_ref).astype(BF16)

        @pl.when(i != me)
        def _():
            backward_copy(i, me).start()

        @pl.when(i == me)
        def _():
            joined_ref[:, pl.ds(pl.multiple_of(i * width, width), width)] = rounded[i]

    def after_self():
        def arrive(step):
            peer = lax.rem(me + step, seqs)
            backward_copy(peer, peer).wait_recv()

        loop(1, seqs, arrive)
        load(3, 0).wait()

        def emit(j, result):
            columns = columns_of(j)
            x2_ref[:, columns] = (
                tokens_ref[:, columns].astype(F32) + result + vectors_ref[8:9, columns]
            )

        dot_tiles(joined_ref[...], weights, 0, emit, unrolled=True)
        norm_into(x2_ref, vector(2), vector(3), h2_ref)
        load(6, 1).wait()

        def emit_query(j, result):
            columns = columns_of(j)
            cq_ref[:, columns] = (result + vectors_ref[9:10, columns]).astype(BF16)

        dot_tiles(h2_ref[...], weights, 1, emit_query, unrolled=True)

    def memory_rows(part):
        load(4 + part, part).start()
        load(4 + part, part).wait()

        def emit(j, result):
            columns = columns_of(j)
            bias = jnp.where(part == 1, vectors_ref[10:11, columns], 0.0)
            mem_ref[part, :, columns] = (result + bias).astype(BF16)

        dot_tiles(memory_all[...], weights, part, emit, unrolled=True)

    def cross_blocks(first, last):
        def one(j):
            columns = pl.ds(pl.multiple_of(j * LANES, LANES), LANES)
            crossed, logs = cross_attend(
                length_ref[0], cq_ref[:, columns], mem_ref[0, :, columns], mem_ref[1, :, columns]
            )
            for head in range(len(logs)):
                cross_log_ref[j, head : head + 1] = logs[head]
            crossed_low_ref[:, columns] = crossed.astype(BF16)

        loop(first, last, one)

    def after_cross():
        load(7, 2).wait()

        def emit(j, result):
            columns = columns_of(j)
            total = x2_ref[:, columns] + result + vectors_ref[11:12, columns]
            x3_ref[:, columns] = total
            down[:, columns] = total + vectors_ref[12 + FF // D : 13 + FF // D, columns]

        dot_tiles(crossed_low_ref[...], weights, 2, emit, unrolled=True)
        norm_into(x3_ref, vector(4), vector(5), h3_ref)

    def hidden_up(j):
        slot = lax.rem(j + 3, 4)
        load(8 + j, slot).wait()

        def emit(r, result):
            columns = columns_of(r)
            spread = pl.ds(pl.multiple_of(j * D + r * tile, tile), tile)
            pre = result + vectors_ref[pl.ds(12 + j, 1), columns]
            cumulative = 0.5 * (1.0 + lax.erf(pre * 0.5**0.5))
            density = jnp.exp(-0.5 * pre * pre) * (2.0 * jnp.pi) ** -0.5
            act_ref[:, spread] = (pre * cumulative).astype(BF16)
            slope_ref[:, spread] = (cumulative + pre * density).astype(BF16)

        dot_tiles(h3_ref[...], weights, slot, emit, turned=True, unrolled=True)

        @pl.when(j < 3)
        def _():
            load(12 + j, slot).start()

    def hidden_down(j):
        slot = lax.rem(j + 3, 4)
        load(12 + j, slot).wait()
        left = act_ref[:, pl.ds(pl.multiple_of(j * D, D), D)]

        def emit(r, result):
            columns = columns_of(r)
            down[:, columns] = down[:, columns] + result

        dot_tiles(left, weights, slot, emit, unrolled=True)

    arrived = gather.arrived

    def tick(t):
        gather.tick(t)

        @pl.when((t >= arrived) & (t < arrived + 3))
        def _():
            project(t - arrived)

        first_block = arrived + 3

        @pl.when((t >= first_block) & (t < first_block + seqs))
        def _():
            query_block(t - first_block)

        @pl.when((t >= arrived + 4) & (t < arrived + 6))
        def _():
            memory_rows(t - arrived - 4)

        early = arrived + 6
        for step, (position, slot) in enumerate(((3, 0), (6, 1), (7, 2), (8, 3))):

            @pl.when(t == early + step)
            def _(position=position, slot=slot):
                load(position, slot).start()

        late = first_block + seqs

        @pl.when(t == late)
        def _():
            after_self()
            load(9, 0).start()
            load(10, 1).start()

        @pl.when((t >= late) & (t < late + 2))
        def _():
            cross_blocks(4 * (t - late), 4 * (t - late) + 4)

        @pl.when(t == late + 1)
        def _():
            after_cross()
            load(11, 2).start()

        hidden = late + 2

        @pl.when((t >= hidden) & (t < hidden + 2))
        def _():
            loop(2 * (t - hidden), 2 * (t - hidden) + 2, hidden_up)

        @pl.when(t == hidden + 2)
        def _():
            load(15, 2).start()

        @pl.when(t > hidden)
        def _():
            loop(jnp.where(t == hidden + 1, 0, 1), jnp.where(t == hidden + 1, 1, 4), hidden_down)

    spread()
    loop(0, gather.groups + arrived, tick)

    def close(block):
        span = pl.ds(pl.multiple_of(block * NORM_ROWS, NORM_ROWS), NORM_ROWS)
        mixed_ref[span] = down[span].astype(BF16)

    loop(0, rows // NORM_ROWS, close)

    def finish(step):
        peer = lax.rem(me + step, seqs)
        loop(0, 3, lambda part: outward(part, peer, me).wait_send())
        backward_copy(peer, me).wait_send()

    loop(1, seqs, finish)
    gather.drain()


def forward_pass(
    seqs, planes, windows, lengths, holder, slot, master, tokens, memory, vectors
):
    mem = seqs * memory.shape[0]
    padded = memory.shape[0] + -memory.shape[0] % 16
    groups = holder.shape[0] // GROUP_UNITS
    slots, unit_rows = master.shape[:2]
    block = (unit_rows // 2 // planes, LANES)
    matrix = (2, D // LANES, planes, GROUP_UNITS) + block
    rows = tokens.shape[0]
    width = D // seqs
    dma = pltpu.SemaphoreType.DMA
    vmem = pl.BlockSpec(memory_space=pltpu.VMEM)
    smem = pl.BlockSpec(memory_space=pltpu.SMEM)
    anywhere = pl.BlockSpec(memory_space=pl.ANY)
    shape = jax.ShapeDtypeStruct
    by_head = (seqs, rows, width)
    outs = (
        shape((groups,) + matrix, BF16),
        shape((rows, D), BF16),
        shape((rows, D), BF16),
        shape((3,) + by_head, BF16),
        shape(by_head, BF16),
        shape((seqs, 8, rows), F32),
        shape((rows, D), F32),
        shape((rows, D), BF16),
        shape((rows, D), BF16),
        shape((2, mem, D), BF16),
        shape((rows, D), BF16),
        shape((D // LANES, 8, rows), F32),
        shape((rows, D), F32),
        shape((rows, D), BF16),
        shape((rows, FF), BF16),
        shape((rows, FF), BF16),
        shape((rows, D), BF16),
        shape((padded, D), BF16),
    )
    return pl.pallas_call(
        functools.partial(forward_kernel, seqs, planes),
        out_shape=outs,
        in_specs=[smem] * 4 + [anywhere, vmem, vmem, vmem],
        out_specs=(anywhere,) + (vmem,) * (len(outs) - 1),
        scratch_shapes=[
            pltpu.VMEM(master.shape, F32),
            pltpu.VMEM(master.shape, BF16),
            pltpu.VMEM((seqs * planes, 2, slots) + block, BF16),
            pltpu.VMEM((groups, 2, GROUP_UNITS) + block, BF16),
            pltpu.VMEM((seqs, padded, D), BF16),
            pltpu.VMEM((mem, D), F32),
            pltpu.VMEM((mem, D), BF16),
            pltpu.VMEM((4,) + matrix, BF16),
            pltpu.VMEM((3,) + by_head, BF16),
            pltpu.VMEM((rows, D), F32),
        ]
        + gather_scratch(planes, groups)
        + [
            dma((4,)),
            dma(()),
            dma((seqs * planes, 2)),
            dma((seqs * planes, 2)),
            dma((seqs,)),
            dma((seqs,)),
        ]
        + [dma((3, seqs)), dma((3, seqs)), dma((seqs,)), dma((seqs,))],
        compiler_params=pltpu.CompilerParams(
            collective_id=2,
            has_side_effects=True,
            vmem_limit_bytes=56 * MIB,
        ),
        name="forward_pass",
    )(windows, lengths, holder, slot, master, tokens, memory, vectors)


GRAD_SLOTS = 4
COLUMN_SLOTS = 8


class Reduce:
    def __init__(
        self,
        planes,
        made,
        theirs_far,
        wide_far,
        chain_far,
        sums_ref,
        theirs,
        wide_in,
        narrow_in,
        narrow_all,
        column,
        chain_in,
        light_in,
        load_sem,
        chain_sem,
        c_send,
        c_recv,
        p_send,
        p_recv,
        z_send,
        z_recv,
    ):
        self.place = Place(planes)
        self.planes = planes
        self.z = self.place.z
        self.made = made
        self.theirs_far, self.wide_far, self.chain_far = theirs_far, wide_far, chain_far
        self.sums_ref = sums_ref
        self.theirs, self.wide_in = theirs, wide_in
        self.narrow_in, self.column, self.chain_in = narrow_in, column, chain_in
        self.narrow_all, self.light_in = narrow_all, light_in
        self.load_sem, self.chain_sem = load_sem, chain_sem
        self.c_send, self.c_recv = c_send, c_recv
        self.p_send, self.p_recv = p_send, p_recv
        self.z_send, self.z_recv = z_send, z_recv
        self.groups = theirs_far.shape[0]
        self.enter = 3
        self.leave = self.enter + 2 * (planes - 1)
        self.last = self.leave + 1
        self.split = self.groups - REDUCE_LIGHT
        self.light_enter = self.enter + 2

    def to_sibling(self, g):
        src = self.made.at[lax.rem(g, GRAD_SLOTS), :, pl.ds((1 - self.place.core) * 4, 4)]
        return remote(
            src, self.theirs_far.at[g], self.c_send.at[g], self.c_recv.at[g], self.place.sibling()
        )

    def planar(self, g, half, order, light=False):
        place = self.place
        wide, narrow = place.bits(half)
        narrow_peer, wide_peer = place.peers(half)
        if order == 0:
            slot = lax.rem(g, GRAD_SLOTS)
            src = self.made.at[slot, half, pl.ds(place.core * 4 + (1 - wide) * 2, 2)]
            dst, target = self.wide_far.at[g, half], wide_peer
        elif light:
            src = self.column.at[lax.rem(g, COLUMN_SLOTS), :, half, 1 - narrow]
            dst, target = self.narrow_all.at[g - self.split, half], narrow_peer
        else:
            src = self.column.at[lax.rem(g, COLUMN_SLOTS), self.z, half, 1 - narrow]
            dst, target = self.narrow_in.at[g, half], narrow_peer
        return remote(
            src, dst, self.p_send.at[g, half, order], self.p_recv.at[g, half, order], target
        )

    def load(self, g, order):
        src, dst = ((self.theirs_far, self.theirs), (self.wide_far, self.wide_in))[order]
        return pltpu.make_async_copy(src.at[g], dst, self.load_sem.at[order])

    def plane_at(self, way, reach):
        return reach if way == 0 else self.planes - 1 - reach

    def chain(self, g, way, reach, light):
        src = self.column.at[lax.rem(g, COLUMN_SLOTS), self.plane_at(way, reach)]
        dst = self.chain_far.at[g, way, reach - 1]
        return remote(
            src.at[:, 0] if light else src,
            dst.at[:, 0] if light else dst,
            self.z_send.at[g, way, reach - 1],
            self.z_recv.at[g, way, reach - 1],
            self.place.above() if way == 0 else self.place.below(),
        )

    def chain_load(self, g, way, reach, light):
        src = self.chain_far.at[g, way, reach - 1]
        dst = self.light_in if light else self.chain_in
        return pltpu.make_async_copy(
            src.at[:, 0] if light else src,
            dst.at[way, reach - 1],
            self.chain_sem.at[1 if light else 0, way, reach - 1],
        )

    def chain_of(self, t, way, action):
        here = self.z if way == 0 else self.planes - 1 - self.z
        for light in (False, True):
            lag = self.light_enter + here if light else self.enter + 2 * here
            g = t - lag
            first, last = (self.split, self.groups) if light else (0, self.split)

            @pl.when((here > 0) & (g >= first) & (g < last))
            def _(light=light, g=g):
                loop(here, self.planes, lambda reach: action(g, way, reach, light))

    def chain_arrive(self, g, way, reach, light):
        self.chain(g, way, reach, light).wait_recv()
        self.chain_load(g, way, reach, light).start()

    def chain_pass(self, g, way, reach, light):
        here = self.z if way == 0 else self.planes - 1 - self.z
        slot, plane = lax.rem(g, COLUMN_SLOTS), self.plane_at(way, reach)
        self.chain_load(g, way, reach, light).wait()
        if light:
            for half in range(2):
                self.column[slot, plane, half, 0] = (
                    self.column[slot, plane, half, 0] + self.light_in[way, reach - 1, half]
                )
        else:
            self.column[slot, plane] = self.column[slot, plane] + self.chain_in[way, reach - 1]

        @pl.when(reach > here)
        def _():
            self.chain(g, way, reach, light).start()

    def start_chains(self, g, light):
        for way in range(2):

            @pl.when(self.z == (0 if way == 0 else self.planes - 1))
            def _(way=way):
                loop(1, self.planes, lambda reach: self.chain(g, way, reach, light).start())

    def enter_line(self, g):
        slot, spot = lax.rem(g, GRAD_SLOTS), lax.rem(g, COLUMN_SLOTS)
        self.load(g, 1).wait()
        for half in range(2):
            wide, narrow = self.place.bits(half)
            first = self.place.core * 4 + wide * 2
            for b in range(2):
                total = self.made[slot, half, first + b] + self.wide_in[half, b]
                for plane in range(self.planes):
                    self.column[spot, plane, half, b] = total[plane]

        @pl.when(g < self.split)
        def _():
            self.start_chains(g, False)

        @pl.when(g >= self.split)
        def _():
            for half in range(2):
                self.planar(g, half, 1, True).start()

    def enter_light(self, g):
        slot = lax.rem(g, COLUMN_SLOTS)
        for half in range(2):
            wide, narrow = self.place.bits(half)
            self.planar(g, half, 1, True).wait()

            def one(plane, half=half, narrow=narrow):
                self.column[slot, plane, half, 0] = (
                    self.column[slot, plane, half, narrow]
                    + self.narrow_all[g - self.split, half, plane]
                )

            loop(0, self.planes, one)
        self.start_chains(g, True)

    def finish_light(self, g):
        slot = lax.rem(g, COLUMN_SLOTS)
        for half in range(2):
            self.sums_ref[g, half] = self.column[slot, self.z, half, 0]

    def finish(self, g):
        for half in range(2):
            wide, narrow = self.place.bits(half)
            self.planar(g, half, 1).wait_recv()
            own = self.column[lax.rem(g, COLUMN_SLOTS), self.z, half, narrow].astype(F32)
            self.sums_ref[g, half] = (own + self.narrow_in[g, half].astype(F32)).astype(BF16)

    def arrive(self, g, order):
        if order == 0:
            self.to_sibling(g).wait_recv()
        else:
            for half in range(2):
                self.planar(g, half, 0).wait_recv()
        self.load(g, order).start()

    def add(self, g):
        slot = lax.rem(g, GRAD_SLOTS)
        self.load(g, 0).wait()
        first = self.place.core * 4
        for half in range(2):
            for b in range(4):
                self.made[slot, half, first + b] = (
                    self.made[slot, half, first + b] + self.theirs[half, b]
                )
            self.planar(g, half, 0).start()

    def leave_line(self, g):
        for half in range(2):
            self.planar(g, half, 1).start()

    def wait_column_sends(self, g, light=False):
        if not light:
            for half in range(2):
                self.planar(g, half, 1).wait_send()
        for way in range(2):
            here = self.z if way == 0 else self.planes - 1 - self.z
            loop(here + 1, self.planes, lambda reach: self.chain(g, way, reach, light).wait_send())

    def wait_made_sends(self, g):
        self.to_sibling(g).wait_send()
        for half in range(2):
            self.planar(g, half, 0).wait_send()

    def during(self, t, lag, action, first=0, last=None):
        g = t - lag

        @pl.when((g >= first) & (g < (self.groups if last is None else last)))
        def _():
            action(g)

    def receive(self, t):
        self.during(t, 1, lambda g: self.arrive(g, 0))
        self.during(t, self.enter, lambda g: self.arrive(g, 1))
        for way in range(2):
            self.chain_of(t, way, self.chain_arrive)
        self.during(t, self.last, self.finish, 0, self.split)

        @pl.when((t >= GRAD_SLOTS) & (t < self.groups))
        def _():
            self.wait_made_sends(t - GRAD_SLOTS)

    def advance(self, t):
        self.during(t, 0, lambda g: self.to_sibling(g).start())
        for way in range(2):
            self.chain_of(t, way, self.chain_pass)
        self.during(t, self.leave, self.leave_line, 0, self.split)
        self.during(t, self.light_enter + self.planes, self.finish_light, self.split)
        self.during(t, self.light_enter, self.enter_light, self.split)

        @pl.when((t >= self.enter + COLUMN_SLOTS) & (t < self.enter + self.groups))
        def _():
            self.wait_column_sends(t - self.enter - COLUMN_SLOTS)

        self.during(t, self.enter, self.enter_line)
        self.during(t, 1, self.add)

    def drain(self):
        loop(self.groups - GRAD_SLOTS, self.groups, self.wait_made_sends)
        loop(self.groups - COLUMN_SLOTS, self.split, self.wait_column_sends)
        loop(self.split, self.groups, lambda g: self.wait_column_sends(g, True))


BACKWARD_READS = (12, 8, 13, 9, 14, 10, 15, 11, 7, 6, 3, 4, 5, 0, 1, 2)
READ_SLOTS = 3


def backward_kernel(
    seqs,
    planes,
    window_ref,
    length_ref,
    group_ref,
    unit_ref,
    whole_ref,
    slope_ref,
    cotangent_ref,
    tokens_ref,
    x2_ref,
    x3_ref,
    h1_ref,
    h2_ref,
    h3_ref,
    act_ref,
    crossed_ref,
    cq_ref,
    mem_ref,
    cross_log_ref,
    joined_ref,
    attended_ref,
    qkv_all,
    log_ref,
    memory_ref,
    vectors_ref,
    theirs_far,
    wide_far,
    chain_far,
    slots_ref,
    grad_tokens_ref,
    grad_memory_ref,
    vec_sum_ref,
    sums_ref,
    vec_ref,
    vec_part,
    vec_came,
    vec_planes,
    made,
    theirs,
    wide_in,
    narrow_in,
    narrow_all,
    column,
    chain_in,
    light_in,
    weights,
    dx,
    dh,
    du,
    dx3_low,
    dx2_low,
    dco,
    dcq,
    mem_parts,
    mem_theirs,
    mem_came,
    mem_low,
    do_all,
    delta,
    dq_total,
    dk_total,
    dv_total,
    dq_low,
    dk_low,
    dv_low,
    dq_back,
    dk_back,
    dv_back,
    load_sem,
    chain_sem,
    c_send,
    c_recv,
    p_send,
    p_recv,
    z_send,
    z_recv,
    read_sem,
    slope_sem,
    fold_send,
    fold_recv,
    mem_send,
    mem_recv,
    do_send,
    do_recv,
    back_send,
    back_recv,
    vec_send,
    vec_recv,
    across_send,
    across_recv,
    slot_send,
    slot_recv,
    own_sem,
):
    reduce = Reduce(
        planes,
        made,
        theirs_far,
        wide_far,
        chain_far,
        sums_ref,
        theirs,
        wide_in,
        narrow_in,
        narrow_all,
        column,
        chain_in,
        light_in,
        load_sem,
        chain_sem,
        c_send,
        c_recv,
        p_send,
        p_recv,
        z_send,
        z_recv,
    )
    place = reduce.place
    me, z = place.seq, place.z
    rows = tokens_ref.shape[0]
    width = D // seqs
    tile = 2 * LANES
    head_count = width // HDIM
    mem_rows = mem_ref.shape[1] // seqs
    padded = memory_ref.shape[0]
    ups = FF // D

    total = seqs * planes
    here = me * planes + z

    def read(k):
        slot = k % READ_SLOTS
        return pltpu.make_async_copy(
            whole_ref.at[BACKWARD_READS[k]], weights.at[slot], read_sem.at[slot]
        )

    def using(k, work):
        read(k).wait()
        work(k % READ_SLOTS)
        if k + READ_SLOTS < len(BACKWARD_READS):
            read(k + READ_SLOTS).start()

    greet_all(here, total, lambda j: (lax.div(j, planes), lax.rem(j, planes)))

    slope_copy = pltpu.make_async_copy(slope_ref, du, slope_sem)
    slope_copy.start()
    for k in range(READ_SLOTS):
        read(k).start()

    def columns_of(j, count=tile):
        return pl.ds(pl.multiple_of(j * count, count), count)

    def vector(index):
        return vectors_ref[index : index + 1]

    def row_sum(values):
        return jnp.sum(values.astype(F32), axis=0, keepdims=True)

    def norm_back(stream_ref, gain_row, base, out_ref, low_ref):
        gain = vector(gain_row)
        part = rows // 4

        def one(block, sums):
            span = pl.ds(pl.multiple_of(block * part, part), part)
            _, form, inverse = norm_forward(stream_ref[span].astype(F32), 1.0, 0.0)
            upstream = dh[span]
            scaled = upstream * gain
            first = jnp.mean(scaled, axis=-1, keepdims=True)
            second = jnp.mean(scaled * form, axis=-1, keepdims=True)
            total = base(span) + inverse * (scaled - first - form * second)
            out_ref[span] = total
            gains, shifts, lows = sums
            if low_ref is not None:
                low = total.astype(BF16)
                low_ref[span] = low
                lows = lows + row_sum(low)
            return (gains + row_sum(upstream * form), shifts + row_sum(upstream), lows)

        zero = jnp.zeros((1, D), F32)
        gains, shifts, lows = lax.fori_loop(0, 4, one, (zero, zero, zero))
        vec_ref[gain_row : gain_row + 1] = gains
        vec_ref[gain_row + 1 : gain_row + 2] = shifts
        return lows

    def grad_matrix(slot, left_ref, first_column, right_ref):
        def one(r):
            first = first_column + r * tile
            left = left_ref[:, pl.ds(pl.multiple_of(first, tile), tile)]
            block = made.shape[5]
            for c in range(2):
                columns = slice(c * (D // 2), (c + 1) * (D // 2))
                result = dot_tn(left, right_ref[:, columns]).astype(BF16)
                for part in range(tile // block):
                    for b in range(D // 2 // LANES):
                        made[slot, part // planes, c * 4 + b, part % planes, r] = result[
                            part * block : (part + 1) * block, b * LANES : (b + 1) * LANES
                        ]

        def two(pair):
            one(2 * pair)
            one(2 * pair + 1)

        loop(0, GROUP_UNITS // 2, two)

    def hidden_back(j):
        if j == 0:
            dh[...] = jnp.zeros_like(dh)
            slope_copy.wait()
            vec_ref[...] = jnp.zeros_like(vec_ref)

        def slopes(slot):
            def emit(r, result):
                spread = pl.ds(pl.multiple_of(j * D + r * tile, tile), tile)
                low = (result * du[:, spread].astype(F32)).astype(BF16)
                du[:, spread] = low
                vec_ref[12 + j : 13 + j, columns_of(r)] = row_sum(low)

            dot_tiles(cotangent_ref[...], weights, slot, emit, turned=True, unrolled=True)

        def inner(slot):
            def emit(r, result):
                dh[:, columns_of(r)] = dh[:, columns_of(r)] + result

            dot_tiles(du[:, j * D : (j + 1) * D], weights, slot, emit, unrolled=True)

        using(2 * j, slopes)
        using(2 * j + 1, inner)

    def mem_fold():
        return remote(
            mem_parts.at[1 - place.core],
            mem_theirs,
            fold_send,
            fold_recv,
            place.sibling(),
        )

    chip = lax.div(me, 2)
    chips = seqs // 2

    def mem_copy(peer, slot):
        return remote(
            mem_parts.at[place.core, peer],
            mem_came.at[slot],
            mem_send.at[peer],
            mem_recv.at[slot],
            (2 * peer + place.core, z),
        )

    def cross_branch():
        vec_ref[12 + ups : 13 + ups] = row_sum(cotangent_ref[...])
        vec_ref[11:12] = norm_back(
            x3_ref, 4, lambda span: cotangent_ref[span].astype(F32), dx, dx3_low
        )

        def branch(slot):
            def emit(r, result):
                dco[:, columns_of(r)] = result.astype(BF16)

            dot_tiles(dx3_low[...], weights, slot, emit, turned=True, unrolled=True)

        using(8, branch)

    def cross_back(first, last):
        def one(j, carry):
            columns = columns_of(j, LANES)
            dq, dk, dv = cross_grads(
                length_ref[0],
                cq_ref[:, columns],
                mem_ref[0, :, columns],
                mem_ref[1, :, columns],
                dco[:, columns],
                crossed_ref[:, columns],
                [cross_log_ref[j, h : h + 1] for h in range(LANES // HDIM)],
            )
            dcq[:, columns] = dq.astype(BF16)
            fill = jnp.zeros((max(padded - mem_rows, 1), LANES), F32)
            for peer in range(seqs):
                span = slice(peer * mem_rows, (peer + 1) * mem_rows)
                for part, values in enumerate((dk, dv)):
                    block = values[span]
                    if padded > mem_rows:
                        block = jnp.concatenate([block, fill], axis=0)
                    mem_parts[peer % 2, peer // 2, part, :, columns] = block.astype(BF16)
            return carry

        lax.fori_loop(first, last, one, 0)

    def memory_send():
        mem_fold().wait()

        def send(step):
            peer = lax.rem(chip + step, chips)
            mem_parts[place.core, peer] = mem_parts[place.core, peer] + mem_theirs[peer]

            @pl.when(step < chips)
            def _():
                mem_copy(peer, chip).start()

            @pl.when(step == chips)
            def _():
                mem_came[chip] = mem_parts[place.core, peer]

        loop(1, chips + 1, send)

    def do_copy(peer, slot):
        return remote(
            dq_low.at[peer], do_all.at[slot], do_send.at[peer], do_recv.at[slot], (peer, z)
        )

    def before_self():
        def inner(slot):
            def emit(r, result):
                dh[:, columns_of(r)] = result

            dot_tiles(dcq[...], weights, slot, emit, turned=True, unrolled=True)

        using(9, inner)
        vec_ref[9:10] = row_sum(dcq[...])
        vec_ref[8:9] = norm_back(x2_ref, 2, lambda span: dx[span], dx, dx2_low)

        def branch(slot):
            def emit(r, result):
                low = result.astype(BF16)
                for piece in range(tile // width):
                    dq_low[r * (tile // width) + piece] = low[
                        :, piece * width : (piece + 1) * width
                    ]

            dot_tiles(dx2_low[...], weights, slot, emit, turned=True, unrolled=True)

        using(10, branch)

        def send(step, carry):
            do_copy(lax.rem(me + step, seqs), me).start()
            return carry

        lax.fori_loop(1, seqs, send, 0)
        do_all[me] = dq_low[me]

    def memory_back():
        def arrive(step):
            peer = lax.rem(chip + step, chips)
            mem_copy(peer, peer).wait_recv()

        loop(1, chips, arrive)
        for part in range(2):
            part_sum = mem_came[0, part].astype(F32)
            for j in range(1, chips):
                part_sum = part_sum + mem_came[j, part].astype(F32)
            mem_low[part] = part_sum.astype(BF16)
        vec_ref[10:11] = row_sum(mem_low[1])

        def keys(slot):
            def emit(r, result):
                grad_memory_ref[:, columns_of(r)] = result

            dot_tiles(mem_low[0], weights, slot, emit, turned=True, unrolled=True)

        def values(slot):
            def emit(r, result):
                grad_memory_ref[:, columns_of(r)] = grad_memory_ref[:, columns_of(r)] + result

            dot_tiles(mem_low[1], weights, slot, emit, turned=True, unrolled=True)

        using(11, keys)
        using(12, values)

    window = window_ref[0]
    outputs = ((dq_low, dq_back), (dk_low, dk_back), (dv_low, dv_back))

    def returned(peer, slot, part):
        src, dst = outputs[part]
        return remote(
            src.at[peer],
            dst.at[:, pl.ds(pl.multiple_of(slot * width, width), width)],
            back_send.at[part, peer],
            back_recv.at[part, slot],
            (peer, z),
        )

    def prepare():
        def one(i, carry):
            @pl.when(i != me)
            def _():
                do_copy(i, i).wait_recv()

            sums = head_sums(do_all[i].astype(F32) * attended_ref[i].astype(F32), head_count)
            for head in range(head_count):
                delta[i, head : head + 1] = sums[head]
            for total in (dq_total, dk_total, dv_total):
                total[i] = jnp.zeros((rows, width), F32)
            return carry

        lax.fori_loop(0, seqs, one, 0)

    span_rows = 2 * rows
    stacked_queries = head_count * span_rows

    def tile_grads(p):
        level = (
            jnp.where(p >= 2, 1, 0) + jnp.where(p >= 6, 1, 0) + jnp.where(p >= 12, 1, 0)
        ).astype(jnp.int32)
        rank = p - level * (level + 1)
        second = jnp.where(rank > level, 1, 0).astype(jnp.int32)
        b = seqs - 1 - 2 * level - second
        q2 = seqs // 2 - 1 - level + rank - second * (level + 1)
        pair = pl.ds(pl.multiple_of(q2 * 2, 2), 2)
        keys, values = qkv_all[1, b], qkv_all[2, b]
        scaled = qkv_all[0, pair].reshape(span_rows, width) * jnp.asarray(HDIM**-0.5, BF16)
        grads = do_all[pair].reshape(span_rows, width)
        queries = jnp.concatenate([only_head(scaled, h, head_count) for h in range(head_count)], 0)
        uppers = jnp.concatenate([only_head(grads, h, head_count) for h in range(head_count)], 0)

        def row_of(ref):
            return jnp.concatenate(
                [ref[q2 * 2 + k, h : h + 1] for h in range(head_count) for k in range(2)], 1
            )

        logs, deltas = row_of(log_ref), row_of(delta)
        shape = (rows, stacked_queries)
        key_row = lax.broadcasted_iota(jnp.int32, shape, 0)
        query_row = lax.rem(lax.broadcasted_iota(jnp.int32, (1, stacked_queries), 1), span_rows)
        reach = query_row + (q2 * 2 - b) * rows

        def work(diagonal):
            scores = dot_nt(keys, queries)
            allowed = key_row <= reach if diagonal else key_row > reach - window
            probs = jnp.exp(jnp.where(allowed, scores, NEG_FILL) - logs)
            grad_scores = (probs * (dot_nt(values, uppers) - deltas)).astype(BF16)
            dv_total[b] = dv_total[b] + dot_nn(probs.astype(BF16), uppers)
            dk_total[b] = dk_total[b] + dot_nn(grad_scores, queries)
            spread = dot_tn(grad_scores, keys)
            part = spread[:span_rows]
            lane = lax.broadcasted_iota(jnp.int32, part.shape, 1)
            for h in range(1, head_count):
                part = jnp.where(
                    lane >= h * HDIM, spread[h * span_rows : (h + 1) * span_rows], part
                )
            dq_total[pair] = dq_total[pair] + part.reshape(2, rows, width)

        diagonal = lax.div(b, 2) == q2

        @pl.when(diagonal)
        def _():
            work(True)

        @pl.when(jnp.logical_not(diagonal))
        def _():
            work(False)

        @pl.when(q2 == seqs // 2 - 1)
        def _():
            dk_low[b] = dk_total[b].astype(BF16)
            dv_low[b] = dv_total[b].astype(BF16)
            send_back(b, 1)
            send_back(b, 2)

    def send_back(i, part):
        low, rows_ref = outputs[part]

        @pl.when(i != me)
        def _():
            returned(i, me, part).start()

        @pl.when(i == me)
        def _():
            rows_ref[:, pl.ds(pl.multiple_of(i * width, width), width)] = low[i]

    def close_self():
        loop(1, seqs, lambda step: do_copy(lax.rem(me + step, seqs), me).wait_send())

        def one(i):
            dq_low[i] = (dq_total[i] * HDIM**-0.5).astype(BF16)
            send_back(i, 0)

        loop(0, seqs, one)

    def first_arrive():
        def arrive(step, carry):
            peer = lax.rem(me + step, seqs)
            for part in range(3):
                returned(peer, peer, part).wait_recv()
            return carry

        lax.fori_loop(1, seqs, arrive, 0)

    def first_back():
        for part in range(3):

            def inner(slot, part=part):
                def emit(r, result):
                    if part == 0:
                        dh[:, columns_of(r)] = result
                    else:
                        dh[:, columns_of(r)] = dh[:, columns_of(r)] + result

                dot_tiles(rows_of_part[part][...], weights, slot, emit, turned=True, unrolled=True)

            using(13 + part, inner)
        vec_ref[6:7] = row_sum(rows_of_part[0][...])
        vec_ref[7:8] = row_sum(rows_of_part[2][...])
        norm_back(tokens_ref, 0, lambda span: dx[span], grad_tokens_ref, None)

    rows_of_part = (dq_back, dk_back, dv_back)

    def fold_copy(order):
        target = (place.sibling(), place.x_peer(), place.y_peer())[order]
        return remote(
            vec_part.at[order],
            vec_came.at[order],
            vec_send.at[order],
            vec_recv.at[order],
            target,
        )

    def across_copy(peer, slot):
        return remote(
            vec_planes.at[slot],
            vec_planes.at[slot],
            across_send.at[peer],
            across_recv.at[slot],
            (me, peer),
        )

    def fold_vectors(order):
        if order == 0:
            vec_part[0] = vec_ref[...]
        else:
            fold_copy(order - 1).wait()
            folded = vec_part[order - 1] + vec_came[order - 1]
            if order < 3:
                vec_part[order] = folded
            else:
                vec_planes[z] = folded
        if order < 3:
            fold_copy(order).start()
        else:

            def send(step, carry):
                across_copy(lax.rem(z + step, planes), z).start()
                return carry

            lax.fori_loop(1, planes, send, 0)

    def close_vectors():
        def arrive(step, carry):
            peer = lax.rem(z + step, planes)
            across_copy(peer, peer).wait()
            return carry

        lax.fori_loop(1, planes, arrive, 0)
        vector_sum = vec_planes[0]
        for plane in range(1, planes):
            vector_sum = vector_sum + vec_planes[plane]
        vec_sum_ref[...] = vector_sum

    slot_count = slots_ref.shape[0]

    def slot_copy(peer, holder, half):
        slot_rows, slot_columns = tile_of(holder, planes, half, slots_ref.shape[1])
        return remote(
            made.at[0, half, lax.div(peer, planes), lax.rem(peer, planes), pl.ds(0, slot_count)],
            slots_ref.at[:, slot_rows, slot_columns],
            slot_send.at[peer, half],
            slot_recv.at[holder, half],
            (lax.div(peer, planes), lax.rem(peer, planes)),
        )

    def return_tiles():
        def fill(peer):
            for s in range(slot_count):
                group, unit = group_ref[peer * slot_count + s], unit_ref[peer * slot_count + s]
                for half in range(2):
                    block = sums_ref[jnp.maximum(group, 0), half, unit]
                    made[0, half, lax.div(peer, planes), lax.rem(peer, planes), s] = jnp.where(
                        group >= 0, block, jnp.zeros_like(block)
                    )

        def start(step, carry):
            peer = lax.rem(here + step, total)
            fill(peer)
            for half in range(2):
                slot_copy(peer, here, half).start()
            return carry

        lax.fori_loop(1, total, start, 0)
        fill(here)
        own = []
        for half in range(2):
            slot_rows, slot_columns = tile_of(here, planes, half, slots_ref.shape[1])
            own.append(
                pltpu.make_async_copy(
                    made.at[0, half, lax.div(here, planes), lax.rem(here, planes), pl.ds(0, slot_count)],
                    slots_ref.at[:, slot_rows, slot_columns],
                    own_sem.at[half],
                )
            )
            own[half].start()
        for copy in own:
            copy.wait()

        def finish_slots(step, carry):
            peer = lax.rem(here + total - step, total)
            for half in range(2):
                slot_copy(peer, peer, half).wait()
            return carry

        lax.fori_loop(1, total, finish_slots, 0)

    def tick(t, carry):
        reduce.receive(t)

        slot = lax.rem(t, GRAD_SLOTS)

        @pl.when(t < ups)
        def _():
            grad_matrix(slot, act_ref, t * D, cotangent_ref)

        @pl.when((t >= ups) & (t < 2 * ups))
        def _():
            grad_matrix(slot, du, (t - ups) * D, h3_ref)

        late = 2 * ups
        pieces = (
            (crossed_ref, dx3_low),
            (h2_ref, dcq),
            (joined_ref, dx2_low),
            (memory_ref, mem_low.at[0]),
            (memory_ref, mem_low.at[1]),
        )
        for step, (left, right) in enumerate(pieces):

            @pl.when(t == late + step)
            def _(left=left, right=right):
                grad_matrix(slot, left, 0, right)

        last = late + len(pieces)

        @pl.when(t == last)
        def _():
            first_arrive()

        for part in range(3):

            @pl.when(t == last + part)
            def _(part=part):
                grad_matrix(slot, h1_ref, 0, rows_of_part[part])

        reduce.advance(t)

        def at(step, work):
            @pl.when(t == step)
            def _():
                work()

        for j in range(ups):
            at(1 + (j + 1) // 2, functools.partial(hidden_back, j))
        at(3, cross_branch)
        blocks = D // LANES
        at(4, functools.partial(cross_back, 0, blocks // 2))
        at(5, functools.partial(cross_back, blocks // 2, blocks))
        at(5, lambda: mem_fold().start())
        at(6, memory_send)
        at(6, before_self)
        at(7, prepare)

        @pl.when((t >= 7) & (t < 13))
        def _():
            loop(lax.div(10 * (t - 7), 3), lax.div(10 * (t - 6), 3), tile_grads)

        at(10, memory_back)
        at(12, close_self)
        at(last + 3, first_back)
        for order in range(4):
            at(last + 4 + order, functools.partial(fold_vectors, order))
        at(last + 9, close_vectors)
        return carry

    lax.fori_loop(0, reduce.groups + reduce.last, tick, 0)

    def finish(step, carry):
        peer = lax.rem(me + step, seqs)
        for part in range(3):
            returned(peer, me, part).wait_send()
        return carry

    lax.fori_loop(1, seqs, finish, 0)
    loop(1, chips, lambda step: mem_copy(lax.rem(chip + step, chips), chip).wait_send())
    reduce.drain()
    return_tiles()


def backward_pass(seqs, planes, windows, lengths, group, unit, whole, slope, arrays):
    groups, matrix = whole.shape[0], whole.shape[1:]
    column = matrix[2:]
    block = matrix[3:]
    cotangent, memory = arrays[0], arrays[-2]
    total = seqs * planes
    slots, unit_rows = group.shape[0] // total, 2 * planes * block[1]
    rows = cotangent.shape[0]
    width = D // seqs
    padded = memory.shape[0]
    dma = pltpu.SemaphoreType.DMA
    vmem = pl.BlockSpec(memory_space=pltpu.VMEM)
    smem = pl.BlockSpec(memory_space=pltpu.SMEM)
    anywhere = pl.BlockSpec(memory_space=pl.ANY)
    shape = jax.ShapeDtypeStruct
    by_head = (seqs, rows, width)
    outs = pl.pallas_call(
        functools.partial(backward_kernel, seqs, planes),
        out_shape=(
            shape((groups, 2, 4) + column, BF16),
            shape((groups, 2, 2) + column, BF16),
            shape((groups, 2, planes - 1, 2, 2) + block, BF16),
            shape((slots, unit_rows, D), BF16),
            shape((rows, D), F32),
            shape((padded, D), F32),
            shape((24, D), F32),
        ),
        in_specs=[smem] * 4 + [anywhere, anywhere] + [vmem] * len(arrays),
        out_specs=(anywhere, anywhere, anywhere, anywhere, vmem, vmem, vmem),
        scratch_shapes=[
            pltpu.VMEM((groups, 2) + block, BF16),
            pltpu.VMEM((24, D), F32),
            pltpu.VMEM((3, 24, D), F32),
            pltpu.VMEM((3, 24, D), F32),
            pltpu.VMEM((planes, 24, D), F32),
            pltpu.VMEM((GRAD_SLOTS,) + matrix, BF16),
            pltpu.VMEM((2, 4) + column, BF16),
            pltpu.VMEM((2, 2) + column, BF16),
            pltpu.VMEM((groups, 2) + block, BF16),
            pltpu.VMEM((REDUCE_LIGHT, 2) + column, BF16),
            pltpu.VMEM((COLUMN_SLOTS, planes, 2, 2) + block, BF16),
            pltpu.VMEM((2, planes - 1, 2, 2) + block, BF16),
            pltpu.VMEM((2, planes - 1, 2) + block, BF16),
            pltpu.VMEM((READ_SLOTS,) + matrix, BF16),
            pltpu.VMEM((rows, D), F32),
            pltpu.VMEM((rows, D), F32),
            pltpu.VMEM((rows, FF), BF16),
            pltpu.VMEM((rows, D), BF16),
            pltpu.VMEM((rows, D), BF16),
            pltpu.VMEM((rows, D), BF16),
            pltpu.VMEM((rows, D), BF16),
            pltpu.VMEM((2, seqs // 2, 2, padded, D), BF16),
            pltpu.VMEM((seqs // 2, 2, padded, D), BF16),
            pltpu.VMEM((seqs // 2, 2, padded, D), BF16),
            pltpu.VMEM((2, padded, D), BF16),
            pltpu.VMEM(by_head, BF16),
            pltpu.VMEM((seqs, 8, rows), F32),
            pltpu.VMEM(by_head, F32),
            pltpu.VMEM(by_head, F32),
            pltpu.VMEM(by_head, F32),
            pltpu.VMEM(by_head, BF16),
            pltpu.VMEM(by_head, BF16),
            pltpu.VMEM(by_head, BF16),
            pltpu.VMEM((rows, D), BF16),
            pltpu.VMEM((rows, D), BF16),
            pltpu.VMEM((rows, D), BF16),
            dma((2,)),
            dma((2, 2, planes - 1)),
            dma((groups,)),
            dma((groups,)),
            dma((groups, 2, 2)),
            dma((groups, 2, 2)),
            dma((groups, 2, planes - 1)),
            dma((groups, 2, planes - 1)),
            dma((READ_SLOTS,)),
            dma(()),
            dma(()),
            dma(()),
            dma((seqs // 2,)),
            dma((seqs // 2,)),
            dma((seqs,)),
            dma((seqs,)),
            dma((3, seqs)),
            dma((3, seqs)),
            dma((3,)),
            dma((3,)),
            dma((planes,)),
            dma((planes,)),
            dma((total, 2)),
            dma((total, 2)),
            dma((2,)),
        ],
        compiler_params=pltpu.CompilerParams(
            collective_id=3,
            has_side_effects=True,
            vmem_limit_bytes=60 * MIB,
        ),
        name="backward_pass",
    )(windows, lengths, group, unit, whole, slope, *arrays)
    return outs[3:]


def dot_nt(left, right):
    return lax.dot_general(left, right, (((1,), (1,)), ((), ())), preferred_element_type=F32)


def dot_tn(left, right):
    return lax.dot_general(left, right, (((0,), (0,)), ((), ())), preferred_element_type=F32)


def dot_nn(left, right):
    return lax.dot_general(left, right, (((1,), (0,)), ((), ())), preferred_element_type=F32)


def only_head(values, head, head_count):
    if head_count == 1:
        return values
    lane = lax.broadcasted_iota(jnp.int32, values.shape, 1)
    inside = (lane >= head * HDIM) & (lane < (head + 1) * HDIM)
    return jnp.where(inside, values, jnp.zeros_like(values))


def stacked_heads(parts):
    whole = parts[0]
    row = lax.broadcasted_iota(jnp.int32, whole.shape, 0)
    for head in range(1, len(parts)):
        whole = jnp.where(row >= head * HDIM, parts[head], whole)
    return whole


def head_sums(values, head_count):
    turned = values.T
    return [
        jnp.sum(turned[head * HDIM : (head + 1) * HDIM], axis=0, keepdims=True)
        for head in range(head_count)
    ]


def attend_block(i, rows, head_count, offset, window, q_all, k_all, v_all, log_ref):
    scaled = q_all[i] * jnp.asarray(HDIM**-0.5, BF16)
    queries = [only_head(scaled, head, head_count) for head in range(head_count)]
    state = []
    for head in range(head_count):
        scores = dot_nt(k_all[i], queries[head])
        scores = jnp.where((offset <= 0) & (offset > -window), scores, NEG_FILL)
        best = jnp.max(scores, axis=0, keepdims=True)
        probs = jnp.exp(scores - best)
        state.append(
            (best, jnp.sum(probs, axis=0, keepdims=True), dot_tn(v_all[i], probs.astype(BF16)))
        )

    def key_block(b, running):
        keys, values = k_all[b], v_all[b]
        limit = (i - b) * rows - window
        renewed = []
        for head in range(head_count):
            best, total, gathered = running[head]
            scores = jnp.where(offset > limit, dot_nt(keys, queries[head]), NEG_FILL)
            new_best = jnp.maximum(best, jnp.max(scores, axis=0, keepdims=True))
            probs = jnp.exp(scores - new_best)
            keep = jnp.exp(best - new_best)
            renewed.append(
                (
                    new_best,
                    total * keep + jnp.sum(probs, axis=0, keepdims=True),
                    gathered * keep + dot_tn(values, probs.astype(BF16)),
                )
            )
        return tuple(renewed)

    state = lax.fori_loop(0, i, key_block, tuple(state))
    for head in range(head_count):
        best, total, _ = state[head]
        log_ref[i, head : head + 1] = best + jnp.log(total)
    return stacked_heads([gathered / total for _, total, gathered in state]).T


def attend_pairs(i, rows, head_count, window, qkv_all, log_ref):
    width = qkv_all.shape[3]
    scaled = qkv_all[0, i] * jnp.asarray(HDIM**-0.5, BF16)
    queries = jnp.concatenate([only_head(scaled, head, head_count) for head in range(head_count)], 0)
    columns = head_count * rows
    key_row = lax.broadcasted_iota(jnp.int32, (2 * rows, columns), 0)
    query_row = lax.rem(lax.broadcasted_iota(jnp.int32, (1, columns), 1), rows)
    last = lax.div(i, 2)

    def two_blocks(part, m):
        return qkv_all[part, pl.ds(pl.multiple_of(2 * m, 2), 2)].reshape(2 * rows, width)

    def one(step, running):
        m = last - step
        best, total, gathered = running
        reach = query_row + (i - 2 * m) * rows
        allowed = (key_row <= reach) & (key_row > reach - window)
        scores = jnp.where(allowed, dot_nt(two_blocks(1, m), queries), NEG_FILL)
        new_best = jnp.maximum(best, jnp.max(scores, axis=0, keepdims=True))
        probs = jnp.exp(scores - new_best)
        keep = jnp.exp(best - new_best)
        return (
            new_best,
            total * keep + jnp.sum(probs, axis=0, keepdims=True),
            gathered * keep + dot_tn(two_blocks(2, m), probs.astype(BF16)),
        )

    best, total, gathered = lax.fori_loop(
        0,
        last + 1,
        one,
        (
            jnp.full((1, columns), NEG_FILL, F32),
            jnp.zeros((1, columns), F32),
            jnp.zeros((width, columns), F32),
        ),
    )
    logs = best + jnp.log(total)
    gathered = gathered / total
    for head in range(head_count):
        log_ref[i, head : head + 1] = logs[:, head * rows : (head + 1) * rows]
    return stacked_heads(
        [gathered[:, head * rows : (head + 1) * rows] for head in range(head_count)]
    ).T


def cross_attend(length, query, keys, values):
    head_count = LANES // HDIM
    rows = query.shape[0]
    scaled = query * jnp.asarray(HDIM**-0.5, BF16)
    queries = jnp.concatenate([only_head(scaled, head, head_count) for head in range(head_count)], 0)
    scores = dot_nt(keys, queries)
    allowed = lax.broadcasted_iota(jnp.int32, scores.shape, 0) < length
    scores = jnp.where(allowed, scores, NEG_FILL)
    best = jnp.max(scores, axis=0, keepdims=True)
    probs = jnp.exp(scores - best)
    total = jnp.sum(probs, axis=0, keepdims=True)
    gathered = dot_tn(values, probs.astype(BF16)) / total
    logs = best + jnp.log(total)
    spans = [slice(head * rows, (head + 1) * rows) for head in range(head_count)]
    crossed = stacked_heads([gathered[:, span] for span in spans]).T
    return crossed, [logs[:, span] for span in spans]


def self_forward_kernel(
    seqs,
    window_ref,
    q_ref,
    k_ref,
    v_ref,
    joined_ref,
    q_all,
    k_all,
    v_all,
    attended_ref,
    log_ref,
    rounded,
    send_sem,
    recv_sem,
    back_send,
    back_recv,
):
    me, z = lax.axis_index("seq"), lax.axis_index("grp")
    rows, width = q_ref.shape[1], q_ref.shape[2]
    head_count = width // HDIM
    greet_all(me, seqs, lambda j: (j, z))
    pairs = ((q_ref, q_all), (k_ref, k_all), (v_ref, v_all))

    def outward(peer, slot, part):
        src, dst = pairs[part]
        return remote(
            src.at[peer], dst.at[slot], send_sem.at[part, peer], recv_sem.at[part, slot], (peer, z)
        )

    def start(step, carry):
        peer = lax.rem(me + step, seqs)
        for part in range(3):
            outward(peer, me, part).start()
        return carry

    lax.fori_loop(1, seqs, start, 0)
    for src, dst in pairs:
        dst[me] = src[me]
    window = window_ref[0]
    offset = lax.broadcasted_iota(jnp.int32, (rows, rows), 0) - lax.broadcasted_iota(
        jnp.int32, (rows, rows), 1
    )

    def backward_copy(peer, slot):
        return remote(
            rounded.at[peer], joined_ref.at[slot], back_send.at[peer], back_recv.at[slot], (peer, z)
        )

    def query_block(i, carry):
        @pl.when(i != me)
        def _():
            for part in range(3):
                outward(i, i, part).wait_recv()

        attended = attend_block(i, rows, head_count, offset, window, q_all, k_all, v_all, log_ref)
        attended_ref[i] = attended
        rounded[i] = attended.astype(BF16)

        @pl.when(i != me)
        def _():
            backward_copy(i, me).start()

        @pl.when(i == me)
        def _():
            joined_ref[i] = rounded[i]

        return carry

    lax.fori_loop(0, seqs, query_block, 0)

    def finish(step, carry):
        peer = lax.rem(me + step, seqs)
        for part in range(3):
            outward(peer, me, part).wait_send()
        backward_copy(peer, peer).wait()
        return carry

    lax.fori_loop(1, seqs, finish, 0)


def self_forward(seqs, windows, query, key, value):
    shape = query.shape
    head_count = shape[2] // HDIM
    dma = pltpu.SemaphoreType.DMA
    vmem = pl.BlockSpec(memory_space=pltpu.VMEM)
    return pl.pallas_call(
        functools.partial(self_forward_kernel, seqs),
        out_shape=(
            jax.ShapeDtypeStruct(shape, BF16),
            jax.ShapeDtypeStruct(shape, BF16),
            jax.ShapeDtypeStruct(shape, BF16),
            jax.ShapeDtypeStruct(shape, BF16),
            jax.ShapeDtypeStruct(shape, F32),
            jax.ShapeDtypeStruct((seqs, max(head_count, 8), shape[1]), F32),
        ),
        in_specs=[pl.BlockSpec(memory_space=pltpu.SMEM), vmem, vmem, vmem],
        out_specs=(vmem,) * 6,
        scratch_shapes=[
            pltpu.VMEM(shape, BF16),
            dma((3, seqs)),
            dma((3, seqs)),
            dma((seqs,)),
            dma((seqs,)),
        ],
        compiler_params=pltpu.CompilerParams(
            collective_id=5, has_side_effects=True, vmem_limit_bytes=40 * MIB
        ),
        name="self_forward",
    )(windows, query, key, value)


def key_grads(
    b, seqs, rows, head_count, offset, window,
    q_all, k_all, v_all, grad_all, log_ref, delta, dq_total,
):
    keys, values = k_all[b], v_all[b]
    width = keys.shape[1]
    scale = jnp.asarray(HDIM**-0.5, BF16)
    key_heads = [only_head(keys, head, head_count) for head in range(head_count)]

    def pair(i, sums, diagonal):
        dk, dv = sums
        scaled = q_all[i] * scale
        grads = grad_all[i]
        if diagonal:
            allowed = (offset <= 0) & (offset > -window)
        else:
            allowed = offset > (i - b) * rows - window
        dq = dq_total[i]
        for head in range(head_count):
            query = only_head(scaled, head, head_count)
            grad = only_head(grads, head, head_count)
            scores = jnp.where(allowed, dot_nt(keys, query), NEG_FILL)
            probs = jnp.exp(scores - log_ref[i, head : head + 1])
            spread = dot_nt(values, grad)
            grad_scores = (probs * (spread - delta[i, head : head + 1])).astype(BF16)
            dv = dv + dot_nn(probs.astype(BF16), grad)
            dk = dk + dot_nn(grad_scores, query)
            dq = dq + dot_tn(grad_scores, key_heads[head])
        dq_total[i] = dq
        return (dk, dv)

    zeros = jnp.zeros((rows, width), F32)
    sums = pair(b, (zeros, zeros), True)
    return lax.fori_loop(b + 1, seqs, lambda i, s: pair(i, s, False), sums)


def cross_grads(length, query, keys, values, grads, crossed, logs):
    head_count = LANES // HDIM
    rows = query.shape[0]
    scaled = query * jnp.asarray(HDIM**-0.5, BF16)
    queries = jnp.concatenate([only_head(scaled, head, head_count) for head in range(head_count)], 0)
    uppers = jnp.concatenate([only_head(grads, head, head_count) for head in range(head_count)], 0)
    deltas = jnp.concatenate(head_sums(grads.astype(F32) * crossed.astype(F32), head_count), 1)
    scores = dot_nt(keys, queries)
    allowed = lax.broadcasted_iota(jnp.int32, scores.shape, 0) < length
    probs = jnp.exp(jnp.where(allowed, scores, NEG_FILL) - jnp.concatenate(logs, 1))
    grad_scores = (probs * (dot_nt(values, uppers) - deltas)).astype(BF16)
    dv = dot_nn(probs.astype(BF16), uppers)
    dk = dot_nn(grad_scores, queries)
    spread = dot_tn(grad_scores, keys)
    dq = spread[:rows]
    lane = lax.broadcasted_iota(jnp.int32, dq.shape, 1)
    for head in range(1, head_count):
        dq = jnp.where(lane >= head * HDIM, spread[head * rows : (head + 1) * rows], dq)
    return dq * HDIM**-0.5, dk, dv


def self_backward_kernel(
    seqs,
    window_ref,
    grad_ref,
    q_all,
    k_all,
    v_all,
    attended_ref,
    log_ref,
    dq_ref,
    dk_ref,
    dv_ref,
    grad_all,
    delta,
    dq_total,
    dq_low,
    dk_low,
    dv_low,
    send_sem,
    recv_sem,
    back_send,
    back_recv,
):
    me, z = lax.axis_index("seq"), lax.axis_index("grp")
    rows, width = grad_ref.shape[1], grad_ref.shape[2]
    head_count = width // HDIM
    greet_all(me, seqs, lambda j: (j, z))

    def outward(peer, slot):
        return remote(
            grad_ref.at[peer], grad_all.at[slot], send_sem.at[peer], recv_sem.at[slot], (peer, z)
        )

    def start(step, carry):
        outward(lax.rem(me + step, seqs), me).start()
        return carry

    lax.fori_loop(1, seqs, start, 0)
    grad_all[me] = grad_ref[me]
    window = window_ref[0]
    offset = lax.broadcasted_iota(jnp.int32, (rows, rows), 0) - lax.broadcasted_iota(
        jnp.int32, (rows, rows), 1
    )

    def prepare(i, carry):
        @pl.when(i != me)
        def _():
            outward(i, i).wait_recv()

        sums = head_sums(grad_all[i].astype(F32) * attended_ref[i].astype(F32), head_count)
        for head in range(head_count):
            delta[i, head : head + 1] = sums[head]
        dq_total[i] = jnp.zeros((rows, width), F32)
        return carry

    lax.fori_loop(0, seqs, prepare, 0)
    outputs = ((dq_low, dq_ref), (dk_low, dk_ref), (dv_low, dv_ref))

    def returned(peer, slot, part):
        src, dst = outputs[part]
        return remote(
            src.at[peer], dst.at[slot], back_send.at[part, peer], back_recv.at[part, slot], (peer, z)
        )

    def key_block(step, carry):
        b = seqs - 1 - step
        dk, dv = key_grads(
            b, seqs, rows, head_count, offset, window,
            q_all, k_all, v_all, grad_all, log_ref, delta, dq_total,
        )
        dk_low[b] = dk.astype(BF16)
        dv_low[b] = dv.astype(BF16)

        @pl.when(b != me)
        def _():
            returned(b, me, 1).start()
            returned(b, me, 2).start()

        return carry

    lax.fori_loop(0, seqs, key_block, 0)

    def close(i, carry):
        dq_low[i] = (dq_total[i] * HDIM**-0.5).astype(BF16)

        @pl.when(i != me)
        def _():
            returned(i, me, 0).start()

        return carry

    lax.fori_loop(0, seqs, close, 0)
    for src, dst in outputs:
        dst[me] = src[me]

    def finish(step, carry):
        peer = lax.rem(me + step, seqs)
        outward(peer, me).wait_send()
        for part in range(3):
            returned(peer, peer, part).wait()
        return carry

    lax.fori_loop(1, seqs, finish, 0)


def self_backward(seqs, windows, grad, query_all, key_all, value_all, attended, logs):
    shape = grad.shape
    dma = pltpu.SemaphoreType.DMA
    vmem = pl.BlockSpec(memory_space=pltpu.VMEM)
    return pl.pallas_call(
        functools.partial(self_backward_kernel, seqs),
        out_shape=(jax.ShapeDtypeStruct(shape, BF16),) * 3,
        in_specs=[pl.BlockSpec(memory_space=pltpu.SMEM)] + [vmem] * 6,
        out_specs=(vmem,) * 3,
        scratch_shapes=[
            pltpu.VMEM(shape, BF16),
            pltpu.VMEM(logs.shape, F32),
            pltpu.VMEM(shape, F32),
            pltpu.VMEM(shape, BF16),
            pltpu.VMEM(shape, BF16),
            pltpu.VMEM(shape, BF16),
            dma((seqs,)),
            dma((seqs,)),
            dma((3, seqs)),
            dma((3, seqs)),
        ],
        compiler_params=pltpu.CompilerParams(
            collective_id=6, has_side_effects=True, vmem_limit_bytes=40 * MIB
        ),
        name="self_backward",
    )(windows, grad, query_all, key_all, value_all, attended, logs)


def cross_forward_kernel(length_ref, q_ref, k_ref, v_ref, crossed_ref, low_ref, log_ref):
    crossed, logs = cross_attend(length_ref[0], q_ref[...], k_ref[...], v_ref[...])
    for head in range(len(logs)):
        log_ref[0, head : head + 1] = logs[head]
    crossed_ref[...] = crossed
    low_ref[...] = crossed.astype(BF16)


def cross_forward(lengths, query, key, value):
    rows, width = query.shape
    blocks = width // LANES
    columns = lambda j: (0, j)
    return pl.pallas_call(
        cross_forward_kernel,
        grid=(blocks,),
        out_shape=(
            jax.ShapeDtypeStruct((rows, width), F32),
            jax.ShapeDtypeStruct((rows, width), BF16),
            jax.ShapeDtypeStruct((blocks, 8, rows), F32),
        ),
        in_specs=[
            pl.BlockSpec(memory_space=pltpu.SMEM),
            pl.BlockSpec((rows, LANES), columns),
            pl.BlockSpec((key.shape[0], LANES), columns),
            pl.BlockSpec((key.shape[0], LANES), columns),
        ],
        out_specs=(
            pl.BlockSpec((rows, LANES), columns),
            pl.BlockSpec((rows, LANES), columns),
            pl.BlockSpec((1, 8, rows), lambda j: (j, 0, 0)),
        ),
        name="cross_forward",
    )(lengths, query, key, value)


def cross_backward_kernel(
    length_ref, q_ref, k_ref, v_ref, grad_ref, crossed_ref, log_ref, dq_ref, dk_ref, dv_ref
):
    dq, dk, dv = cross_grads(
        length_ref[0],
        q_ref[...],
        k_ref[...],
        v_ref[...],
        grad_ref[...],
        crossed_ref[...],
        [log_ref[0, head : head + 1] for head in range(LANES // HDIM)],
    )
    dq_ref[...] = dq.astype(BF16)
    dk_ref[...] = dk.astype(BF16)
    dv_ref[...] = dv.astype(BF16)


def cross_backward(lengths, query, key, value, grad, crossed, logs):
    rows, width = query.shape
    keys = key.shape[0]
    columns = lambda j: (0, j)
    token_block = pl.BlockSpec((rows, LANES), columns)
    key_block = pl.BlockSpec((keys, LANES), columns)
    return pl.pallas_call(
        cross_backward_kernel,
        grid=(width // LANES,),
        out_shape=(
            jax.ShapeDtypeStruct((rows, width), BF16),
            jax.ShapeDtypeStruct((keys, width), BF16),
            jax.ShapeDtypeStruct((keys, width), BF16),
        ),
        in_specs=[
            pl.BlockSpec(memory_space=pltpu.SMEM),
            token_block,
            key_block,
            key_block,
            token_block,
            token_block,
            pl.BlockSpec((1, 8, rows), lambda j: (j, 0, 0)),
        ],
        out_specs=(token_block, key_block, key_block),
        name="cross_backward",
    )(lengths, query, key, value, grad, crossed, logs)


def memory_sum_kernel(seqs, parts_ref, total_ref, arrived, send_sem, recv_sem):
    me, z = lax.axis_index("seq"), lax.axis_index("grp")
    greet_all(me, seqs, lambda j: (j, z))

    def copy_of(peer, slot):
        return remote(
            parts_ref.at[peer], arrived.at[slot], send_sem.at[peer], recv_sem.at[slot], (peer, z)
        )

    def start(step, carry):
        copy_of(lax.rem(me + step, seqs), me).start()
        return carry

    def finish(step, carry):
        peer = lax.rem(me + step, seqs)
        copy_of(peer, peer).wait()
        return carry

    lax.fori_loop(1, seqs, start, 0)
    arrived[me] = parts_ref[me]
    lax.fori_loop(1, seqs, finish, 0)
    total = arrived[0].astype(F32)
    for j in range(1, seqs):
        total = total + arrived[j].astype(F32)
    total_ref[...] = total.astype(BF16)


def memory_sum(seqs, parts):
    dma = pltpu.SemaphoreType.DMA
    vmem = pl.BlockSpec(memory_space=pltpu.VMEM)
    return pl.pallas_call(
        functools.partial(memory_sum_kernel, seqs),
        out_shape=jax.ShapeDtypeStruct(parts.shape[1:], BF16),
        in_specs=[vmem],
        out_specs=vmem,
        scratch_shapes=[pltpu.VMEM(parts.shape, BF16), dma((seqs,)), dma((seqs,))],
        compiler_params=pltpu.CompilerParams(
            collective_id=7, has_side_effects=True, vmem_limit_bytes=32 * MIB
        ),
        name="memory_sum",
    )(parts)


def tiled_layer(
    tokens, memory, cotangent, windows, mem_lengths, owners, master, vectors
):
    rows = tokens.shape[1]
    mem_rows = memory.shape[1]
    seqs, planes = lax.axis_size("seq"), lax.axis_size("grp")
    holder, slot, group, unit = owner_tables(owners, master.shape[0], seqs * planes)
    flat = tokens.reshape(rows, D)
    (
        whole,
        h1,
        joined,
        qkv,
        attended,
        logs,
        x2,
        h2,
        cross_queries,
        mem_acts,
        crossed,
        cross_logs,
        x3,
        h3,
        activation,
        slope,
        mixed,
        memory_padded,
    ) = forward_pass(
        seqs,
        planes,
        windows,
        mem_lengths,
        holder,
        slot,
        master,
        flat,
        memory.reshape(mem_rows, D),
        vectors,
    )
    grad_slots, grad_tokens, grad_memory, vector_sums = backward_pass(
        seqs,
        planes,
        windows,
        mem_lengths,
        group,
        unit,
        whole,
        slope,
        (
            cotangent.reshape(rows, D),
            flat,
            x2,
            x3,
            h1,
            h2,
            h3,
            activation,
            crossed,
            cross_queries,
            mem_acts,
            cross_logs,
            joined,
            attended,
            qkv,
            logs,
            memory_padded,
            vectors,
        ),
    )
    return mixed.reshape(tokens.shape), grad_tokens.reshape(tokens.shape), grad_memory, grad_slots, vector_sums


def plain_layer(
    tokens, memory, cotangent, windows, mem_lengths, owners, master, vectors
):
    rows = tokens.shape[1]
    seqs, planes = lax.axis_size("seq"), lax.axis_size("grp")
    units = owners.shape[0]
    slot_count, unit_rows = (master.shape[0], master.shape[1])
    bias_rows = FF // D
    placed, unit_at, occupied = slot_tables(owners, slot_count, seqs * planes)
    gathered = lax.all_gather(master.astype(BF16), ("seq", "grp"), axis=0, tiled=True)
    stacked = jnp.take(gathered, placed, axis=0).reshape(-1, D)
    memory_whole = lax.all_gather(memory[0], "seq", axis=0, tiled=True)
    self_query, self_key, self_value, self_out = (stacked[i * D : (i + 1) * D] for i in range(4))
    cross_query, cross_key, cross_value, cross_out = (
        stacked[i * D : (i + 1) * D] for i in range(4, 8)
    )
    hidden_in, hidden_out = stacked[8 * D : 8 * D + FF], stacked[8 * D + FF :]

    def by_device(tensor):
        return jnp.swapaxes(tensor.reshape(rows, seqs, D // seqs), 0, 1)

    def by_token(tensor):
        return jnp.swapaxes(tensor, 0, 1).reshape(rows, D)

    stream = tokens.astype(F32).reshape(rows, D)
    normed_one, form_one, inverse_one = norm_forward(stream, vectors[0], vectors[1])
    normed_self = normed_one.astype(BF16)
    query_act = (product(normed_self, self_query) + vectors[6]).astype(BF16)
    key_act = product(normed_self, self_key).astype(BF16)
    value_act = (product(normed_self, self_value) + vectors[7]).astype(BF16)
    joined, query_all, key_all, value_all, attended32, logs = self_forward(
        seqs, windows, by_device(query_act), by_device(key_act), by_device(value_act)
    )
    attended = by_token(joined)
    after_self = stream + product(attended, self_out) + vectors[8]
    normed_two, form_two, inverse_two = norm_forward(after_self, vectors[2], vectors[3])
    normed_cross = normed_two.astype(BF16)
    cross_queries = (product(normed_cross, cross_query) + vectors[9]).astype(BF16)
    mem_key_act = product(memory_whole, cross_key).astype(BF16)
    mem_value_act = (product(memory_whole, cross_value) + vectors[10]).astype(BF16)
    crossed32, crossed, cross_logs = cross_forward(
        mem_lengths, cross_queries, mem_key_act, mem_value_act
    )
    after_cross = after_self + product(crossed, cross_out) + vectors[11]
    normed_three, form_three, inverse_three = norm_forward(after_cross, vectors[4], vectors[5])
    normed_mlp = normed_three.astype(BF16)
    pre_act = product_nt(normed_mlp, hidden_in) + vectors[12 : 12 + bias_rows].reshape(FF)
    activation, slope = jax.jvp(gelu_exact, (pre_act,), (jnp.ones_like(pre_act),))
    activation_bf = activation.astype(BF16)
    result_rows = after_cross + product(activation_bf, hidden_out) + vectors[12 + bias_rows]
    mixed = result_rows.astype(BF16).reshape(tokens.shape)
    grad_out_bf = cotangent.reshape(rows, D)
    grad_stream = cotangent.astype(F32).reshape(rows, D)
    grad_hidden_out = product_tn(activation_bf, grad_out_bf)
    grad_down_bias = jnp.sum(grad_stream, axis=0)
    grad_activation = product_nt(grad_out_bf, hidden_out)
    grad_pre = (grad_activation * slope).astype(BF16)
    grad_hidden_in = product_tn(grad_pre, normed_mlp)
    grad_up_bias = jnp.sum(grad_pre.astype(F32), axis=0)
    grad_normed_mlp = product(grad_pre, hidden_in)
    back_three, grad_gain_three, grad_shift_three = norm_backward(
        grad_normed_mlp, form_three, inverse_three, vectors[4]
    )
    grad_after_cross = grad_stream + back_three
    grad_cross_branch = grad_after_cross.astype(BF16)
    grad_cross_out = product_tn(crossed, grad_cross_branch)
    grad_cross_out_bias = jnp.sum(grad_cross_branch.astype(F32), axis=0)
    grad_crossed = product_nt(grad_cross_branch, cross_out).astype(BF16)
    grad_cross_queries, part_mem_keys, part_mem_values = cross_backward(
        mem_lengths, cross_queries, mem_key_act, mem_value_act, grad_crossed, crossed32, cross_logs
    )
    mem_rows = memory.shape[1]
    mem_parts = jnp.concatenate(
        [part_mem_keys.reshape(seqs, mem_rows, D), part_mem_values.reshape(seqs, mem_rows, D)],
        axis=1,
    )
    mem_sums = memory_sum(seqs, mem_parts)
    mem_flat = memory.reshape(-1, D)
    mem_keys_flat = mem_sums[:mem_rows]
    mem_values_flat = mem_sums[mem_rows:]
    grad_cross_key = product_tn(mem_flat, mem_keys_flat)
    grad_cross_value = product_tn(mem_flat, mem_values_flat)
    grad_cross_value_bias = jnp.sum(mem_values_flat.astype(F32), axis=0)
    grad_memory = (
        product_nt(mem_keys_flat, cross_key) + product_nt(mem_values_flat, cross_value)
    ).reshape(memory.shape)
    grad_cross_query = product_tn(normed_cross, grad_cross_queries)
    grad_cross_query_bias = jnp.sum(grad_cross_queries.astype(F32), axis=0)
    grad_normed_cross = product_nt(grad_cross_queries, cross_query)
    back_two, grad_gain_two, grad_shift_two = norm_backward(
        grad_normed_cross, form_two, inverse_two, vectors[2]
    )
    grad_after_self = grad_after_cross + back_two
    grad_self_branch = grad_after_self.astype(BF16)
    grad_self_out = product_tn(attended, grad_self_branch)
    grad_self_out_bias = jnp.sum(grad_self_branch.astype(F32), axis=0)
    grad_attended = product_nt(grad_self_branch, self_out).astype(BF16)
    grad_queries, grad_keys, grad_values = (
        by_token(part)
        for part in self_backward(
            seqs, windows, by_device(grad_attended), query_all, key_all, value_all, attended32, logs
        )
    )
    grad_self_query = product_tn(normed_self, grad_queries)
    grad_self_key = product_tn(normed_self, grad_keys)
    grad_self_value = product_tn(normed_self, grad_values)
    grad_query_bias = jnp.sum(grad_queries.astype(F32), axis=0)
    grad_value_bias = jnp.sum(grad_values.astype(F32), axis=0)
    grad_normed_self = (
        product_nt(grad_queries, self_query)
        + product_nt(grad_keys, self_key)
        + product_nt(grad_values, self_value)
    )
    back_one, grad_gain_one, grad_shift_one = norm_backward(
        grad_normed_self, form_one, inverse_one, vectors[0]
    )
    grad_tokens = (grad_after_self + back_one).reshape(tokens.shape)
    grad_matrices = jnp.concatenate(
        [
            part.astype(BF16)
            for part in (
                grad_self_query,
                grad_self_key,
                grad_self_value,
                grad_self_out,
                grad_cross_query,
                grad_cross_key,
                grad_cross_value,
                grad_cross_out,
                grad_hidden_in,
                grad_hidden_out,
            )
        ],
        axis=0,
    )
    grad_units = grad_matrices.reshape(units, unit_rows, D)
    small_rows = jnp.stack(
        [
            grad_gain_one,
            grad_shift_one,
            grad_gain_two,
            grad_shift_two,
            grad_gain_three,
            grad_shift_three,
            grad_query_bias,
            grad_value_bias,
            grad_self_out_bias,
            grad_cross_query_bias,
            grad_cross_value_bias,
            grad_cross_out_bias,
        ]
    )
    grad_vectors = jnp.concatenate(
        [small_rows, grad_up_bias.reshape(bias_rows, D), grad_down_bias[None]], axis=0
    )
    grad_slots = lax.psum_scatter(
        jnp.where(
            occupied[:, None, None], jnp.take(grad_units, unit_at, axis=0), jnp.zeros((), BF16)
        ),
        ("seq", "grp"),
        scatter_dimension=0,
        tiled=True,
    )
    grad_vectors = lax.psum(grad_vectors, ("seq", "grp"))
    return mixed, grad_tokens, grad_memory, grad_slots, grad_vectors


def update_kernel(
    master_ref,
    first_ref,
    second_ref,
    grad_ref,
    vectors_ref,
    vec_first_ref,
    vec_second_ref,
    vec_grad_ref,
    memory_ref,
    first_out,
    second_out,
    master_out,
    low_out,
    vec_first_out,
    vec_second_out,
    vectors_out,
    memory_out,
    bias_out,
):
    first, second, weight = adam_step(
        master_ref[...],
        first_ref[...],
        second_ref[...],
        grad_ref[...].astype(F32),
        RATE_MATRIX,
        WEIGHT_DECAY,
    )
    first_out[...] = first
    second_out[...] = second
    master_out[...] = weight
    low_out[...] = weight.astype(BF16)

    @pl.when((pl.program_id(0) == 0) & (pl.program_id(1) == 0))
    def _():
        rows = vectors_ref.shape[0]
        sums = vec_grad_ref[...][:rows]
        vec_first_out[...], vec_second_out[...], vectors_out[...] = adam_step(
            vectors_ref[...], vec_first_ref[...], vec_second_ref[...], sums, RATE_VECTOR, 0.0
        )
        memory_out[...] = memory_ref[...][: memory_out.shape[0]]
        bias_out[...] = sums[rows - 1 :]


def update(master, first, second, grad, vectors, vec_first, vec_second, vec_grad, grad_memory, mem):
    slots, rows, width = master.shape
    part = rows // 4
    block = pl.BlockSpec((1, part, width), lambda s, p: (s, p, 0))

    def whole(shape):
        return pl.BlockSpec(shape, lambda s, p: (0, 0))

    shape = jax.ShapeDtypeStruct
    vec = whole(vectors.shape)
    return pl.pallas_call(
        update_kernel,
        grid=(slots, rows // part),
        out_shape=(shape(master.shape, F32),) * 3
        + (shape(master.shape, BF16),)
        + (shape(vectors.shape, F32),) * 3
        + (shape((mem, width), F32), shape((1, width), F32)),
        in_specs=[block] * 4 + [vec] * 3 + [whole(vec_grad.shape), whole(grad_memory.shape)],
        out_specs=(block,) * 4 + (vec,) * 3 + (whole((mem, width)), whole((1, width))),
        compiler_params=pltpu.CompilerParams(vmem_limit_bytes=60 * MIB),
        name="update",
    )(master, first, second, grad, vectors, vec_first, vec_second, vec_grad, grad_memory)


def local(
    tokens,
    memory,
    cotangent,
    windows,
    mem_lengths,
    owners,
    master,
    first_moment,
    second_moment,
    vectors,
    vec_first,
    vec_second,
):
    tiled = lax.axis_size("seq") == 8 and master.shape[1] % (32 * lax.axis_size("grp")) == 0
    layer = tiled_layer if tiled else plain_layer
    mixed, grad_tokens, grad_memory, grad_slots, grad_vectors = layer(
        tokens, memory, cotangent, windows, mem_lengths, owners, master, vectors
    )
    if tiled:
        (
            new_first,
            new_second,
            new_master,
            master_copy,
            vec_first_out,
            vec_second_out,
            vectors_out,
            grad_memory,
            grad_out_bias,
        ) = update(
            master,
            first_moment,
            second_moment,
            grad_slots,
            vectors,
            vec_first,
            vec_second,
            grad_vectors,
            grad_memory,
            memory.shape[1],
        )
        grad_memory = grad_memory.reshape(memory.shape)
        grad_out_bias = grad_out_bias.reshape(D)
    else:
        new_first, new_second, new_master = adam_step(
            master,
            first_moment,
            second_moment,
            grad_slots.astype(F32),
            RATE_MATRIX,
            WEIGHT_DECAY,
        )
        master_copy = new_master.astype(BF16)
        vec_first_out, vec_second_out, vectors_out = adam_step(
            vectors, vec_first, vec_second, grad_vectors, RATE_VECTOR, 0.0
        )
        grad_out_bias = grad_vectors[vectors.shape[0] - 1]
    return (
        mixed,
        grad_tokens,
        grad_memory,
        new_first,
        new_second,
        new_master,
        master_copy,
        vec_first_out,
        vec_second_out,
        vectors_out,
        grad_out_bias,
    )


def solution(mesh):
    placed = (
        P("grp", "seq", None),
        P("grp", "seq", None),
        P("grp", "seq", None),
        P("grp"),
        P("grp"),
        P(),
        P(("seq", "grp"), None, None),
        P(("seq", "grp"), None, None),
        P(("seq", "grp"), None, None),
        P(),
        P(),
        P(),
    )
    return jax.shard_map(
        local,
        mesh=mesh,
        in_specs=placed,
        out_specs=(
            P("grp", "seq", None),
            P("grp", "seq", None),
            P("grp", "seq", None),
            P(("seq", "grp"), None, None),
            P(("seq", "grp"), None, None),
            P(("seq", "grp"), None, None),
            P(("seq", "grp"), None, None),
            P(),
            P(),
            P(),
            P(),
        ),
        check_vma=False,
    )
```
